32 devices in a mesh: seq: 8 (over z, core), ch: 2 (over y), win: 2 (over x).
Axes of the slice: x: 2, y: 2, z: 4, core: 2. Of those that a mesh axis runs over, the one named last changes fastest.
Arguments:
- inputs: bfloat16 [8, 768, 24576], P('win', 'ch', 'seq')
- lengths: int32 [8], P('win'), may hold values from 6144 to 24576, as said below
- gain_in: float32 [768], P('ch'), may hold values from 0.1 to 1.9
- offset_in: float32 [768], P('ch'), may hold values from -3 to 3
- conv_weight: bfloat16 [3, 768, 384], P(None, 'ch'), may hold values from -0.125 to 0.125
- gain_mid: float32 [384], replicated, may hold values from 0.1 to 1.9
- offset_mid: float32 [384], replicated, may hold values from -3 to 3
- point_weight: bfloat16 [384, 768], P(None, 'ch'), may hold values from -0.625 to 0.625
- point_bias: float32 [768], P('ch'), may hold values from -3 to 3
- cotangent: bfloat16 [8, 768, 24576], P('win', 'ch', 'seq'), may hold values from -6 to 6
Outputs:
- outputs: bfloat16 [8, 768, 24576], P('win', 'ch', 'seq')
- grad_inputs: bfloat16 [8, 768, 24576], P('win', 'ch', 'seq')
- grad_gain_in: float32 [768], P('ch')
- grad_offset_in: float32 [768], P('ch')
- grad_conv: float32 [3, 768, 384], P(None, 'ch')
- grad_gain_mid: float32 [384], P('ch')
- grad_offset_mid: float32 [384], P('ch')
- grad_point: float32 [384, 768], P(None, 'ch')
- grad_bias: float32 [768], P('ch')
The draws below stay inside these ranges and needn't reach their ends.
Inputs may be any that keep to these rules, and one draw needn't show every extreme that they name: `lengths`: among the 4 windows of each index of win, one has all 24576 bins valid and another a quarter of them.
All inputs are finite; a program needn't handle non-finite values.
Results may differ from the reference program's by a relative error of at most 0.0068.
Values may be sent and summed in bfloat16 or wider, within the bound.
A program may use at most 256 MiB of HBM per device.

```python
import math
import jax
import jax.numpy as jnp
from jax import lax

CH = 768
BOT = 384
KERNEL_TAPS = 3
DILATION_BINS = 57
WIN_DEV = 4
WINDOW_LENGTH = 24576
WINDOWS = 8


def draw_inputs(key, part):
    keys = jax.random.split(key, 4)
    base = jax.random.normal(keys[0], (WINDOWS, CH, WINDOW_LENGTH), jnp.float32)
    place = jnp.arange(WINDOW_LENGTH, dtype=jnp.float32) / WINDOW_LENGTH
    rise = jnp.exp(math.log(3.0) * (place - 0.5))
    row_scale = jnp.exp(jax.random.uniform(keys[1], (WINDOWS, 1, WINDOW_LENGTH), jnp.float32, math.log(0.6), math.log(1.7)))
    col_scale = jnp.exp(jax.random.uniform(keys[2], (CH, 1), jnp.float32, math.log(0.5), math.log(2.0)))
    col_shift = jax.random.uniform(keys[3], (CH, 1), jnp.float32, -0.5, 0.5)
    values = (base * col_scale + col_shift) * row_scale * rise[None, None, :]
    return values.astype(jnp.bfloat16)


def draw_lengths(key, part):
    keys = jax.random.split(key, 3)
    values = jax.random.randint(keys[0], (WINDOWS,), WINDOW_LENGTH // 4, WINDOW_LENGTH + 1, dtype=jnp.int32)
    group_count = WINDOWS // WIN_DEV
    longest = jax.random.randint(keys[1], (group_count,), 0, WIN_DEV, dtype=jnp.int32)
    shortest = (longest + 1 + jax.random.randint(keys[2], (group_count,), 0, WIN_DEV - 1, dtype=jnp.int32)) % WIN_DEV
    starts = jnp.arange(group_count, dtype=jnp.int32) * WIN_DEV
    values = values.at[starts + longest].set(WINDOW_LENGTH)
    values = values.at[starts + shortest].set(WINDOW_LENGTH // 4)
    return values.astype(jnp.int32)


def level_of(key, shape, cuts, smallest, top_value):
    loudness, own = 1.0, jax.random.fold_in(key, 6)
    for axis_at, parts in cuts:
        steps = jnp.exp(jax.random.uniform(jax.random.fold_in(own, axis_at), (parts,), jnp.float32, smallest / len(cuts), top_value / len(cuts)))
        loudness = loudness * jnp.repeat(steps, shape[axis_at] // parts).reshape([-1 if axis == axis_at else 1 for axis in range(len(shape))])
    return loudness


def gaussian(stream_key, extent, width, limit, cuts=(), held_as=jnp.bfloat16):
    array = width * jax.random.normal(stream_key, extent, jnp.float32)
    if cuts:
        array = array * level_of(stream_key, extent, cuts, -0.22, 0.18)
    return jnp.clip(array, -limit, limit).astype(held_as)


def setup_inputs(seed: int = 0) -> dict:
    key_of = jax.random.split(jax.random.key(seed), 11)
    return {
        "inputs": draw_inputs(jax.random.fold_in(key_of[10], 71), 0),
        "lengths": draw_lengths(jax.random.fold_in(key_of[10], 71), 0),
        "gain_in": jnp.clip(1.0 + 0.18 * jax.random.normal(key_of[2], (CH,), jnp.float32), 0.1, 1.9),
        "offset_in": gaussian(key_of[3], (CH,), 0.5, 3.0, ((0, 2),), jnp.float32),
        "conv_weight": gaussian(key_of[4], (KERNEL_TAPS, CH, BOT), (KERNEL_TAPS * CH) ** -0.5, 0.125, ((1, 2),)),
        "gain_mid": jnp.clip(1.0 + 0.18 * jax.random.normal(key_of[5], (BOT,), jnp.float32), 0.1, 1.9),
        "offset_mid": gaussian(key_of[6], (BOT,), 0.5, 3.0, (), jnp.float32),
        "point_weight": gaussian(key_of[7], (BOT, CH), (BOT // 4) ** -0.5, 0.625, ((1, 2),)),
        "point_bias": gaussian(key_of[8], (CH,), 0.5, 3.0, ((0, 2),), jnp.float32),
        "cotangent": gaussian(key_of[9], (WINDOWS, CH, WINDOW_LENGTH), 1.0, 6.0, ((0, 2), (1, 2), (2, 8))),
    }


EPS = 1e-05
HIGH = lax.Precision.HIGHEST

@jax.custom_vjp
def low(v):
    return lax.optimization_barrier(v.astype(jnp.bfloat16)).astype(jnp.float32)

@jax.custom_vjp
def low_back(v):
    return v

def low_keep(v):
    return (low(v), None)

def low_pass(kept, grad):
    return (grad,)

def back_keep(v):
    return (v, None)

def back_low(kept, grad):
    return (low(grad),)
low.defvjp(low_keep, low_pass)
low_back.defvjp(back_keep, back_low)

def reference(inputs, lengths, gain_in, offset_in, conv_weight, gain_mid, offset_mid, point_weight, point_bias, cotangent):
    valid_rows = (jnp.arange(WINDOW_LENGTH, dtype=jnp.int32)[None, :] < lengths[:, None]).astype(jnp.float32)
    filled = jnp.sum(valid_rows)
    per_block = math.gcd(WINDOWS, max(1, 4096 // WINDOW_LENGTH))
    block_count = WINDOWS // per_block
    mask_blocks = valid_rows.reshape(block_count, per_block, WINDOW_LENGTH, 1)

    def forward(x_full, g_in, o_in, w_conv, g_mid, o_mid, w_point, b_point):
        x_blocks = x_full.reshape(block_count, per_block, WINDOW_LENGTH, CH)

        def moments(pair_in):
            x_block, m_block = pair_in
            return (lax.optimization_barrier(jnp.sum(m_block * x_block, axis=(0, 1))), lax.optimization_barrier(jnp.sum(m_block * x_block * x_block, axis=(0, 1))))
        first_in, second_in = lax.map(jax.checkpoint(moments), (x_blocks, mask_blocks))
        mean_in = lax.optimization_barrier(jnp.sum(first_in, axis=0)) / filled
        scale_in = lax.rsqrt(lax.optimization_barrier(jnp.sum(second_in, axis=0)) / filled - mean_in * mean_in + EPS)

        def convolve(pair_in):
            x_block, m_block = pair_in
            input_activation = low(jax.nn.gelu((x_block - mean_in) * scale_in * g_in + o_in) * m_block)
            padded_input = jnp.pad(input_activation, ((0, 0), (DILATION_BINS, DILATION_BINS), (0, 0)))
            stacked_taps = jnp.stack([padded_input[:, kernel_tap_index * DILATION_BINS:kernel_tap_index * DILATION_BINS + WINDOW_LENGTH, :] for kernel_tap_index in range(KERNEL_TAPS)], axis=2)
            return jnp.einsum('wtkc,kcf->wtf', stacked_taps, w_conv, precision=HIGH)
        conv_out = low_back(lax.map(jax.checkpoint(convolve), (x_blocks, mask_blocks)))
        mean_mid = lax.optimization_barrier(jnp.sum(mask_blocks * conv_out, axis=(0, 1, 2))) / filled
        scale_mid = lax.rsqrt(lax.optimization_barrier(jnp.sum(mask_blocks * conv_out * conv_out, axis=(0, 1, 2))) / filled - mean_mid * mean_mid + EPS)

        def mix(triple_in):
            x_block, m_block, c_block = triple_in
            act_mid = low(jax.nn.gelu((c_block - mean_mid) * scale_mid * g_mid + o_mid) * m_block)
            branch = jnp.einsum('wtf,fc->wtc', act_mid, w_point, precision=HIGH)
            return x_block + branch + b_point
        result = lax.map(jax.checkpoint(mix), (x_blocks, mask_blocks, conv_out))
        return result.reshape(WINDOWS, WINDOW_LENGTH, CH)
    x_rows = jnp.transpose(inputs.astype(jnp.float32), (0, 2, 1))
    result, pullback = jax.vjp(forward, x_rows, gain_in, offset_in, conv_weight.astype(jnp.float32), gain_mid, offset_mid, point_weight.astype(jnp.float32), point_bias)
    grads = pullback(jnp.transpose(cotangent.astype(jnp.float32), (0, 2, 1)))
    outputs = jnp.transpose(result, (0, 2, 1)).astype(jnp.bfloat16)
    grad_inputs = jnp.transpose(grads[0], (0, 2, 1)).astype(jnp.bfloat16)
    return (outputs, grad_inputs, grads[1], grads[2], grads[3], grads[4], grads[5], grads[6], grads[7])
```

```python
import functools

import jax
import jax.numpy as jnp
from jax import lax
from jax.experimental import pallas as pl
from jax.experimental.pallas import tpu as pltpu
from jax.sharding import PartitionSpec as P

DILATION_BINS = 57


EPS = 1e-05
LANES = 128
TILE = 384
VMEM_BYTES = 48 * 1024 * 1024


def with_halo(cells, sides, width):
    for axis, dim in sides:
        count = lax.axis_size(axis)
        ends = count - 1
        head = lax.slice_in_dim(cells, 0, width, axis=dim)
        tail = lax.slice_in_dim(cells, cells.shape[dim] - width, cells.shape[dim], axis=dim)
        cells = jnp.concatenate(
            [
                lax.ppermute(tail, axis, [(i, (i + 1) % count) for i in range(ends)]),
                cells,
                lax.ppermute(head, axis, [((i + 1) % count, i) for i in range(ends)]),
            ],
            axis=dim,
        )
    return cells


def norm_sums(first_term, second_term):
    return lax.psum((first_term, second_term), ("seq", "win"))


def column(vector):
    return vector[:, None]


def local_any(
    inputs,
    lengths,
    gain_in,
    offset_in,
    conv_weight,
    gain_mid,
    offset_mid,
    point_weight,
    point_bias,
    cotangent,
):
    win_count, chan_local, count_of_bins = inputs.shape
    count_of_taps = conv_weight.shape[0]
    bottle = conv_weight.shape[2]
    bottle_local = bottle // lax.axis_size("ch")
    offset_at = lax.axis_index("ch") * bottle_local
    places = lax.axis_index("seq") * count_of_bins + jnp.arange(count_of_bins, dtype=jnp.int32)
    valid_rows = (places[None, :] < lengths[:, None]).astype(jnp.float32)[:, None, :]
    x_wide = inputs.astype(jnp.float32)
    sum_first = jnp.sum(valid_rows * x_wide, axis=(0, 2))
    sum_second = jnp.sum(valid_rows * x_wide * x_wide, axis=(0, 2))
    sum_first, sum_second, filled = lax.psum(
        (sum_first, sum_second, jnp.sum(valid_rows)), ("seq", "win")
    )
    mean_in = sum_first / filled
    scale_in = lax.rsqrt(sum_second / filled - mean_in * mean_in + EPS)
    norm_in = (x_wide - column(mean_in)) * column(scale_in)
    pre_in = norm_in * column(gain_in) + column(offset_in)
    input_activation, gelu_in_back = jax.vjp(jax.nn.gelu, pre_in)
    lowered_activation = (input_activation * valid_rows).astype(jnp.bfloat16)
    padded_input = with_halo(lowered_activation, (("seq", 2),), DILATION_BINS)
    stacked_taps = jnp.concatenate(
        [
            padded_input[
                :,
                :,
                kernel_tap_index * DILATION_BINS : kernel_tap_index * DILATION_BINS + count_of_bins,
            ]
            for kernel_tap_index in range(count_of_taps)
        ],
        axis=1,
    )
    flat_weight = conv_weight.reshape(count_of_taps * chan_local, bottle)
    partial_value = jnp.einsum(
        "wkt,kf->wft", stacked_taps, flat_weight, preferred_element_type=jnp.float32
    )
    conv_out = lax.psum_scatter(partial_value, "ch", scatter_dimension=1, tiled=True)
    gain_part = lax.dynamic_slice_in_dim(gain_mid, offset_at, bottle_local)
    offset_part = lax.dynamic_slice_in_dim(offset_mid, offset_at, bottle_local)
    mid_first, mid_second = norm_sums(
        jnp.sum(valid_rows * conv_out, axis=(0, 2)),
        jnp.sum(valid_rows * conv_out * conv_out, axis=(0, 2)),
    )
    mean_mid = mid_first / filled
    scale_mid = lax.rsqrt(mid_second / filled - mean_mid * mean_mid + EPS)
    norm_mid = (conv_out - column(mean_mid)) * column(scale_mid)
    pre_mid = norm_mid * column(gain_part) + column(offset_part)
    act_mid, gelu_mid_back = jax.vjp(jax.nn.gelu, pre_mid)
    act_mid_low = (act_mid * valid_rows).astype(jnp.bfloat16)
    mixed_in = lax.all_gather(act_mid_low, "ch", axis=1, tiled=True)
    branch = jnp.einsum("wft,fc->wct", mixed_in, point_weight, preferred_element_type=jnp.float32)
    outputs = (x_wide + branch + column(point_bias)).astype(jnp.bfloat16)
    grad_point = jnp.einsum("wft,wct->fc", mixed_in, cotangent, preferred_element_type=jnp.float32)
    grad_bias = jnp.sum(cotangent.astype(jnp.float32), axis=(0, 2))
    partial_back = jnp.einsum(
        "wct,fc->wft", cotangent, point_weight, preferred_element_type=jnp.float32
    )
    grad_act_mid = lax.psum_scatter(partial_back, "ch", scatter_dimension=1, tiled=True)
    grad_pre_mid = gelu_mid_back(grad_act_mid * valid_rows)[0]
    local_beta = jnp.sum(grad_pre_mid, axis=(0, 2))
    local_gamma = jnp.sum(grad_pre_mid * norm_mid, axis=(0, 2))
    grad_point, grad_bias, beta_mid, gamma_mid = lax.psum(
        (grad_point, grad_bias, local_beta, local_gamma), ("seq", "win")
    )
    grad_conv_out = column(gain_part * scale_mid) * (
        grad_pre_mid - valid_rows * (column(beta_mid) + norm_mid * column(gamma_mid)) / filled
    )
    grad_low = grad_conv_out.astype(jnp.bfloat16)
    complete_gradient = lax.all_gather(grad_low, "ch", axis=1, tiled=True)
    grad_conv = jnp.einsum(
        "wkt,wft->kf", stacked_taps, complete_gradient, preferred_element_type=jnp.float32
    )
    grad_conv = grad_conv.reshape(count_of_taps, chan_local, bottle)
    padded_gradient = with_halo(complete_gradient, (("seq", 2),), DILATION_BINS)
    back_taps = jnp.concatenate(
        [
            padded_gradient[
                :,
                :,
                (count_of_taps - 1 - kernel_tap_index)
                * DILATION_BINS : (count_of_taps - 1 - kernel_tap_index)
                * DILATION_BINS
                + count_of_bins,
            ]
            for kernel_tap_index in range(count_of_taps)
        ],
        axis=1,
    )
    back_weight = jnp.transpose(conv_weight, (0, 2, 1)).reshape(count_of_taps * bottle, chan_local)
    grad_act_in = jnp.einsum(
        "wkt,kc->wct", back_taps, back_weight, preferred_element_type=jnp.float32
    )
    grad_pre_in = gelu_in_back(grad_act_in * valid_rows)[0]
    local_beta_in = jnp.sum(grad_pre_in, axis=(0, 2))
    local_gamma_in = jnp.sum(grad_pre_in * norm_in, axis=(0, 2))
    grad_conv, beta_in, gamma_in = lax.psum(
        (grad_conv, local_beta_in, local_gamma_in), ("seq", "win")
    )
    grad_inputs = (
        cotangent.astype(jnp.float32)
        + column(gain_in * scale_in)
        * (grad_pre_in - valid_rows * (column(beta_in) + norm_in * column(gamma_in)) / filled)
    ).astype(jnp.bfloat16)
    return (
        outputs,
        grad_inputs,
        gamma_in,
        beta_in,
        grad_conv,
        gamma_mid,
        beta_mid,
        grad_point,
        grad_bias,
    )


def params(flops, moved):
    return dict(
        compiler_params=pltpu.CompilerParams(vmem_limit_bytes=VMEM_BYTES),
        cost_estimate=pl.CostEstimate(flops=flops, bytes_accessed=moved, transcendentals=0),
    )


def dot(a, b):
    return jnp.dot(a, b, preferred_element_type=jnp.float32)


def dot_t(a, b):
    return lax.dot_general(a, b, (((1,), (1,)), ((), ())), preferred_element_type=jnp.float32)


def lane_sum(cells):
    total = cells[:, :LANES]
    for at in range(LANES, cells.shape[1], LANES):
        total = total + cells[:, at : at + LANES]
    return total


GELU_A = 0.7978845608028654
GELU_B = 0.044715


def gelu(v):
    return 0.5 * v * (1.0 + jnp.tanh(GELU_A * (v + GELU_B * (v * v * v))))


def gelu_slope(v):
    square = v * v
    th = jnp.tanh(GELU_A * (v + GELU_B * (v * square)))
    return 0.5 * (1.0 + th) + 0.5 * v * (1.0 - th * th) * (GELU_A * (1.0 + 3.0 * GELU_B * square))


def ext_start(tile, tiles):
    first, second, _ = tiles
    extra = jnp.where(tile >= first, 2 * LANES, 0) + jnp.where(tile >= first + second, 2 * LANES, 0)
    return pl.multiple_of(tile * TILE + extra, LANES)


def fill_taps(cat, refs, start):
    chans = refs[0].shape[0]
    row = 0
    for ref in refs:
        wide = ref[:, pl.ds(start, TILE + 2 * LANES)]
        for tap in range(3):
            at = LANES + (tap - 1) * DILATION_BINS
            cat[row : row + chans, :] = wide[:, at : at + TILE]
            row += chans


def conv_kernel(tiles, own, other, weight, valid, out, first, second, cat):
    tile = pl.program_id(0)
    fill_taps(cat, (own, other), ext_start(tile, tiles))
    acc = dot(weight[...], cat[...])
    out[...] = acc
    kept = acc * valid[...]

    @pl.when(tile == 0)
    def _():
        first[...] = jnp.zeros_like(first)
        second[...] = jnp.zeros_like(second)

    first[...] += lane_sum(kept)
    second[...] += lane_sum(kept * acc)


def conv_forward(own, other, weight, valid, tiles):
    chans, wide = own.shape
    bottle, depth = weight.shape
    count = sum(tiles)
    whole = lambda shape: pl.BlockSpec(shape, lambda i: (0, 0))
    return pl.pallas_call(
        functools.partial(conv_kernel, tiles),
        grid=(count,),
        in_specs=[
            whole((chans, wide)),
            whole((chans, wide)),
            whole((bottle, depth)),
            pl.BlockSpec((1, TILE), lambda i: (0, i)),
        ],
        out_specs=[
            pl.BlockSpec((bottle, TILE), lambda i: (0, i)),
            whole((bottle, LANES)),
            whole((bottle, LANES)),
        ],
        out_shape=[
            jax.ShapeDtypeStruct((bottle, count * TILE), jnp.float32),
            jax.ShapeDtypeStruct((bottle, LANES), jnp.float32),
            jax.ShapeDtypeStruct((bottle, LANES), jnp.float32),
        ],
        scratch_shapes=[pltpu.VMEM((depth, TILE), jnp.bfloat16)],
        **params(2 * bottle * depth * count * TILE, 4 * bottle * count * TILE + 4 * chans * wide),
    )(own, other, weight, valid)


def mid_kernel(conv, act, valid, own, other, point, cols, grad, beta, gamma, outer):
    chans = own.shape[0]
    mean, scale, gain, offset = (cols[:, i : i + 1] for i in range(4))
    back = dot(point[:, :chans], own[...]) + dot(point[:, chans:], other[...])
    norm = (conv[...] - mean) * scale
    part = valid[...] * gelu_slope(norm * gain + offset) * back
    grad[...] = part

    @pl.when(pl.program_id(0) == 0)
    def _():
        beta[...] = jnp.zeros_like(beta)
        gamma[...] = jnp.zeros_like(gamma)
        outer[...] = jnp.zeros_like(outer)

    beta[...] += lane_sum(part)
    gamma[...] += lane_sum(part * norm)
    outer[:, :chans] += dot_t(act[...], own[...])
    outer[:, chans:] += dot_t(act[...], other[...])


def mid_back(conv, act, valid, own, other, point, cols, base):
    bottle = conv.shape[0]
    chans, bins = own.shape
    count = bins // TILE
    whole = lambda shape: pl.BlockSpec(shape, lambda i: (0, 0))
    shifted = lambda rows: pl.BlockSpec((rows, TILE), lambda i: (0, i + base))
    plain = lambda rows: pl.BlockSpec((rows, TILE), lambda i: (0, i))
    return pl.pallas_call(
        mid_kernel,
        grid=(count,),
        in_specs=[
            shifted(bottle),
            shifted(bottle),
            shifted(1),
            plain(chans),
            plain(chans),
            whole(point.shape),
            whole(cols.shape),
        ],
        out_specs=[
            plain(bottle),
            whole((bottle, LANES)),
            whole((bottle, LANES)),
            whole((bottle, 2 * chans)),
        ],
        out_shape=[
            jax.ShapeDtypeStruct((bottle, bins), jnp.float32),
            jax.ShapeDtypeStruct((bottle, LANES), jnp.float32),
            jax.ShapeDtypeStruct((bottle, LANES), jnp.float32),
            jax.ShapeDtypeStruct((bottle, 2 * chans), jnp.float32),
        ],
        **params(8 * bottle * chans * bins, (10 * bottle + 4 * chans) * bins),
    )(conv, act, valid, own, other, point, cols)


def weight_kernel(tiles, own, other, near, far, out, cat):
    tile = pl.program_id(0)
    fill_taps(cat, (own, other), ext_start(tile, tiles))

    @pl.when(tile == 0)
    def _():
        out[...] = jnp.zeros_like(out)

    @pl.when(tile < tiles[0])
    def _():
        out[...] += dot_t(cat[...], near[...])

    @pl.when(tile >= tiles[0])
    def _():
        out[...] += dot_t(cat[...], far[...])


def conv_weight_back(own, other, near, far, tiles):
    chans, wide = own.shape
    bottle = near.shape[0]
    depth = 6 * chans
    count = sum(tiles)
    whole = lambda shape: pl.BlockSpec(shape, lambda i: (0, 0))
    return pl.pallas_call(
        functools.partial(weight_kernel, tiles),
        grid=(count,),
        in_specs=[
            whole((chans, wide)),
            whole((chans, wide)),
            pl.BlockSpec((bottle, TILE), lambda i: (0, jnp.minimum(i, tiles[0] - 1))),
            pl.BlockSpec((bottle, TILE), lambda i: (0, jnp.maximum(i - tiles[0], 0))),
        ],
        out_specs=whole((depth, bottle)),
        out_shape=jax.ShapeDtypeStruct((depth, bottle), jnp.float32),
        scratch_shapes=[pltpu.VMEM((depth, TILE), jnp.bfloat16)],
        **params(2 * bottle * depth * count * TILE, 4 * chans * wide),
    )(own, other, near, far)


def out_kernel(place, act, x, weight, bias, *rest):
    out = rest[-1]
    out[0] = (x[0].astype(jnp.float32) + dot(weight[...], act[...]) + bias[...]).astype(out.dtype)


def write_outputs(prev, act, count, place, x, weight, bias):
    windows, chans, bins = x.shape
    bottle = act.shape[0]
    tile = 2 * TILE
    at = pl.BlockSpec((1, chans, tile), lambda i, p: (p[0], 0, p[1] + i))
    whole = lambda shape: pl.BlockSpec(shape, lambda i, p: (0, 0))
    in_specs = [
        pl.BlockSpec((bottle, tile), lambda i, p: (0, i)),
        at,
        whole((chans, bottle)),
        whole((chans, 1)),
    ]
    operands = [place, act, x, weight, bias]
    aliases = {}
    if prev is not None:
        in_specs.append(pl.BlockSpec(memory_space=pl.ANY))
        operands.append(prev)
        aliases = {5: 0}
    return pl.pallas_call(
        out_kernel,
        grid_spec=pltpu.PrefetchScalarGridSpec(
            num_scalar_prefetch=1, grid=(count,), in_specs=in_specs, out_specs=at
        ),
        out_shape=jax.ShapeDtypeStruct(x.shape, x.dtype),
        input_output_aliases=aliases,
        **params(2 * bottle * chans * count * tile, (4 * chans + 2 * bottle) * count * tile),
    )(*operands)


def back_kernel(order, grads, x, valid, weight, cols, out, beta, gamma, cat):
    bottle = grads.shape[1]
    start = pl.multiple_of(pl.program_id(1) * TILE, LANES)
    wide = grads[0, :, pl.ds(start, TILE + 2 * LANES)]
    for tap in range(3):
        at = LANES - (tap - 1) * DILATION_BINS
        cat[tap * bottle : (tap + 1) * bottle, :] = wide[:, at : at + TILE]
    mean, scale, gain, offset = (cols[:, i : i + 1] for i in range(4))
    norm = (x[0].astype(jnp.float32) - mean) * scale
    part = valid[0] * gelu_slope(norm * gain + offset) * dot(weight[...], cat[...])
    out[0] = part

    @pl.when((pl.program_id(0) == 0) & (pl.program_id(1) == 0))
    def _():
        beta[...] = jnp.zeros_like(beta)
        gamma[...] = jnp.zeros_like(gamma)

    beta[...] += lane_sum(part)
    gamma[...] += lane_sum(part * norm)


def input_back(order, grads, x, valid, weight, cols):
    windows, chans, bins = x.shape
    bottle, wide = grads.shape[1:]
    at = pl.BlockSpec((1, chans, TILE), lambda w, i, p: (p[w], 0, i))
    whole = lambda shape: pl.BlockSpec(shape, lambda w, i, p: (0, 0))
    return pl.pallas_call(
        back_kernel,
        grid_spec=pltpu.PrefetchScalarGridSpec(
            num_scalar_prefetch=1,
            grid=(windows, bins // TILE),
            in_specs=[
                pl.BlockSpec((1, bottle, wide), lambda w, i, p: (w, 0, 0)),
                at,
                pl.BlockSpec((1, 1, TILE), lambda w, i, p: (w, 0, i)),
                whole(weight.shape),
                whole(cols.shape),
            ],
            out_specs=[at, whole((chans, LANES)), whole((chans, LANES))],
            scratch_shapes=[pltpu.VMEM((3 * bottle, TILE), jnp.bfloat16)],
        ),
        out_shape=[
            jax.ShapeDtypeStruct(x.shape, jnp.float32),
            jax.ShapeDtypeStruct((chans, LANES), jnp.float32),
            jax.ShapeDtypeStruct((chans, LANES), jnp.float32),
        ],
        **params(6 * bottle * chans * windows * bins, 6 * chans * windows * bins),
    )(order, grads, x, valid, weight, cols)


def after(cells, done):
    spot = lax.slice(done, (0,) * done.ndim, (1,) * done.ndim).reshape(())
    return cells + (spot * 0).astype(cells.dtype)


def local_pair(
    inputs,
    lengths,
    gain_in,
    offset_in,
    conv_weight,
    gain_mid,
    offset_mid,
    point_weight,
    point_bias,
    cotangent,
):
    windows, chans, bins = inputs.shape
    taps, _, bottle = conv_weight.shape
    count_seq, count_win = lax.axis_size("seq"), lax.axis_size("win")
    side, shard, group_at = (lax.axis_index(name) for name in ("ch", "seq", "win"))
    quarter = count_seq // 4
    group = shard // quarter
    piece, half, eighth = bins // 4, bins // 2, bins // 8
    tiles = (bins // TILE, half // TILE, eighth // TILE)
    axes = ("seq", "ch", "win")
    swap = [(0, 1), (1, 0)]
    over = lambda cells: lax.ppermute(cells, "ch", swap)
    low_lanes = lax.broadcasted_iota(jnp.int32, (1, LANES), 1) < LANES // 2

    ids = jnp.arange(windows, dtype=jnp.int32)
    ahead = (lengths[None, :] > lengths[:, None]) | (
        (lengths[None, :] == lengths[:, None]) & (ids[None, :] < ids[:, None])
    )
    rank = jnp.sum(ahead.astype(jnp.int32), axis=1)
    chosen = rank[None, :] == ids[:, None]
    order = jnp.sum(jnp.where(chosen, ids[None, :], 0), axis=1)
    ranked = jnp.sum(jnp.where(chosen, lengths[None, :], 0), axis=1)
    pick = lambda cells, slot: lax.dynamic_index_in_dim(cells, order[slot], 0, keepdims=False)
    by_side = lambda role, first, second: jnp.where(role == 0, first, second)

    x1_mine = pick(inputs, side)
    x1_other = over(pick(inputs, 1 - side))

    flat = jnp.concatenate([conv_weight.reshape(taps * chans, bottle), point_weight], axis=0)
    share = flat.shape[0] // (count_seq * count_win)
    device_at = group_at * count_seq + shard
    flat_other = lax.all_gather(
        over(lax.dynamic_slice_in_dim(flat, device_at * share, share, 0)),
        ("win", "seq"),
        axis=0,
        tiled=True,
    )
    conv_other = flat_other[: taps * chans].reshape(taps, chans, bottle)
    point_other = flat_other[taps * chans :]

    ends = [(i, i + 1) for i in range(count_seq - 1)]
    back_ends = [(i + 1, i) for i in range(count_seq - 1)]

    def halo_of(cells):
        right = lax.ppermute(cells[..., :LANES], "seq", back_ends)
        left = lax.ppermute(cells[..., -LANES:], "seq", ends)
        return jnp.where(low_lanes, right, left)

    halo = halo_of(inputs)

    def spread(parts):
        total = jnp.where(group == 0, parts[0], jnp.zeros_like(parts[0]))
        for k in range(1, 4):
            total = total + lax.ppermute(parts[k], "seq", [(i, i + k * quarter) for i in range(quarter)])
        return total

    def collect(cells):
        parts = [jnp.where(group == 0, cells, jnp.zeros_like(cells))]
        for k in range(1, 4):
            parts.append(lax.ppermute(cells, "seq", [(i + k * quarter, i) for i in range(quarter)]))
        return jnp.concatenate(parts, axis=1)

    quarter_x, quarter_halo = pick(inputs, 3), pick(halo, 3)
    wide_x = jnp.concatenate([quarter_halo, quarter_x, quarter_halo], axis=1)

    def piece_of(k):
        right = wide_x[:, LANES + piece * (k + 1) : 2 * LANES + piece * (k + 1)]
        left = wide_x[:, piece * k : LANES + piece * k]
        return jnp.concatenate(
            [jnp.where(low_lanes, right, left), quarter_x[:, piece * k : piece * (k + 1)]], axis=1
        )

    extra_x = spread([piece_of(k) for k in range(4)])
    third_x, third_halo = pick(inputs, 2), pick(halo, 2)

    def second_part(role):
        e, e_halo = extra_x[:, LANES:], extra_x[:, :LANES]
        h2 = by_side(
            role,
            jnp.where(low_lanes, third_x[:, half : half + LANES], third_halo),
            jnp.where(low_lanes, third_halo, third_x[:, half - LANES : half]),
        )
        h3 = by_side(
            role,
            jnp.where(low_lanes, e[:, eighth : eighth + LANES], e_halo),
            jnp.where(low_lanes, e_halo, e[:, eighth - LANES : eighth]),
        )
        s2 = by_side(role, third_x[:, :half], third_x[:, half:])
        s3 = by_side(role, e[:, :eighth], e[:, eighth:])
        return jnp.concatenate([pick(halo, role), h2, h3, s2, s3], axis=1)

    x2_mine = second_part(side)
    x2_other = over(second_part(1 - side))

    extra_c = spread([pick(cotangent, 3)[:, piece * k : piece * (k + 1)] for k in range(4)])
    third_c = pick(cotangent, 2)

    def second_cot(role):
        s2 = by_side(role, third_c[:, :half], third_c[:, half:])
        s3 = by_side(role, extra_c[:, :eighth], extra_c[:, eighth:])
        return jnp.concatenate([s2, s3], axis=1)

    c1_mine, c2_mine = pick(cotangent, side), second_cot(side)
    c1_other = over(after(pick(cotangent, 1 - side), x1_other))
    c2_other = over(after(second_cot(1 - side), x2_other))

    places = shard * bins + jnp.arange(bins, dtype=jnp.int32)
    valid_rows = (places[None, :] < lengths[:, None]).astype(jnp.float32)[:, None, :]
    x_wide = inputs.astype(jnp.float32)
    mine = (jnp.arange(2) == side).astype(jnp.float32)[:, None, None]
    lead = ((shard == 0) & (group_at == 0)).astype(jnp.float32)
    stats = jnp.stack(
        [
            jnp.sum(valid_rows * x_wide, axis=(0, 2)),
            jnp.sum(valid_rows * x_wide * x_wide, axis=(0, 2)),
            lead * gain_in,
            lead * offset_in,
        ]
    )
    stats, filled = lax.psum(
        (mine * stats[None], 0.5 * jnp.sum(valid_rows)), axes
    )
    mean = stats[:, 0] / filled
    scale = lax.rsqrt(stats[:, 1] / filled - mean * mean + EPS)
    norm_all = jnp.stack([mean, scale, stats[:, 2], stats[:, 3]], axis=-1)
    cols_mine = lax.dynamic_index_in_dim(norm_all, side, 0, keepdims=False)
    cols_other = lax.dynamic_index_in_dim(norm_all, 1 - side, 0, keepdims=False)

    starts = (
        shard * bins,
        shard * bins + side * half,
        (shard % quarter) * bins + group * piece + side * eighth,
    )
    limits = (lax.dynamic_index_in_dim(ranked, side, 0, keepdims=False), ranked[2], ranked[3])
    valid_ext, valid_own = [], []
    for at, size, limit in zip(starts, (bins, half, eighth), limits, strict=True):
        spots = at - LANES + jnp.arange(size + 2 * LANES, dtype=jnp.int32)
        good = ((spots >= 0) & (spots < limit)).astype(jnp.float32)[None, :]
        valid_ext.append(good)
        valid_own.append(good[:, LANES : LANES + size])
    valid_ext = jnp.concatenate(valid_ext, axis=1)
    valid_own = jnp.concatenate(valid_own, axis=1)

    def activate(first, second, cols):
        h1, h2, h3 = (second[:, LANES * i : LANES * (i + 1)] for i in range(3))
        s2, s3 = second[:, 3 * LANES : 3 * LANES + half], second[:, 3 * LANES + half :]
        wide = jnp.concatenate([h1, first, h1, h2, s2, h2, h3, s3, h3], axis=1).astype(jnp.float32)
        norm = (wide - cols[:, 0:1]) * cols[:, 1:2]
        return (gelu(norm * cols[:, 2:3] + cols[:, 3:4]) * valid_ext).astype(jnp.bfloat16)

    act_mine = activate(x1_mine, x2_mine, cols_mine)
    act_other = activate(x1_other, x2_other, cols_other)

    turn = lambda w: jnp.transpose(w, (2, 0, 1)).reshape(bottle, taps * chans)
    conv_out, sum_first, sum_second = conv_forward(
        act_mine,
        act_other,
        jnp.concatenate([turn(conv_weight), turn(conv_other)], axis=1),
        valid_own,
        tiles,
    )
    sum_first, sum_second = lax.psum(
        (jnp.sum(sum_first, axis=1), jnp.sum(sum_second, axis=1)), axes
    )
    mean_mid = sum_first / filled
    scale_mid = lax.rsqrt(sum_second / filled - mean_mid * mean_mid + EPS)
    cols_mid = jnp.stack([mean_mid, scale_mid, gain_mid, offset_mid], axis=-1)

    norm_mid = (conv_out - cols_mid[:, 0:1]) * cols_mid[:, 1:2]
    act_mid = (gelu(norm_mid * cols_mid[:, 2:3] + cols_mid[:, 3:4]) * valid_own).astype(jnp.bfloat16)

    point_all = jnp.concatenate([point_weight, point_other], axis=1)
    grad1, beta1, gamma1, outer1 = mid_back(
        conv_out, act_mid, valid_own, c1_mine, c1_other, point_all, cols_mid, 0
    )
    grad2, beta2, gamma2, outer2 = mid_back(
        conv_out, act_mid, valid_own, c2_mine, c2_other, point_all, cols_mid, tiles[0]
    )
    grad_bias = jnp.sum(cotangent.astype(jnp.float32), axis=(0, 2))
    beta_mid, gamma_mid, grad_bias = lax.psum(
        (
            jnp.sum(beta1 + beta2, axis=1),
            jnp.sum(gamma1 + gamma2, axis=1),
            mine[:, 0] * grad_bias[None],
        ),
        axes,
    )
    grad_bias = lax.dynamic_index_in_dim(grad_bias, side, 0, keepdims=False)
    factor = (gain_mid * scale_mid)[:, None]

    def conv_grad(grad, lo, hi):
        kept = valid_own[:, lo:hi] * (beta_mid[:, None] + norm_mid[:, lo:hi] * gamma_mid[:, None])
        return (factor * (grad - kept / filled)).astype(jnp.bfloat16)

    low2 = conv_grad(grad2, bins, bins + half + eighth)
    low1 = conv_grad(grad1, 0, bins)

    act2_mine = after(act_mid[:, bins:], c1_other)
    act2_other = over(act2_mine)
    low2_other = over(after(low2, c2_other))
    low1_other = over(after(low1, act2_other))
    act1_mine = act_mid[:, :bins]
    act1_other = over(after(act1_mine, low2_other))

    grad_conv = conv_weight_back(act_mine, act_other, low1, low2, tiles)
    outer = outer1 + outer2
    depth = taps * chans
    sums = jnp.stack(
        [
            jnp.concatenate([grad_conv[:depth], outer[:, :chans]], axis=0),
            jnp.concatenate([grad_conv[depth:], outer[:, chans:]], axis=0),
        ]
    )
    sums = lax.psum_scatter(sums, ("win", "seq"), scatter_dimension=1, tiled=True)
    sums = lax.all_gather(sums[0] + over(sums[1]), ("win", "seq"), axis=0, tiled=True)
    grad_conv = sums[:depth].reshape(taps, chans, bottle)
    grad_point = sums[depth:]

    weight_out = jnp.transpose(point_weight)
    bias = point_bias[:, None]
    pair_of = lambda cells_mine, cells_other: by_side(
        side,
        jnp.concatenate([cells_mine, cells_other], axis=1),
        jnp.concatenate([cells_other, cells_mine], axis=1),
    )
    out_tile = 2 * TILE
    at_slot = lambda slot, tile: jnp.stack(
        [lax.dynamic_index_in_dim(order, slot, 0, keepdims=False), jnp.asarray(tile, jnp.int32)]
    )
    write = lambda prev, act, size, place: write_outputs(
        prev, act, size // out_tile, place, inputs, weight_out, bias
    )
    half_tiles = half // out_tile
    outputs = write(None, act1_mine, bins, at_slot(side, 0))
    outputs = write(outputs, act2_mine, half, at_slot(2, side * half_tiles))
    outputs = write(outputs, act2_other, half, at_slot(2, (1 - side) * half_tiles))
    act_quarter = collect(pair_of(act2_mine[:, half:], act2_other[:, half:]))
    outputs = write(outputs, act_quarter, bins, at_slot(3, 0))
    outputs = write(outputs, act1_other, bins, at_slot(1 - side, 0))

    low_quarter = collect(pair_of(low2[:, half:], low2_other[:, half:]))
    low_third = pair_of(low2[:, :half], low2_other[:, :half])
    slots = jnp.stack(
        [by_side(side, low1, low1_other), by_side(side, low1_other, low1), low_third, low_quarter]
    )
    edges = jnp.concatenate([slots[..., :LANES], slots[..., -LANES:]], axis=2)
    right = lax.ppermute(edges[..., :LANES], "seq", back_ends)
    left = lax.ppermute(edges[..., LANES:], "seq", ends)
    border = jnp.where(low_lanes, right, left)
    slots = jnp.concatenate([border, slots, border], axis=2)
    valid_slots = (places[None, :] < ranked[:, None]).astype(jnp.float32)[:, None, :]
    weight_back = jnp.transpose(conv_weight, (1, 0, 2)).reshape(chans, taps * bottle)
    grad_in, beta_in, gamma_in = input_back(
        order, slots, inputs, valid_slots, weight_back, cols_mine
    )
    beta_in, gamma_in = lax.psum(
        (jnp.sum(beta_in, axis=1), jnp.sum(gamma_in, axis=1)), ("seq", "win")
    )
    norm_in = (x_wide - cols_mine[:, 0:1]) * cols_mine[:, 1:2]
    factor_in = (cols_mine[:, 2] * cols_mine[:, 1])[:, None]
    grad_inputs = (
        cotangent.astype(jnp.float32)
        + factor_in
        * (grad_in - valid_rows * (column(beta_in) + norm_in * column(gamma_in)) / filled)
    ).astype(jnp.bfloat16)
    part = bottle // 2
    return (
        outputs,
        grad_inputs,
        gamma_in,
        beta_in,
        grad_conv,
        lax.dynamic_slice_in_dim(gamma_mid, side * part, part),
        lax.dynamic_slice_in_dim(beta_mid, side * part, part),
        grad_point,
        grad_bias,
    )


def solution(mesh):
    two_groups = mesh.shape["ch"] == 2 and mesh.shape["seq"] % 4 == 0

    def local(*args):
        windows, _, bins = args[0].shape
        if two_groups and windows == 4 and bins % (8 * TILE) == 0:
            return local_pair(*args)
        return local_any(*args)

    return jax.shard_map(
        local,
        mesh=mesh,
        in_specs=(
            P("win", "ch", "seq"),
            P("win"),
            P("ch"),
            P("ch"),
            P(None, "ch", None),
            P(),
            P(),
            P(None, "ch"),
            P("ch"),
            P("win", "ch", "seq"),
        ),
        out_specs=(
            P("win", "ch", "seq"),
            P("win", "ch", "seq"),
            P("ch"),
            P("ch"),
            P(None, "ch", None),
            P("ch"),
            P("ch"),
            P(None, "ch"),
            P("ch"),
        ),
        check_vma=False,
    )
```

```python
import jax
import jax.numpy as jnp
from jax import lax
from jax.experimental import pallas as pl
from jax.experimental.pallas import tpu as pltpu
from jax.sharding import PartitionSpec as P

DILATION_BINS = 57


EPS = 1e-05
LANES = 128
TILE = 384
VMEM_BYTES = 63 * 1000 * 1000


def with_halo(cells, sides, width):
    for axis, dim in sides:
        count = lax.axis_size(axis)
        ends = count - 1
        head = lax.slice_in_dim(cells, 0, width, axis=dim)
        tail = lax.slice_in_dim(cells, cells.shape[dim] - width, cells.shape[dim], axis=dim)
        cells = jnp.concatenate(
            [
                lax.ppermute(tail, axis, [(i, (i + 1) % count) for i in range(ends)]),
                cells,
                lax.ppermute(head, axis, [((i + 1) % count, i) for i in range(ends)]),
            ],
            axis=dim,
        )
    return cells


def norm_sums(first_term, second_term):
    return lax.psum((first_term, second_term), ("seq", "win"))


def column(vector):
    return vector[:, None]


def local_any(
    inputs,
    lengths,
    gain_in,
    offset_in,
    conv_weight,
    gain_mid,
    offset_mid,
    point_weight,
    point_bias,
    cotangent,
):
    win_count, chan_local, count_of_bins = inputs.shape
    count_of_taps = conv_weight.shape[0]
    bottle = conv_weight.shape[2]
    bottle_local = bottle // lax.axis_size("ch")
    offset_at = lax.axis_index("ch") * bottle_local
    places = lax.axis_index("seq") * count_of_bins + jnp.arange(count_of_bins, dtype=jnp.int32)
    valid_rows = (places[None, :] < lengths[:, None]).astype(jnp.float32)[:, None, :]
    x_wide = inputs.astype(jnp.float32)
    sum_first = jnp.sum(valid_rows * x_wide, axis=(0, 2))
    sum_second = jnp.sum(valid_rows * x_wide * x_wide, axis=(0, 2))
    sum_first, sum_second, filled = lax.psum(
        (sum_first, sum_second, jnp.sum(valid_rows)), ("seq", "win")
    )
    mean_in = sum_first / filled
    scale_in = lax.rsqrt(sum_second / filled - mean_in * mean_in + EPS)
    norm_in = (x_wide - column(mean_in)) * column(scale_in)
    pre_in = norm_in * column(gain_in) + column(offset_in)
    input_activation, gelu_in_back = jax.vjp(jax.nn.gelu, pre_in)
    lowered_activation = (input_activation * valid_rows).astype(jnp.bfloat16)
    padded_input = with_halo(lowered_activation, (("seq", 2),), DILATION_BINS)
    stacked_taps = jnp.concatenate(
        [
            padded_input[
                :,
                :,
                kernel_tap_index * DILATION_BINS : kernel_tap_index * DILATION_BINS + count_of_bins,
            ]
            for kernel_tap_index in range(count_of_taps)
        ],
        axis=1,
    )
    flat_weight = conv_weight.reshape(count_of_taps * chan_local, bottle)
    partial_value = jnp.einsum(
        "wkt,kf->wft", stacked_taps, flat_weight, preferred_element_type=jnp.float32
    )
    conv_out = lax.psum_scatter(partial_value, "ch", scatter_dimension=1, tiled=True)
    gain_part = lax.dynamic_slice_in_dim(gain_mid, offset_at, bottle_local)
    offset_part = lax.dynamic_slice_in_dim(offset_mid, offset_at, bottle_local)
    mid_first, mid_second = norm_sums(
        jnp.sum(valid_rows * conv_out, axis=(0, 2)),
        jnp.sum(valid_rows * conv_out * conv_out, axis=(0, 2)),
    )
    mean_mid = mid_first / filled
    scale_mid = lax.rsqrt(mid_second / filled - mean_mid * mean_mid + EPS)
    norm_mid = (conv_out - column(mean_mid)) * column(scale_mid)
    pre_mid = norm_mid * column(gain_part) + column(offset_part)
    act_mid, gelu_mid_back = jax.vjp(jax.nn.gelu, pre_mid)
    act_mid_low = (act_mid * valid_rows).astype(jnp.bfloat16)
    mixed_in = lax.all_gather(act_mid_low, "ch", axis=1, tiled=True)
    branch = jnp.einsum("wft,fc->wct", mixed_in, point_weight, preferred_element_type=jnp.float32)
    outputs = (x_wide + branch + column(point_bias)).astype(jnp.bfloat16)
    grad_point = jnp.einsum("wft,wct->fc", mixed_in, cotangent, preferred_element_type=jnp.float32)
    grad_bias = jnp.sum(cotangent.astype(jnp.float32), axis=(0, 2))
    partial_back = jnp.einsum(
        "wct,fc->wft", cotangent, point_weight, preferred_element_type=jnp.float32
    )
    grad_act_mid = lax.psum_scatter(partial_back, "ch", scatter_dimension=1, tiled=True)
    grad_pre_mid = gelu_mid_back(grad_act_mid * valid_rows)[0]
    local_beta = jnp.sum(grad_pre_mid, axis=(0, 2))
    local_gamma = jnp.sum(grad_pre_mid * norm_mid, axis=(0, 2))
    grad_point, grad_bias, beta_mid, gamma_mid = lax.psum(
        (grad_point, grad_bias, local_beta, local_gamma), ("seq", "win")
    )
    grad_conv_out = column(gain_part * scale_mid) * (
        grad_pre_mid - valid_rows * (column(beta_mid) + norm_mid * column(gamma_mid)) / filled
    )
    grad_low = grad_conv_out.astype(jnp.bfloat16)
    complete_gradient = lax.all_gather(grad_low, "ch", axis=1, tiled=True)
    grad_conv = jnp.einsum(
        "wkt,wft->kf", stacked_taps, complete_gradient, preferred_element_type=jnp.float32
    )
    grad_conv = grad_conv.reshape(count_of_taps, chan_local, bottle)
    padded_gradient = with_halo(complete_gradient, (("seq", 2),), DILATION_BINS)
    back_taps = jnp.concatenate(
        [
            padded_gradient[
                :,
                :,
                (count_of_taps - 1 - kernel_tap_index)
                * DILATION_BINS : (count_of_taps - 1 - kernel_tap_index)
                * DILATION_BINS
                + count_of_bins,
            ]
            for kernel_tap_index in range(count_of_taps)
        ],
        axis=1,
    )
    back_weight = jnp.transpose(conv_weight, (0, 2, 1)).reshape(count_of_taps * bottle, chan_local)
    grad_act_in = jnp.einsum(
        "wkt,kc->wct", back_taps, back_weight, preferred_element_type=jnp.float32
    )
    grad_pre_in = gelu_in_back(grad_act_in * valid_rows)[0]
    local_beta_in = jnp.sum(grad_pre_in, axis=(0, 2))
    local_gamma_in = jnp.sum(grad_pre_in * norm_in, axis=(0, 2))
    grad_conv, beta_in, gamma_in = lax.psum(
        (grad_conv, local_beta_in, local_gamma_in), ("seq", "win")
    )
    grad_inputs = (
        cotangent.astype(jnp.float32)
        + column(gain_in * scale_in)
        * (grad_pre_in - valid_rows * (column(beta_in) + norm_in * column(gamma_in)) / filled)
    ).astype(jnp.bfloat16)
    return (
        outputs,
        grad_inputs,
        gamma_in,
        beta_in,
        grad_conv,
        gamma_mid,
        beta_mid,
        grad_point,
        grad_bias,
    )


MESH = pl.DeviceIdType.MESH
ROWS = 32
PLANE = 16
F32 = jnp.float32
BF16 = jnp.bfloat16
GELU_A = 0.7978845608028654
GELU_B = 0.044715


def dot(a, b):
    return jnp.dot(a, b, preferred_element_type=F32)


def dot_t(a, b):
    return lax.dot_general(a, b, (((1,), (1,)), ((), ())), preferred_element_type=F32)


def lane_sum(cells):
    total = cells[:, :LANES]
    for at in range(LANES, cells.shape[1], LANES):
        total = total + cells[:, at : at + LANES]
    return total


def gelu(v):
    return 0.5 * v * (1.0 + jnp.tanh(GELU_A * (v + GELU_B * (v * v * v))))


def gelu_slope(v):
    square = v * v
    th = jnp.tanh(GELU_A * (v + GELU_B * (v * square)))
    return 0.5 * (1.0 + th) + 0.5 * v * (1.0 - th * th) * (GELU_A * (1.0 + 3.0 * GELU_B * square))


def lanes_at(at, size):
    return pl.ds(pl.multiple_of(at, LANES), size)


def by_rows(count, body):
    def step(i, carry):
        body(pl.ds(pl.multiple_of(i * ROWS, ROWS), ROWS))
        return carry

    lax.fori_loop(0, count // ROWS, step, 0)


def times(count, body):
    def step(i, carry):
        body(i)
        return carry

    lax.fori_loop(0, count, step, 0)


def spread_lanes(cells, size):
    return jnp.concatenate([cells] * (size // LANES), axis=1)


def to_column(row):
    return jnp.transpose(jnp.broadcast_to(row, (LANES, row.shape[1])))


def to_row(cells):
    return jnp.sum(jnp.transpose(cells), axis=0, keepdims=True)


class Copies:
    def __init__(self, send, recv):
        self.send, self.recv, self.used = send, recv, 0

    def take(self, count=1):
        self.used += count
        return self.used - count

    def remote(self, src, dst, device, send_at=None, recv_at=None):
        if send_at is None:
            send_at = self.take()
        if recv_at is None:
            recv_at = send_at
        return pltpu.make_async_remote_copy(
            src_ref=src,
            dst_ref=dst,
            send_sem=self.send.at[send_at],
            recv_sem=self.recv.at[recv_at],
            device_id=device,
            device_id_type=MESH,
        )

    def local(self, src, dst):
        return pltpu.make_async_copy(src, dst, self.send.at[self.take()])


class Place:
    def __init__(self):
        self.side, self.shard, self.win = (lax.axis_index(n) for n in ("ch", "seq", "win"))
        self.group, self.core = self.shard // 2, self.shard % 2
        self.me = self.win * 8 + self.shard
        self.partner = {"ch": 1 - self.side}

    def peer(self, step):
        at = (self.me + step) % PLANE
        return at, {"seq": at % 8, "win": at // 8}

    def greet(self):
        barrier = pltpu.get_barrier_semaphore()
        pl.semaphore_signal(barrier, 1, device_id=self.partner, device_id_type=MESH)
        for step in range(1, PLANE):
            pl.semaphore_signal(barrier, 1, device_id=self.peer(step)[1], device_id_type=MESH)
        pl.semaphore_wait(barrier, PLANE)


class PlaneSum:
    def __init__(self, copies, place, mine, slots):
        self.place, self.mine, self.slots = place, mine, slots
        first = copies.take(PLANE)
        self.out, self.into = [], []
        for step in range(1, PLANE):
            at, device = place.peer(step)
            self.out.append(
                copies.remote(mine, slots.at[place.me], device, first + step, first + place.me)
            )
            self.into.append(copies.remote(mine, slots.at[at], device, first + step, first + at))

    def start(self, rows):
        for at, row in enumerate(rows):
            self.mine[at : at + 1, :] = row
        for copy in self.out:
            copy.start()
        self.slots[self.place.me] = self.mine[...]

    def finish(self):
        for copy in self.into:
            copy.wait_recv()
        total = self.slots[0]
        for at in range(1, PLANE):
            total = total + self.slots[at]
        return total

    def drain(self):
        for copy in self.out:
            copy.wait_send()


A_MINE, B_MINE, A_OTHER, B_OTHER, MEAN, SCALE, GAIN, OFFSET, FACTOR, BETA, GAMMA = range(11)


def first_kernel(
    order, xin, cin, flat, w_mine, point, valid_rows, valid_ext, valid_own, vec,
    acts, g_own, g_two, g_extra, gw, gp, rows_out,
    xbuf, p1a, p2a, p1b, p2b, qext, ex, ec, halo_r, halo_l, hb,
    act_m, act_o, conv, actm, gco, w_all, w_other, e_act, cat, tmp, acc1, acc2, cols,
    msg, slots, ymsg, yin, send, recv,
):
    place = Place()
    side, group, core, partner = place.side, place.group, place.core, place.partner
    other = 1 - side
    copies = Copies(send, recv)
    windows, chans, bins = xbuf.shape
    half, piece, eighth, chunk = bins // 2, bins // 4, bins // 8, bins // 4
    base2, base3 = bins + 2 * LANES, bins + half + 4 * LANES
    own2, own3 = bins, bins + half
    low = lax.broadcasted_iota(jnp.int32, (ROWS, LANES), 1) < LANES // 2

    def put_rows(dst, at, load, size):
        def body(rows):
            dst[rows, lanes_at(at, size)] = load(rows)

        by_rows(chans, body)

    def column(at, row):
        cols[at] = to_column(row)

    def wide(at, rows, size):
        return spread_lanes(cols[at, rows, :], size)

    loads = [copies.local(xin.at[w], xbuf.at[w]) for w in range(windows)]
    for copy in loads:
        copy.start()
    place.greet()
    share = w_other.shape[0] // PLANE
    share_rows = lambda w, c, z, size=1: pl.ds(
        pl.multiple_of((w * 8 + c * 4 + z) * share, share), size * share
    )
    mine_at = share_rows(place.win, core, group)
    w_first = copies.remote(flat.at[mine_at], w_other.at[mine_at], partner)
    w_first.start()
    for copy in loads:
        copy.wait()
    put_rows(p1a, 0, lambda rows: xbuf[order[other], rows, :], bins)
    x1 = [
        copies.remote(p1a.at[:, i * chunk : (i + 1) * chunk], p2a.at[:, i * chunk : (i + 1) * chunk], partner)
        for i in range(4)
    ]
    x1[0].start()
    x1[1].start()
    to_left = copies.remote(xbuf.at[:, :, 0:LANES], halo_r, {"seq": jnp.maximum(place.shard - 1, 0)})
    to_right = copies.remote(xbuf.at[:, :, bins - LANES : bins], halo_l, {"seq": jnp.minimum(place.shard + 1, 7)})
    pl.when(place.shard > 0)(to_left.start)
    pl.when(place.shard < 7)(to_right.start)

    @pl.when(place.shard == 0)
    def _():
        halo_l[...] = jnp.zeros_like(halo_l)

    @pl.when(place.shard == 7)
    def _():
        halo_r[...] = jnp.zeros_like(halo_r)

    acc1[...] = jnp.zeros_like(acc1)
    acc2[...] = jnp.zeros_like(acc2)
    for w in range(windows):

        def body(rows, w=w):
            first, second = acc1[rows, :], acc2[rows, :]
            for at in range(0, bins, TILE):
                x = xbuf[w, rows, at : at + TILE].astype(F32)
                kept = x * valid_rows[w : w + 1, at : at + TILE]
                first = first + lane_sum(kept)
                second = second + lane_sum(kept * x)
            acc1[rows, :] = first
            acc2[rows, :] = second

        by_rows(chans, body)
    plane = [PlaneSum(copies, place, msg.at[i], slots.at[i]) for i in range(3)]
    over_y = [copies.remote(ymsg.at[i], yin.at[i], partner) for i in range(3)]
    plane[0].start([to_row(acc1[...]), to_row(acc2[...]), vec[4:5, :]])

    put_rows(qext, LANES, lambda rows: xbuf[order[3], rows, :], bins)
    w_all[:, : 3 * chans] = w_mine[...]
    total = plane[0].finish()
    filled = total[2:3, :]
    ymsg[0] = jnp.concatenate([total[0:3, :], vec[0:2, :], total[0:3, :]], axis=0)
    over_y[0].start()
    x1[2].start()
    x1[3].start()

    def norm_of(first, second, gain, offset):
        mean = first / filled
        scale = lax.rsqrt(second / filled - mean * mean + EPS)
        return mean, scale, scale * gain, offset - mean * scale * gain

    mean, scale, a_mine, b_mine = norm_of(total[0:1, :], total[1:2, :], vec[0:1, :], vec[1:2, :])
    column(A_MINE, a_mine)
    column(B_MINE, b_mine)
    rows_out[...] = jnp.zeros_like(rows_out)
    rows_out[0:1, :] = mean
    rows_out[1:2, :] = scale
    rows_out[2:3, :] = filled
    rows_out[6:8, :] = vec[0:2, :]

    w_first.wait_recv()
    z_first = copies.take(4)
    w_z = []
    for step in range(1, 4):
        z = (group + step) % 4
        device = {"seq": z * 2 + core}
        out = copies.remote(
            w_other.at[mine_at], w_other.at[mine_at], device, z_first + step, z_first + group
        )
        from_at = share_rows(place.win, core, z)
        w_z.append(
            copies.remote(w_other.at[from_at], w_other.at[from_at], device, z_first + step, z_first + z)
        )
        out.start()

    pl.when(place.shard < 7)(to_left.wait_recv)
    pl.when(place.shard > 0)(to_right.wait_recv)
    put_rows(qext, 0, lambda rows: halo_l[order[3], rows, :], LANES)
    put_rows(qext, LANES + bins, lambda rows: halo_r[order[3], rows, :], LANES)
    ex_at, ec_at = copies.take(3), copies.take(3)
    ex_out = [
        copies.remote(
            qext.at[:, k * piece : (k + 1) * piece + 2 * LANES], ex,
            {"seq": jnp.minimum(place.shard + 2 * k, 7)}, ex_at + k - 1, ex_at,
        )
        for k in range(1, 4)
    ]
    ec_out = [
        copies.remote(
            qext.at[:, LANES + k * piece : LANES + (k + 1) * piece], ec,
            {"seq": jnp.minimum(place.shard + 2 * k, 7)}, ec_at + k - 1, ec_at,
        )
        for k in range(1, 4)
    ]

    @pl.when(group == 0)
    def _():
        for copy in ex_out:
            copy.start()
        put_rows(ex, 0, lambda rows: qext[rows, 0 : piece + 2 * LANES], piece + 2 * LANES)

    def activate(a, b, load, dst, at, size):
        mask = valid_ext[:, lanes_at(at, size)]

        def body(rows):
            pre = load(rows).astype(F32) * wide(a, rows, size) + wide(b, rows, size)
            dst[rows, lanes_at(at, size)] = (gelu(pre) * mask).astype(BF16)

        by_rows(chans, body)

    def mixed(right, left):
        return jnp.where(low, right.astype(F32), left.astype(F32)).astype(BF16)

    def first_halo(role):
        w = order[role]
        return lambda rows: mixed(halo_r[w, rows, :], halo_l[w, rows, :])

    def second_halo(role):
        w = order[2]

        def load(rows):
            near = xbuf[w, rows, half : half + LANES].astype(F32)
            far = xbuf[w, rows, half - LANES : half].astype(F32)
            right = jnp.where(role == 0, near, halo_r[w, rows, :].astype(F32))
            left = jnp.where(role == 0, halo_l[w, rows, :].astype(F32), far)
            return jnp.where(low, right, left).astype(BF16)

        return load

    def third_halo(role):
        return lambda rows: mixed(
            ex[rows, lanes_at(LANES + (role + 1) * eighth, LANES)], ex[rows, lanes_at(role * eighth, LANES)]
        )

    def run_segment(a, b, load, dst, at, size):
        def body(i):
            activate(a, b, lambda rows: load(rows, i * TILE), dst, at + i * TILE, TILE)

        times(size // TILE, body)

    put_rows(hb.at[0], 0, first_halo(side), LANES)
    put_rows(hb.at[1], 0, second_halo(side), LANES)
    activate(A_MINE, B_MINE, lambda rows: hb[0, rows, :], act_m, 0, LANES)
    activate(A_MINE, B_MINE, lambda rows: hb[0, rows, :], act_m, LANES + bins, LANES)
    run_segment(
        A_MINE, B_MINE, lambda rows, at: xbuf[order[side], rows, lanes_at(at, TILE)], act_m, LANES, bins
    )
    put_rows(p1b, 0, first_halo(other), LANES)
    put_rows(p1b, LANES, second_halo(other), LANES)
    put_rows(p1b, 2 * LANES, lambda rows: xbuf[order[2], rows, lanes_at(other * half, half)], half)
    cuts2 = (0, 2 * LANES + half // 2, 2 * LANES + half, 3 * LANES + half + eighth)
    x2 = [copies.remote(p1b.at[:, lo:hi], p2b.at[:, lo:hi], partner) for lo, hi in zip(cuts2, cuts2[1:])]
    x2[0].start()
    for copy in w_z:
        copy.wait_recv()
    block = share_rows(place.win, core, 0, 4)
    block_in = share_rows(1 - place.win, core, 0, 4)
    across = {"win": 1 - place.win}
    w_x_at = copies.take()
    w_x = copies.remote(w_other.at[block], w_other.at[block], across, w_x_at, w_x_at)
    w_x_in = copies.remote(w_other.at[block_in], w_other.at[block_in], across, w_x_at, w_x_at)
    w_x.start()
    activate(A_MINE, B_MINE, lambda rows: hb[1, rows, :], act_m, base2, LANES)
    activate(A_MINE, B_MINE, lambda rows: hb[1, rows, :], act_m, base2 + LANES + half, LANES)
    run_segment(
        A_MINE, B_MINE, lambda rows, at: xbuf[order[2], rows, lanes_at(side * half + at, TILE)],
        act_m, base2 + LANES, half,
    )
    pl.when(place.shard > 0)(to_left.wait_send)
    pl.when(place.shard < 7)(to_right.wait_send)
    cot_loads = [copies.local(cin.at[w], xbuf.at[w]) for w in range(windows)]
    for copy in cot_loads:
        copy.start()
    w_x_in.wait_recv()
    sibling = {"seq": group * 2 + 1 - core}
    w_c_at = [copies.take() for _ in range(2)]
    w_c, w_c_in = [], []
    for w in range(2):
        rows = share_rows(w, core, 0, 4)
        rows_in = share_rows(w, 1 - core, 0, 4)
        w_c.append(copies.remote(w_other.at[rows], w_other.at[rows], sibling, w_c_at[w], w_c_at[w]))
        w_c_in.append(
            copies.remote(w_other.at[rows_in], w_other.at[rows_in], sibling, w_c_at[w], w_c_at[w])
        )
        w_c[w].start()

    over_y[0].wait_recv()
    _, _, a_other, b_other = norm_of(*(yin[0, i : i + 1, :] for i in (0, 1, 3, 4)))
    column(A_OTHER, a_other)
    column(B_OTHER, b_other)
    for copy in w_c_in:
        copy.wait_recv()
    for tap in range(3):
        w_all[:, (3 + tap) * chans : (4 + tap) * chans] = jnp.transpose(
            w_other[tap * chans : (tap + 1) * chans, :]
        )
    for i in range(4):
        x1[i].wait_recv()
        run_segment(
            A_OTHER, B_OTHER, lambda rows, at, i=i: p2a[rows, lanes_at(i * chunk + at, TILE)],
            act_o, LANES + i * chunk, chunk,
        )
        if i == 2:
            for copy in x1:
                copy.wait_send()
            x2[1].start()
    pl.when(group > 0)(lambda: ex_out[0].wait_recv())
    put_rows(p1b, cuts2[2], third_halo(other), LANES)
    put_rows(
        p1b, cuts2[2] + LANES, lambda rows: ex[rows, lanes_at(LANES + other * eighth, eighth)], eighth
    )
    x2[2].start()
    put_rows(hb.at[2], 0, third_halo(side), LANES)
    activate(A_MINE, B_MINE, lambda rows: hb[2, rows, :], act_m, base3, LANES)
    activate(A_MINE, B_MINE, lambda rows: hb[2, rows, :], act_m, base3 + LANES + eighth, LANES)
    run_segment(
        A_MINE, B_MINE, lambda rows, at: ex[rows, lanes_at(LANES + side * eighth + at, TILE)],
        act_m, base3 + LANES, eighth,
    )
    for copy in cot_loads:
        copy.wait()
    put_rows(p2a, 0, lambda rows: xbuf[order[other], rows, :], bins)

    @pl.when(group == 0)
    def _():
        for copy in ex_out:
            copy.wait_send()

    put_rows(qext, LANES, lambda rows: xbuf[order[3], rows, :], bins)

    @pl.when(group == 0)
    def _():
        for copy in ec_out:
            copy.start()
        put_rows(ec, 0, lambda rows: qext[rows, LANES : LANES + piece], piece)

    def fill_taps(start):
        for at_half, ref in enumerate((act_m, act_o)):
            cells = ref[:, lanes_at(start, TILE + 2 * LANES)]
            for tap in range(3):
                at = LANES + (tap - 1) * DILATION_BINS
                row = (at_half * 3 + tap) * chans
                cat[row : row + chans, :] = cells[:, at : at + TILE]

    def conv_tiles(start, own, count):
        def body(i):
            fill_taps(start + i * TILE)
            out = dot(w_all[...], cat[...])
            conv[:, lanes_at(own + i * TILE, TILE)] = out
            kept = out * valid_own[:, lanes_at(own + i * TILE, TILE)]
            acc1[...] += lane_sum(kept)
            acc2[...] += lane_sum(kept * out)

        times(count, body)

    acc1[...] = jnp.zeros_like(acc1)
    acc2[...] = jnp.zeros_like(acc2)
    x2[0].wait_recv()
    other_halo = lambda at: lambda rows: p2b[rows, at : at + LANES]
    activate(A_OTHER, B_OTHER, other_halo(0), act_o, 0, LANES)
    activate(A_OTHER, B_OTHER, other_halo(0), act_o, LANES + bins, LANES)
    activate(A_OTHER, B_OTHER, other_halo(LANES), act_o, base2, LANES)
    activate(A_OTHER, B_OTHER, other_halo(LANES), act_o, base2 + LANES + half, LANES)
    other_second = lambda rows, at: p2b[rows, lanes_at(2 * LANES + at, TILE)]
    run_segment(A_OTHER, B_OTHER, other_second, act_o, base2 + LANES, half // 2)
    conv_tiles(0, 0, bins // TILE)
    x2[1].wait_recv()
    c1 = [
        copies.remote(p2a.at[:, i * chunk : (i + 1) * chunk], p1a.at[:, i * chunk : (i + 1) * chunk], partner)
        for i in range(4)
    ]
    c1[0].start()
    c1[1].start()
    run_segment(
        A_OTHER, B_OTHER, lambda rows, at: other_second(rows, half // 2 + at),
        act_o, base2 + LANES + half // 2, half // 2,
    )
    conv_tiles(base2, own2, half // TILE)
    x2[2].wait_recv()
    activate(A_OTHER, B_OTHER, other_halo(cuts2[2]), act_o, base3, LANES)
    activate(A_OTHER, B_OTHER, other_halo(cuts2[2]), act_o, base3 + LANES + eighth, LANES)
    run_segment(
        A_OTHER, B_OTHER, lambda rows, at: p2b[rows, lanes_at(cuts2[2] + LANES + at, TILE)],
        act_o, base3 + LANES, eighth,
    )
    conv_tiles(base3, own3, eighth // TILE)
    plane[1].start([to_row(acc1[...]), to_row(acc2[...])])
    for copy in x2:
        copy.wait_send()
    c1[2].start()

    acc1[...] = jnp.zeros_like(acc1)
    for w in range(windows):

        def body(rows, w=w):
            acc1[rows, :] += lane_sum(xbuf[w, rows, :].astype(F32))

        by_rows(chans, body)
    bias_row = to_row(acc1[...])
    total = plane[1].finish()
    ymsg[1] = total
    over_y[1].start()
    c1[3].start()
    pl.when(group > 0)(lambda: ec_out[0].wait_recv())
    put_rows(p2b, 0, lambda rows: xbuf[order[2], rows, lanes_at(other * half, half)], half)
    put_rows(p2b, half, lambda rows: ec[rows, lanes_at(other * eighth, eighth)], eighth)
    cuts = (0, half // 2, half, half + eighth)
    c2 = [copies.remote(p2b.at[:, lo:hi], p1b.at[:, lo:hi], partner) for lo, hi in zip(cuts, cuts[1:])]
    c1[2].wait_recv()
    c2[0].start()

    over_y[1].wait_recv()
    total = ymsg[1] + yin[1]
    gain_mid, offset_mid = vec[2:3, :], vec[3:4, :]
    mean = total[0:1, :] / filled
    scale = lax.rsqrt(total[1:2, :] / filled - mean * mean + EPS)
    for at, row in ((MEAN, mean), (SCALE, scale), (GAIN, gain_mid), (OFFSET, offset_mid), (FACTOR, gain_mid * scale)):
        column(at, row)

    def act_tile(i):
        at = lanes_at(i * TILE, TILE)
        mask = valid_own[:, at]

        def body(rows):
            norm = (conv[rows, at] - wide(MEAN, rows, TILE)) * wide(SCALE, rows, TILE)
            pre = norm * wide(GAIN, rows, TILE) + wide(OFFSET, rows, TILE)
            actm[rows, at] = (gelu(pre) * mask).astype(BF16)

        by_rows(chans, body)

    times(conv.shape[1] // TILE, act_tile)
    keeps = [
        copies.local(actm.at[:, 0:bins], acts.at[side]),
        copies.local(actm.at[:, own2:own3], acts.at[2, :, lanes_at(side * half, half)]),
    ]
    for copy in keeps:
        copy.start()

    acc1[...] = jnp.zeros_like(acc1)
    acc2[...] = jnp.zeros_like(acc2)
    gp[...] = jnp.zeros_like(gp)

    def back_product(mine, theirs):
        cat[0:chans, :] = mine
        cat[chans : 2 * chans, :] = theirs
        tmp[...] = dot(point[...], cat[0:chans, :]) + dot(w_other[3 * chans :, :], cat[chans : 2 * chans, :])

    def grad_rows(rows, at, mask):
        norm = (conv[rows, at] - wide(MEAN, rows, TILE)) * wide(SCALE, rows, TILE)
        pre = norm * wide(GAIN, rows, TILE) + wide(OFFSET, rows, TILE)
        return norm, mask * gelu_slope(pre) * tmp[rows, :]

    def sum_tile(mine, theirs, own):
        back_product(mine, theirs)
        at = lanes_at(own, TILE)
        mask = valid_own[:, at]

        def body(rows):
            norm, part = grad_rows(rows, at, mask)
            acc1[rows, :] += lane_sum(part)
            acc2[rows, :] += lane_sum(part * norm)

        by_rows(chans, body)
        gp[...] += dot_t(actm[:, at], cat[0 : 2 * chans, :])

    def grad_tile(mine, theirs, own):
        back_product(mine, theirs)
        at = lanes_at(own, TILE)
        mask = valid_own[:, at]

        def body(rows):
            norm, part = grad_rows(rows, at, mask)
            kept = mask * (wide(BETA, rows, TILE) + norm * wide(GAMMA, rows, TILE))
            gco[rows, at] = (wide(FACTOR, rows, TILE) * (part - kept)).astype(BF16)

        by_rows(chans, body)

    def over_first(run, lo, hi):
        def body(i):
            at = lanes_at(lo + i * TILE, TILE)
            run(xbuf[order[side], :, at], p1a[:, at], lo + i * TILE)

        times((hi - lo) // TILE, body)

    def over_second(run, lo, hi):
        def body(i):
            at = lo + i * TILE
            run(
                xbuf[order[2], :, lanes_at(side * half + at, TILE)], p1b[:, lanes_at(at, TILE)], own2 + at
            )

        times((hi - lo) // TILE, body)

    def over_third(run):
        run(ec[:, lanes_at(side * eighth, TILE)], p1b[:, half : half + TILE], own3)

    t3_extra = copies.remote(actm.at[:, own3:], e_act, partner)
    t3 = [
        copies.remote(
            actm.at[:, own2 + i * TILE : own2 + (i + 1) * TILE],
            acts.at[2, :, lanes_at(side * half + i * TILE, TILE)],
            partner,
        )
        for i in range(half // TILE)
    ]
    for i in range(4):
        if i != 2:
            c1[i].wait_recv()
        if i == 3:
            c2[1].start()
            c2[2].start()
        over_first(sum_tile, i * chunk, (i + 1) * chunk)
    c2[0].wait_recv()
    over_second(sum_tile, 0, half // 2)
    c2[1].wait_recv()
    t3_extra.start()
    t3[0].start()
    over_second(sum_tile, half // 2, half)
    c2[2].wait_recv()
    over_third(sum_tile)
    plane[2].start([to_row(acc1[...]), to_row(acc2[...]), bias_row])
    total = plane[2].finish()
    ymsg[2] = total
    over_y[2].start()
    for copy in t3[1:]:
        copy.start()
    over_y[2].wait_recv()
    beta = ymsg[2, 0:1, :] + yin[2, 0:1, :]
    gamma = ymsg[2, 1:2, :] + yin[2, 1:2, :]
    rows_out[3:4, :] = beta
    rows_out[4:5, :] = gamma
    rows_out[5:6, :] = ymsg[2, 2:3, :]
    column(BETA, beta / filled)
    column(GAMMA, gamma / filled)

    over_third(grad_tile)
    t4_extra = copies.remote(gco.at[:, own3:], g_extra, partner)
    t4_extra.start()
    over_second(grad_tile, 0, half // 2)
    t4 = copies.remote(gco.at[:, own2 : own2 + half // 2], g_two, partner)
    t4.start()
    over_second(grad_tile, half // 2, half)
    over_first(grad_tile, 0, bins)
    g_keep = copies.local(gco, g_own)
    g_keep.start()

    back_to = {"seq": core}
    e_at = copies.take(8)
    t3_extra.wait_recv()
    e_home = [
        copies.remote(
            src, acts.at[3, :, lanes_at(group * piece + role * eighth, eighth)], back_to,
            e_at + which, e_at + 2 * group + which,
        )
        for which, (src, role) in enumerate(((actm.at[:, own3:], side), (e_act, other)))
    ]
    e_mine = [
        copies.local(src, acts.at[3, :, lanes_at(role * eighth, eighth)])
        for src, role in ((actm.at[:, own3:], side), (e_act, other))
    ]

    @pl.when(group > 0)
    def _():
        for copy in e_home:
            copy.start()

    @pl.when(group == 0)
    def _():
        for copy in e_mine:
            copy.start()

    weight_sum = conv.at[:, 0 : 6 * chans]
    weight_sum[...] = jnp.zeros_like(weight_sum)

    def weight_tiles(start, own, count):
        def body(i):
            fill_taps(start + i * TILE)
            weight_sum[...] += dot_t(gco[:, lanes_at(own + i * TILE, TILE)], cat[...])

        times(count, body)

    weight_tiles(0, 0, bins // TILE)
    weight_tiles(base2, own2, half // TILE)
    weight_tiles(base3, own3, eighth // TILE)

    gw_keep = copies.local(weight_sum, gw)
    gw_keep.start()

    @pl.when(group > 0)
    def _():
        for copy in e_home:
            copy.wait_send()

    @pl.when(group == 0)
    def _():
        for copy in e_mine:
            copy.wait()
        for copy in ec_out:
            copy.wait_send()
        for z in range(1, 4):
            for which, role in enumerate((side, other)):
                at = acts.at[3, :, lanes_at(z * piece + role * eighth, eighth)]
                copies.remote(at, at, back_to, e_at, e_at + 2 * z + which).wait_recv()

    for copy in keeps + [g_keep, gw_keep]:
        copy.wait()
    for copy in plane:
        copy.drain()
    for copy in [w_first, w_x, *w_c, *w_z, *over_y, *c1, *c2, t3_extra, *t3, t4_extra, t4]:
        copy.wait_send()
    for copy in [*t3, t4_extra, t4]:
        copy.wait_recv()


def second_kernel(
    order, xin, acts_in, g_own, g_two, g_extra, gw, gp, weight, valid, rows_in,
    acts, grads, rows_out, conv_grad, point_grad,
    gs, xbuf, halo_r, halo_l, cat, tmp, acc1, acc2, cols, msg, slots,
    parts, parts_core, parts_win, parts_z, parts_side, summed, send, recv,
):
    del acts_in
    place = Place()
    side, group, core, partner = place.side, place.group, place.core, place.partner
    other = 1 - side
    copies = Copies(send, recv)
    windows, chans, bins = xbuf.shape
    half, piece, eighth, chunk = bins // 2, bins // 4, bins // 8, bins // 4
    own2, own3 = bins, bins + half

    own_loads = [
        copies.local(g_own.at[:, 0:bins], gs.at[side, :, LANES : LANES + bins]),
        copies.local(g_own.at[:, own2:own3], gs.at[2, :, lanes_at(LANES + side * half, half)]),
        copies.local(g_two, gs.at[2, :, lanes_at(LANES + other * half, half // 2)]),
    ]
    extra = ((g_own.at[:, own3:], side), (g_extra, other))
    extra_loads = [
        copies.local(src, gs.at[3, :, lanes_at(LANES + role * eighth, eighth)]) for src, role in extra
    ]
    loads = [copies.local(xin.at[w], xbuf.at[w]) for w in range(windows)]
    depth = conv_grad.shape[0] * chans
    part_loads = [copies.local(gw.at[:, i * depth : (i + 1) * depth], parts.at[i, :, :depth]) for i in (0, 1)]
    part_loads += [copies.local(gp.at[:, i * chans : (i + 1) * chans], parts.at[i, :, depth:]) for i in (0, 1)]
    for copy in own_loads + loads + part_loads:
        copy.start()

    @pl.when(group == 0)
    def _():
        for copy in extra_loads:
            copy.start()

    place.greet()
    t4 = copies.remote(
        g_own.at[:, own2 + half // 2 : own3],
        gs.at[2, :, lanes_at(LANES + side * half + half // 2, half // 2)],
        partner,
    )
    t4_first = [
        copies.remote(
            g_own.at[:, i * chunk : (i + 1) * chunk],
            gs.at[side, :, LANES + i * chunk : LANES + (i + 1) * chunk],
            partner,
        )
        for i in range(4)
    ]
    t3_first = []
    for i in range(4):
        at = acts.at[side, :, i * chunk : (i + 1) * chunk]
        t3_first.append(copies.remote(at, at, partner))
    t4.start()
    for copy in t4_first:
        copy.start()
    t3_first[0].start()

    tail = parts_side.shape[0]
    core_rows = lambda c: pl.ds(pl.multiple_of(8 * tail * c, tail), 8 * tail)
    win_rows = lambda w: pl.ds(pl.multiple_of(8 * tail * core + 4 * tail * w, tail), 4 * tail)
    z_rows = lambda z: pl.ds(
        pl.multiple_of(8 * tail * core + 4 * tail * place.win + tail * z, tail), tail
    )
    sibling, across = {"seq": group * 2 + 1 - core}, {"win": 1 - place.win}
    s_core = copies.remote(parts.at[:, core_rows(1 - core), :], parts_core, sibling)
    s_win = copies.remote(parts.at[:, win_rows(1 - place.win), :], parts_win, across)
    s_z_at = copies.take(4)
    s_z, s_z_in = [], []
    g_z_at = copies.take(4)
    g_z, g_z_in = [], []
    for step in range(1, 4):
        z = (group + step) % 4
        device = {"seq": z * 2 + core}
        s_z.append(
            copies.remote(parts.at[:, z_rows(z), :], parts_z.at[group], device, s_z_at + step, s_z_at + group)
        )
        s_z_in.append(
            copies.remote(parts.at[:, z_rows(z), :], parts_z.at[z], device, s_z_at + step, s_z_at + z)
        )
        g_z.append(
            copies.remote(
                summed.at[z_rows(group), :], summed.at[z_rows(group), :], device, g_z_at + step, g_z_at + group
            )
        )
        g_z_in.append(
            copies.remote(summed.at[z_rows(z), :], summed.at[z_rows(z), :], device, g_z_at + step, g_z_at + z)
        )
    s_side = copies.remote(parts.at[1, z_rows(group), :], parts_side, partner)
    g_win_at, g_core_at = copies.take(), copies.take()
    both = lambda at, rows, rows_in, device: tuple(
        copies.remote(summed.at[r, :], summed.at[r, :], device, at, at) for r in (rows, rows_in)
    )
    g_win, g_win_in = both(g_win_at, win_rows(place.win), win_rows(1 - place.win), across)
    g_core, g_core_in = both(g_core_at, core_rows(core), core_rows(1 - core), sibling)
    for copy in part_loads:
        copy.wait()
    s_core.start()

    class Halo:
        def __init__(self, slot, last):
            self.slot, self.last = slot, last
            self.left = copies.remote(
                gs.at[slot, :, LANES : 2 * LANES], halo_r.at[slot], {"seq": jnp.maximum(place.shard - 1, 0)}
            )
            self.right = copies.remote(
                gs.at[slot, :, bins : bins + LANES], halo_l.at[slot], {"seq": jnp.minimum(place.shard + 1, 7)}
            )

        def start(self):
            pl.when((place.shard > 0) & (place.shard <= self.last))(self.left.start)
            pl.when(place.shard < self.last)(self.right.start)

        def finish(self):
            @pl.when(place.shard < self.last)
            def _():
                self.left.wait_recv()
                gs[self.slot, :, LANES + bins :] = halo_r[self.slot]

            @pl.when(place.shard >= self.last)
            def _():
                gs[self.slot, :, LANES + bins :] = jnp.zeros((chans, LANES), BF16)

            @pl.when(place.shard > 0)
            def _():
                self.right.wait_recv()
                gs[self.slot, :, 0:LANES] = halo_l[self.slot]

            @pl.when(place.shard == 0)
            def _():
                gs[self.slot, :, 0:LANES] = jnp.zeros((chans, LANES), BF16)

            pl.when((place.shard > 0) & (place.shard <= self.last))(self.left.wait_send)
            pl.when(place.shard < self.last)(self.right.wait_send)

    halos = {name: Halo(slot, last) for name, slot, last in (("own", side, 7), ("third", 2, 7), ("other", other, 7), ("quarter", 3, 1))}
    own_loads[0].wait()
    halos["own"].start()
    e_at = copies.take(8)
    back_to = {"seq": core}
    e_home = [
        copies.remote(
            src, gs.at[3, :, lanes_at(LANES + group * piece + role * eighth, eighth)], back_to,
            e_at + which, e_at + 2 * group + which,
        )
        for which, (src, role) in enumerate(extra)
    ]

    @pl.when(group > 0)
    def _():
        for copy in e_home:
            copy.start()

    names = {"mean": 0, "scale": 1, "gain": 2, "offset": 3}
    for at, row in enumerate((0, 1, 6, 7)):
        cols[at] = to_column(rows_in[row : row + 1, :])
    wide = lambda name, rows: spread_lanes(cols[names[name], rows, :], TILE)
    acc1[...] = jnp.zeros_like(acc1)
    acc2[...] = jnp.zeros_like(acc2)

    def through(slot):
        def tile(i):
            cells = gs[slot, :, lanes_at(i * TILE, TILE + 2 * LANES)]
            for tap in range(3):
                at = LANES - (tap - 1) * DILATION_BINS
                cat[tap * chans : (tap + 1) * chans, :] = cells[:, at : at + TILE]
            tmp[...] = dot(weight[...], cat[...])
            at = lanes_at(i * TILE, TILE)
            mask = valid[pl.ds(slot, 1), at]
            window = order[slot]

            def body(rows):
                norm = (xbuf[window, rows, at].astype(F32) - wide("mean", rows)) * wide("scale", rows)
                part = mask * gelu_slope(norm * wide("gain", rows) + wide("offset", rows)) * tmp[rows, :]
                acc1[rows, :] += lane_sum(part)
                acc2[rows, :] += lane_sum(part * norm)
                gs[slot, rows, at] = part.astype(BF16)

            by_rows(chans, body)

        times(bins // TILE, tile)

    keeps = []

    def keep(slot):
        copy = copies.local(gs.at[slot, :, 0:bins], grads.at[slot])
        copy.start()
        keeps.append(copy)

    for copy in loads:
        copy.wait()
    halos["own"].finish()
    through(side)
    keep(side)
    s_core.wait_recv()
    parts[:, core_rows(core), :] += parts_core[...]
    s_win.start()
    own_loads[1].wait()
    own_loads[2].wait()
    t4.wait_recv()
    halos["third"].start()
    quarter_keep = copies.local(gs.at[3, :, 0:bins], grads.at[3])

    @pl.when(group == 0)
    def _():
        for copy in extra_loads:
            copy.wait()
        for z in range(1, 4):
            for which, role in enumerate((side, other)):
                at = gs.at[3, :, lanes_at(LANES + z * piece + role * eighth, eighth)]
                copies.remote(at, at, back_to, e_at, e_at + 2 * z + which).wait_recv()
        halos["quarter"].start()

    halos["third"].finish()
    through(2)
    keep(2)
    s_win.wait_recv()
    parts[:, win_rows(place.win), :] += parts_win[...]
    for copy in s_z:
        copy.start()

    @pl.when(group == 0)
    def _():
        halos["quarter"].finish()
        through(3)
        quarter_keep.start()

    for copy in s_z_in:
        copy.wait_recv()
    parts_z[group] = parts[:, z_rows(group), :]
    total = parts_z[0]
    for z in range(1, 4):
        total = total + parts_z[z]
    parts[:, z_rows(group), :] = total
    s_side.start()
    for copy in t3_first[1:]:
        copy.start()
    for copy in t4_first:
        copy.wait_recv()
    halos["other"].start()
    halos["other"].finish()
    s_side.wait_recv()
    summed[z_rows(group), :] = parts[0, z_rows(group), :] + parts_side[...]
    for copy in g_z:
        copy.start()
    through(other)
    keep(other)
    plane = PlaneSum(copies, place, msg, slots)
    plane.start([to_row(acc1[...]), to_row(acc2[...])])
    for copy in g_z_in:
        copy.wait_recv()
    g_win.start()
    rows_out[...] = plane.finish()
    g_win_in.wait_recv()
    g_core.start()
    plane.drain()
    g_core_in.wait_recv()
    for tap in range(conv_grad.shape[0]):
        conv_grad[tap] = jnp.transpose(summed[:, tap * chans : (tap + 1) * chans])
    point_grad[...] = summed[:, depth:]
    for copy in [s_core, s_win, s_side, *s_z, *g_z, g_win, g_core]:
        copy.wait_send()
    for copy in keeps:
        copy.wait()

    @pl.when(group == 0)
    def _():
        quarter_keep.wait()

    @pl.when(group > 0)
    def _():
        for copy in e_home:
            copy.wait_send()

    for copy in [t4, *t4_first, *t3_first]:
        copy.wait_send()
    for copy in t3_first:
        copy.wait_recv()


def last_kernel(slot, x, c, act, grad, valid, weight, rows_one, rows_two, bias, out, grad_out, cols, tmp):
    del slot

    @pl.when((pl.program_id(0) == 0) & (pl.program_id(1) == 0))
    def _():
        mean, scale, filled, gain = (rows_one[i : i + 1, :] for i in (0, 1, 2, 6))
        for at, row in enumerate(
            (mean, scale, gain * scale, rows_two[0:1, :] / filled, rows_two[1:2, :] / filled, bias[...])
        ):
            cols[at] = to_column(row)

    mask = valid[0] > 0.0
    size = x.shape[2]
    cells = jnp.where(mask, act[0].astype(F32), 0.0).astype(BF16)
    tmp[...] = dot(weight[...], cells)
    wide = lambda at, rows: spread_lanes(cols[at, rows, :], size)

    def body(rows):
        xs = x[0, rows, :].astype(F32)
        out[0, rows, :] = (xs + tmp[rows, :] + wide(5, rows)).astype(BF16)
        norm = (xs - wide(0, rows)) * wide(1, rows)
        back = wide(2, rows) * (grad[0, rows, :].astype(F32) - (wide(3, rows) + norm * wide(4, rows)))
        grad_out[0, rows, :] = (c[0, rows, :].astype(F32) + jnp.where(mask, back, 0.0)).astype(BF16)

    by_rows(x.shape[1], body)


def local_pair(
    inputs,
    lengths,
    gain_in,
    offset_in,
    conv_weight,
    gain_mid,
    offset_mid,
    point_weight,
    point_bias,
    cotangent,
):
    windows, chans, bins = inputs.shape
    taps, _, bottle = conv_weight.shape
    side, shard, _ = (lax.axis_index(name) for name in ("ch", "seq", "win"))
    group = shard // 2
    piece, half, eighth = bins // 4, bins // 2, bins // 8
    widened, packed = bins + half + eighth + 6 * LANES, bins + half + eighth

    ids = jnp.arange(windows, dtype=jnp.int32)
    ahead = (lengths[None, :] > lengths[:, None]) | (
        (lengths[None, :] == lengths[:, None]) & (ids[None, :] < ids[:, None])
    )
    rank = jnp.sum(ahead.astype(jnp.int32), axis=1)
    chosen = rank[None, :] == ids[:, None]
    order = jnp.sum(jnp.where(chosen, ids[None, :], 0), axis=1)
    ranked = jnp.sum(jnp.where(chosen, lengths[None, :], 0), axis=1)

    places = shard * bins + jnp.arange(bins, dtype=jnp.int32)
    valid_rows = (places[None, :] < lengths[:, None]).astype(F32)
    valid_slots = (places[None, :] < ranked[:, None]).astype(F32)
    starts = (
        shard * bins,
        shard * bins + side * half,
        (shard % 2) * bins + group * piece + side * eighth,
    )
    limits = (jnp.where(side == 0, ranked[0], ranked[1]), ranked[2], ranked[3])
    spots = jnp.concatenate(
        [
            at - LANES + jnp.arange(size + 2 * LANES, dtype=jnp.int32)
            for at, size in zip(starts, (bins, half, eighth), strict=True)
        ]
    )
    limit = jnp.concatenate(
        [
            jnp.full((size + 2 * LANES,), at, jnp.int32)
            for at, size in zip(limits, (bins, half, eighth), strict=True)
        ]
    )
    valid_ext = ((spots >= 0) & (spots < limit)).astype(F32)[None, :]
    valid_own = jnp.concatenate(
        [
            valid_ext[:, at : at + size]
            for at, size in (
                (LANES, bins),
                (bins + 3 * LANES, half),
                (bins + half + 5 * LANES, eighth),
            )
        ],
        axis=1,
    )
    kept = jnp.sum(jnp.clip(lengths - shard * bins, 0, bins)).astype(F32)
    zero = jnp.zeros((chans,), F32)
    vec = jnp.stack(
        [gain_in, offset_in, gain_mid, offset_mid, jnp.full((chans,), kept), zero, zero, zero]
    )
    turn = lambda w: jnp.transpose(w, (2, 0, 1)).reshape(bottle, taps * chans)
    flat = jnp.concatenate([conv_weight.reshape(taps * chans, bottle), point_weight], axis=0)

    vmem = pl.BlockSpec(memory_space=pltpu.VMEM)
    hbm = pl.BlockSpec(memory_space=pl.ANY)
    smem = pl.BlockSpec(memory_space=pltpu.SMEM)
    shape = jax.ShapeDtypeStruct
    acts, g_own, g_two, g_extra, gw, gp, rows_one = pl.pallas_call(
        first_kernel,
        in_specs=[smem, hbm, hbm, hbm, vmem, vmem, vmem, vmem, vmem, vmem],
        out_specs=[hbm, hbm, hbm, hbm, hbm, vmem, vmem],
        out_shape=[
            shape((windows, bottle, bins), BF16),
            shape((bottle, packed), BF16),
            shape((bottle, half // 2), BF16),
            shape((bottle, eighth), BF16),
            shape((bottle, 2 * taps * chans), F32),
            shape((bottle, 2 * chans), F32),
            shape((8, chans), F32),
        ],
        scratch_shapes=[
            pltpu.VMEM((windows, chans, bins), BF16),
            pltpu.VMEM((chans, bins), BF16),
            pltpu.VMEM((chans, bins), BF16),
            pltpu.VMEM((chans, half + eighth + 3 * LANES), BF16),
            pltpu.VMEM((chans, half + eighth + 3 * LANES), BF16),
            pltpu.VMEM((chans, bins + 2 * LANES), BF16),
            pltpu.VMEM((chans, piece + 2 * LANES), BF16),
            pltpu.VMEM((chans, piece), BF16),
            pltpu.VMEM((windows, chans, LANES), BF16),
            pltpu.VMEM((windows, chans, LANES), BF16),
            pltpu.VMEM((3, chans, LANES), BF16),
            pltpu.VMEM((chans, widened), BF16),
            pltpu.VMEM((chans, widened), BF16),
            pltpu.VMEM((bottle, packed), F32),
            pltpu.VMEM((bottle, packed), BF16),
            pltpu.VMEM((bottle, packed), BF16),
            pltpu.VMEM((bottle, 2 * taps * chans), BF16),
            pltpu.VMEM(((taps + 1) * chans, bottle), BF16),
            pltpu.VMEM((bottle, eighth), BF16),
            pltpu.VMEM((2 * taps * chans, TILE), BF16),
            pltpu.VMEM((bottle, TILE), F32),
            pltpu.VMEM((chans, LANES), F32),
            pltpu.VMEM((chans, LANES), F32),
            pltpu.VMEM((11, chans, LANES), F32),
            pltpu.VMEM((3, 8, chans), F32),
            pltpu.VMEM((3, PLANE, 8, chans), F32),
            pltpu.VMEM((3, 8, chans), F32),
            pltpu.VMEM((3, 8, chans), F32),
            pltpu.SemaphoreType.DMA((128,)),
            pltpu.SemaphoreType.DMA((128,)),
        ],
        compiler_params=pltpu.CompilerParams(
            collective_id=0, has_side_effects=True, vmem_limit_bytes=VMEM_BYTES
        ),
        cost_estimate=pl.CostEstimate(flops=60 * 10**9, bytes_accessed=10**8, transcendentals=0),
    )(
        order, inputs, cotangent, flat, turn(conv_weight), point_weight,
        valid_rows, valid_ext, valid_own, vec,
    )

    weight_back = jnp.transpose(conv_weight, (1, 0, 2)).reshape(chans, taps * bottle)
    share = bottle // PLANE
    acts, grads, rows_two, conv_grad, point_grad = pl.pallas_call(
        second_kernel,
        in_specs=[smem, hbm, hbm, hbm, hbm, hbm, hbm, hbm, vmem, vmem, vmem],
        out_specs=[hbm, hbm, vmem, vmem, vmem],
        out_shape=[
            shape((windows, bottle, bins), BF16),
            shape((windows, chans, bins), BF16),
            shape((8, chans), F32),
            shape((taps, chans, bottle), F32),
            shape((bottle, chans), F32),
        ],
        input_output_aliases={2: 0},
        scratch_shapes=[
            pltpu.VMEM((windows, bottle, bins + 2 * LANES), BF16),
            pltpu.VMEM((windows, chans, bins), BF16),
            pltpu.VMEM((windows, bottle, LANES), BF16),
            pltpu.VMEM((windows, bottle, LANES), BF16),
            pltpu.VMEM((taps * bottle, TILE), BF16),
            pltpu.VMEM((chans, TILE), F32),
            pltpu.VMEM((chans, LANES), F32),
            pltpu.VMEM((chans, LANES), F32),
            pltpu.VMEM((4, chans, LANES), F32),
            pltpu.VMEM((8, chans), F32),
            pltpu.VMEM((PLANE, 8, chans), F32),
            pltpu.VMEM((2, bottle, (taps + 1) * chans), F32),
            pltpu.VMEM((2, bottle // 2, (taps + 1) * chans), F32),
            pltpu.VMEM((2, bottle // 4, (taps + 1) * chans), F32),
            pltpu.VMEM((4, 2, share, (taps + 1) * chans), F32),
            pltpu.VMEM((share, (taps + 1) * chans), F32),
            pltpu.VMEM((bottle, (taps + 1) * chans), F32),
            pltpu.SemaphoreType.DMA((128,)),
            pltpu.SemaphoreType.DMA((128,)),
        ],
        compiler_params=pltpu.CompilerParams(
            collective_id=1, has_side_effects=True, vmem_limit_bytes=52 * 1000 * 1000
        ),
        cost_estimate=pl.CostEstimate(flops=60 * 10**9, bytes_accessed=10**8, transcendentals=0),
    )(order, inputs, acts, g_own, g_two, g_extra, gw, gp, weight_back, valid_slots, rows_one)

    tile = 2 * TILE
    at = pl.BlockSpec((1, chans, tile), lambda w, i, p: (w, 0, i))
    at_slot = pl.BlockSpec((1, chans, tile), lambda w, i, p: (p[w], 0, i))
    whole = lambda rows, size: pl.BlockSpec((rows, size), lambda w, i, p: (0, 0))
    outputs, grad_inputs = pl.pallas_call(
        last_kernel,
        grid_spec=pltpu.PrefetchScalarGridSpec(
            num_scalar_prefetch=1,
            grid=(windows, bins // tile),
            in_specs=[
                at, at, at_slot, at_slot,
                pl.BlockSpec((1, 1, tile), lambda w, i, p: (w, 0, i)),
                whole(chans, bottle), whole(8, chans), whole(8, chans), whole(1, chans),
            ],
            out_specs=[at, at],
            scratch_shapes=[pltpu.VMEM((6, chans, LANES), F32), pltpu.VMEM((chans, tile), F32)],
        ),
        out_shape=[shape(inputs.shape, BF16), shape(inputs.shape, BF16)],
        compiler_params=pltpu.CompilerParams(vmem_limit_bytes=40 * 1024 * 1024),
        cost_estimate=pl.CostEstimate(flops=4 * 10**9, bytes_accessed=6 * 10**7, transcendentals=0),
    )(
        rank, inputs, cotangent, acts, grads, valid_rows[:, None, :], jnp.transpose(point_weight),
        rows_one, rows_two, point_bias[None, :],
    )
    part = bottle // 2
    return (
        outputs,
        grad_inputs,
        rows_two[1],
        rows_two[0],
        conv_grad,
        lax.dynamic_slice_in_dim(rows_one[4], side * part, part),
        lax.dynamic_slice_in_dim(rows_one[3], side * part, part),
        point_grad,
        rows_one[5],
    )


def solution(mesh):
    paired = mesh.shape["ch"] == 2 and mesh.shape["seq"] == 8 and mesh.shape["win"] == 2

    def local(*args):
        windows, chans, bins = args[0].shape
        if paired and windows == 4 and chans == args[4].shape[2] and bins == 8 * TILE:
            return local_pair(*args)
        return local_any(*args)

    return jax.shard_map(
        local,
        mesh=mesh,
        in_specs=(
            P("win", "ch", "seq"),
            P("win"),
            P("ch"),
            P("ch"),
            P(None, "ch", None),
            P(),
            P(),
            P(None, "ch"),
            P("ch"),
            P("win", "ch", "seq"),
        ),
        out_specs=(
            P("win", "ch", "seq"),
            P("win", "ch", "seq"),
            P("ch"),
            P("ch"),
            P(None, "ch", None),
            P("ch"),
            P("ch"),
            P(None, "ch"),
            P("ch"),
        ),
        check_vma=False,
    )
```

```python
import jax
import jax.numpy as jnp
from jax import lax
from jax.experimental import pallas as pl
from jax.experimental.pallas import tpu as pltpu
from jax.sharding import PartitionSpec as P

DILATION_BINS = 57


EPS = 1e-05
LANES = 128
TILE = 384
VMEM_BYTES = 63 * 1000 * 1000


def with_halo(cells, sides, width):
    for axis, dim in sides:
        count = lax.axis_size(axis)
        ends = count - 1
        head = lax.slice_in_dim(cells, 0, width, axis=dim)
        tail = lax.slice_in_dim(cells, cells.shape[dim] - width, cells.shape[dim], axis=dim)
        cells = jnp.concatenate(
            [
                lax.ppermute(tail, axis, [(i, (i + 1) % count) for i in range(ends)]),
                cells,
                lax.ppermute(head, axis, [((i + 1) % count, i) for i in range(ends)]),
            ],
            axis=dim,
        )
    return cells


def norm_sums(first_term, second_term):
    return lax.psum((first_term, second_term), ("seq", "win"))


def column(vector):
    return vector[:, None]


def local_any(
    inputs,
    lengths,
    gain_in,
    offset_in,
    conv_weight,
    gain_mid,
    offset_mid,
    point_weight,
    point_bias,
    cotangent,
):
    win_count, chan_local, count_of_bins = inputs.shape
    count_of_taps = conv_weight.shape[0]
    bottle = conv_weight.shape[2]
    bottle_local = bottle // lax.axis_size("ch")
    offset_at = lax.axis_index("ch") * bottle_local
    places = lax.axis_index("seq") * count_of_bins + jnp.arange(count_of_bins, dtype=jnp.int32)
    valid_rows = (places[None, :] < lengths[:, None]).astype(jnp.float32)[:, None, :]
    x_wide = inputs.astype(jnp.float32)
    sum_first = jnp.sum(valid_rows * x_wide, axis=(0, 2))
    sum_second = jnp.sum(valid_rows * x_wide * x_wide, axis=(0, 2))
    sum_first, sum_second, filled = lax.psum(
        (sum_first, sum_second, jnp.sum(valid_rows)), ("seq", "win")
    )
    mean_in = sum_first / filled
    scale_in = lax.rsqrt(sum_second / filled - mean_in * mean_in + EPS)
    norm_in = (x_wide - column(mean_in)) * column(scale_in)
    pre_in = norm_in * column(gain_in) + column(offset_in)
    input_activation, gelu_in_back = jax.vjp(jax.nn.gelu, pre_in)
    lowered_activation = (input_activation * valid_rows).astype(jnp.bfloat16)
    padded_input = with_halo(lowered_activation, (("seq", 2),), DILATION_BINS)
    stacked_taps = jnp.concatenate(
        [
            padded_input[
                :,
                :,
                kernel_tap_index * DILATION_BINS : kernel_tap_index * DILATION_BINS + count_of_bins,
            ]
            for kernel_tap_index in range(count_of_taps)
        ],
        axis=1,
    )
    flat_weight = conv_weight.reshape(count_of_taps * chan_local, bottle)
    partial_value = jnp.einsum(
        "wkt,kf->wft", stacked_taps, flat_weight, preferred_element_type=jnp.float32
    )
    conv_out = lax.psum_scatter(partial_value, "ch", scatter_dimension=1, tiled=True)
    gain_part = lax.dynamic_slice_in_dim(gain_mid, offset_at, bottle_local)
    offset_part = lax.dynamic_slice_in_dim(offset_mid, offset_at, bottle_local)
    mid_first, mid_second = norm_sums(
        jnp.sum(valid_rows * conv_out, axis=(0, 2)),
        jnp.sum(valid_rows * conv_out * conv_out, axis=(0, 2)),
    )
    mean_mid = mid_first / filled
    scale_mid = lax.rsqrt(mid_second / filled - mean_mid * mean_mid + EPS)
    norm_mid = (conv_out - column(mean_mid)) * column(scale_mid)
    pre_mid = norm_mid * column(gain_part) + column(offset_part)
    act_mid, gelu_mid_back = jax.vjp(jax.nn.gelu, pre_mid)
    act_mid_low = (act_mid * valid_rows).astype(jnp.bfloat16)
    mixed_in = lax.all_gather(act_mid_low, "ch", axis=1, tiled=True)
    branch = jnp.einsum("wft,fc->wct", mixed_in, point_weight, preferred_element_type=jnp.float32)
    outputs = (x_wide + branch + column(point_bias)).astype(jnp.bfloat16)
    grad_point = jnp.einsum("wft,wct->fc", mixed_in, cotangent, preferred_element_type=jnp.float32)
    grad_bias = jnp.sum(cotangent.astype(jnp.float32), axis=(0, 2))
    partial_back = jnp.einsum(
        "wct,fc->wft", cotangent, point_weight, preferred_element_type=jnp.float32
    )
    grad_act_mid = lax.psum_scatter(partial_back, "ch", scatter_dimension=1, tiled=True)
    grad_pre_mid = gelu_mid_back(grad_act_mid * valid_rows)[0]
    local_beta = jnp.sum(grad_pre_mid, axis=(0, 2))
    local_gamma = jnp.sum(grad_pre_mid * norm_mid, axis=(0, 2))
    grad_point, grad_bias, beta_mid, gamma_mid = lax.psum(
        (grad_point, grad_bias, local_beta, local_gamma), ("seq", "win")
    )
    grad_conv_out = column(gain_part * scale_mid) * (
        grad_pre_mid - valid_rows * (column(beta_mid) + norm_mid * column(gamma_mid)) / filled
    )
    grad_low = grad_conv_out.astype(jnp.bfloat16)
    complete_gradient = lax.all_gather(grad_low, "ch", axis=1, tiled=True)
    grad_conv = jnp.einsum(
        "wkt,wft->kf", stacked_taps, complete_gradient, preferred_element_type=jnp.float32
    )
    grad_conv = grad_conv.reshape(count_of_taps, chan_local, bottle)
    padded_gradient = with_halo(complete_gradient, (("seq", 2),), DILATION_BINS)
    back_taps = jnp.concatenate(
        [
            padded_gradient[
                :,
                :,
                (count_of_taps - 1 - kernel_tap_index)
                * DILATION_BINS : (count_of_taps - 1 - kernel_tap_index)
                * DILATION_BINS
                + count_of_bins,
            ]
            for kernel_tap_index in range(count_of_taps)
        ],
        axis=1,
    )
    back_weight = jnp.transpose(conv_weight, (0, 2, 1)).reshape(count_of_taps * bottle, chan_local)
    grad_act_in = jnp.einsum(
        "wkt,kc->wct", back_taps, back_weight, preferred_element_type=jnp.float32
    )
    grad_pre_in = gelu_in_back(grad_act_in * valid_rows)[0]
    local_beta_in = jnp.sum(grad_pre_in, axis=(0, 2))
    local_gamma_in = jnp.sum(grad_pre_in * norm_in, axis=(0, 2))
    grad_conv, beta_in, gamma_in = lax.psum(
        (grad_conv, local_beta_in, local_gamma_in), ("seq", "win")
    )
    grad_inputs = (
        cotangent.astype(jnp.float32)
        + column(gain_in * scale_in)
        * (grad_pre_in - valid_rows * (column(beta_in) + norm_in * column(gamma_in)) / filled)
    ).astype(jnp.bfloat16)
    return (
        outputs,
        grad_inputs,
        gamma_in,
        beta_in,
        grad_conv,
        gamma_mid,
        beta_mid,
        grad_point,
        grad_bias,
    )


MESH = pl.DeviceIdType.MESH
ROWS = 32
PLANE = 16
F32 = jnp.float32
BF16 = jnp.bfloat16
GELU_A = 0.7978845608028654
GELU_B = 0.044715


def dot(a, b):
    return jnp.dot(a, b, preferred_element_type=F32)


def dot_t(a, b):
    return lax.dot_general(a, b, (((1,), (1,)), ((), ())), preferred_element_type=F32)


def lane_sum(cells):
    total = cells[:, :LANES]
    for at in range(LANES, cells.shape[1], LANES):
        total = total + cells[:, at : at + LANES]
    return total


def gelu(v):
    return 0.5 * v * (1.0 + jnp.tanh(GELU_A * (v + GELU_B * (v * v * v))))


def gelu_slope(v):
    square = v * v
    th = jnp.tanh(GELU_A * (v + GELU_B * (v * square)))
    return 0.5 * (1.0 + th) + 0.5 * v * (1.0 - th * th) * (GELU_A * (1.0 + 3.0 * GELU_B * square))


def lanes_at(at, size):
    return pl.ds(pl.multiple_of(at, LANES), size)


def by_rows(count, body):
    def step(i, carry):
        body(pl.ds(pl.multiple_of(i * ROWS, ROWS), ROWS))
        return carry

    lax.fori_loop(0, count // ROWS, step, 0)


def times(count, body):
    def step(i, carry):
        body(i)
        return carry

    lax.fori_loop(0, count, step, 0)


def spread_lanes(cells, size):
    return jnp.concatenate([cells] * (size // LANES), axis=1)


def to_column(row):
    return jnp.transpose(jnp.broadcast_to(row, (LANES, row.shape[1])))


def to_row(cells):
    return jnp.sum(jnp.transpose(cells), axis=0, keepdims=True)


class Copies:
    def __init__(self, send, recv):
        self.send, self.recv, self.used = send, recv, 0

    def take(self, count=1):
        self.used += count
        return self.used - count

    def remote(self, src, dst, device, send_at=None, recv_at=None):
        if send_at is None:
            send_at = self.take()
        if recv_at is None:
            recv_at = send_at
        return pltpu.make_async_remote_copy(
            src_ref=src,
            dst_ref=dst,
            send_sem=self.send.at[send_at],
            recv_sem=self.recv.at[recv_at],
            device_id=device,
            device_id_type=MESH,
        )

    def local(self, src, dst):
        return pltpu.make_async_copy(src, dst, self.send.at[self.take()])


class Place:
    def __init__(self):
        self.side, self.shard, self.win = (lax.axis_index(n) for n in ("ch", "seq", "win"))
        self.group, self.core = self.shard // 2, self.shard % 2
        self.me = self.win * 8 + self.shard
        self.partner = {"ch": 1 - self.side}

    def peer(self, step):
        at = (self.me + step) % PLANE
        return at, {"seq": at % 8, "win": at // 8}

    def greet(self):
        barrier = pltpu.get_barrier_semaphore()
        pl.semaphore_signal(barrier, 1, device_id=self.partner, device_id_type=MESH)
        for step in range(1, PLANE):
            pl.semaphore_signal(barrier, 1, device_id=self.peer(step)[1], device_id_type=MESH)
        pl.semaphore_wait(barrier, PLANE)


class PlaneSum:
    def __init__(self, copies, place, mine, slots):
        self.place, self.mine, self.slots = place, mine, slots
        first = copies.take(PLANE)
        self.out, self.into = [], []
        for step in range(1, PLANE):
            at, device = place.peer(step)
            self.out.append(
                copies.remote(mine, slots.at[place.me], device, first + step, first + place.me)
            )
            self.into.append(copies.remote(mine, slots.at[at], device, first + step, first + at))

    def start(self, rows):
        for at, row in enumerate(rows):
            self.mine[at : at + 1, :] = row
        for copy in self.out:
            copy.start()
        self.slots[self.place.me] = self.mine[...]

    def finish(self):
        for copy in self.into:
            copy.wait_recv()
        total = self.slots[0]
        for at in range(1, PLANE):
            total = total + self.slots[at]
        return total

    def drain(self):
        for copy in self.out:
            copy.wait_send()


A_MINE, B_MINE, A_OTHER, B_OTHER, MEAN, SCALE, GAIN, OFFSET, FACTOR, BETA, GAMMA = range(11)


class Order:
    def __init__(self, lengths):
        self.lengths = [lengths[i] for i in range(4)]
        ranks = []
        for i, mine in enumerate(self.lengths):
            rank = jnp.int32(0)
            for j, their in enumerate(self.lengths):
                if j < i:
                    rank = rank + jnp.where(their >= mine, 1, 0)
                elif j > i:
                    rank = rank + jnp.where(their > mine, 1, 0)
            ranks.append(rank)

        def at_slot(slot, values):
            found = jnp.int32(0)
            for rank, value in zip(ranks, values, strict=True):
                found = found + jnp.where(rank == slot, value, 0)
            return found

        self.windows = [at_slot(slot, range(4)) for slot in range(4)]
        self.sizes = [at_slot(slot, self.lengths) for slot in range(4)]

    def of(self, values, slot):
        if isinstance(slot, int):
            return values[slot]
        found = values[0]
        for at in range(1, 4):
            found = jnp.where(slot == at, values[at], found)
        return found

    def __getitem__(self, slot):
        return self.of(self.windows, slot)

    def size(self, slot):
        return self.of(self.sizes, slot)


def valid_lanes(start, size, limit):
    spots = start + lax.broadcasted_iota(jnp.int32, (1, size), 1)
    return ((spots >= 0) & (spots < limit)).astype(F32)


def as_row(ref):
    return ref[...].reshape(1, ref.shape[0])


def first_kernel(
    lengths, xin, cin, weight_hbm, point_hbm, weight, point, gains_in, offsets_in, gains_mid, offsets_mid,
    acts, g_own, g_two, g_extra, gw, gp, rows_out,
    xbuf, p1a, p2a, p1b, p2b, qext, ex, ec, halo_r, halo_l, hb,
    act_m, act_o, conv, actm, gco, w_all, w_other, e_act, cat, tmp, acc1, acc2, cols,
    msg, slots, ymsg, yin, valid_rows, valid_ext, valid_own, send, recv,
):
    place = Place()
    side, group, core, partner = place.side, place.group, place.core, place.partner
    other = 1 - side
    copies = Copies(send, recv)
    windows, chans, bins = xbuf.shape
    half, piece, eighth, chunk = bins // 2, bins // 4, bins // 8, bins // 4
    base2, base3 = bins + 2 * LANES, bins + half + 4 * LANES
    own2, own3 = bins, bins + half
    low = lax.broadcasted_iota(jnp.int32, (ROWS, LANES), 1) < LANES // 2
    order = Order(lengths)

    def put_rows(dst, at, load, size):
        def body(rows):
            dst[rows, lanes_at(at, size)] = load(rows)

        by_rows(chans, body)

    def column(at, row):
        cols[at] = to_column(row)

    def wide(at, rows, size):
        return spread_lanes(cols[at, rows, :], size)

    loads = [copies.local(xin.at[w], xbuf.at[w]) for w in range(windows)]
    for copy in loads:
        copy.start()
    place.greet()
    share = w_other.shape[0] // PLANE
    share_rows = lambda w, c, z, size=1: pl.ds(
        pl.multiple_of((w * 8 + c * 4 + z) * share, share), size * share
    )
    mine_at = share_rows(place.win, core, group)
    share_at = place.win * 8 + core * 4 + group
    taps, conv_shares = weight.shape[0], weight.shape[0] * chans // share
    per_tap = chans // share
    w_at = copies.take()
    w_tap = copies.remote(
        weight_hbm.at[jnp.minimum(share_at // per_tap, taps - 1), pl.ds(pl.multiple_of(share_at % per_tap * share, share), share)],
        w_other.at[mine_at], partner, w_at, w_at,
    )
    w_point = copies.remote(
        point_hbm.at[pl.ds(pl.multiple_of(share_at % per_tap * share, share), share)],
        w_other.at[mine_at], partner, w_at, w_at,
    )
    w_first = w_point
    pl.when(share_at < conv_shares)(w_tap.start)
    pl.when(share_at >= conv_shares)(w_point.start)
    for copy in loads:
        copy.wait()
    x1 = [
        copies.remote(p1a.at[:, i * chunk : (i + 1) * chunk], p2a.at[:, i * chunk : (i + 1) * chunk], partner)
        for i in range(4)
    ]
    for i in range(4):
        put_rows(p1a, i * chunk, lambda rows, i=i: xbuf[order[other], rows, i * chunk : (i + 1) * chunk], chunk)
        if i < 2:
            x1[i].start()
    to_left = copies.remote(xbuf.at[:, :, 0:LANES], halo_r, {"seq": jnp.maximum(place.shard - 1, 0)})
    to_right = copies.remote(xbuf.at[:, :, bins - LANES : bins], halo_l, {"seq": jnp.minimum(place.shard + 1, 7)})
    pl.when(place.shard > 0)(to_left.start)
    pl.when(place.shard < 7)(to_right.start)

    @pl.when(place.shard == 0)
    def _():
        halo_l[...] = jnp.zeros_like(halo_l)

    @pl.when(place.shard == 7)
    def _():
        halo_r[...] = jnp.zeros_like(halo_r)

    for w in range(windows):
        valid_rows[w : w + 1, :] = valid_lanes(place.shard * bins, bins, order.lengths[w])
    at = 0
    for start, size, limit in (
        (place.shard * bins, bins, order.size(side)),
        (place.shard * bins + side * half, half, order.size(2)),
        (core * bins + group * piece + side * eighth, eighth, order.size(3)),
    ):
        valid_ext[:, at : at + size + 2 * LANES] = valid_lanes(start - LANES, size + 2 * LANES, limit)
        at += size + 2 * LANES
    for to, at, size in ((0, LANES, bins), (own2, base2 + LANES, half), (own3, base3 + LANES, eighth)):
        valid_own[:, to : to + size] = valid_ext[:, at : at + size]
    count = jnp.int32(0)
    for length in order.lengths:
        count = count + jnp.clip(length - place.shard * bins, 0, bins)
    count_row = jnp.full((1, chans), count, jnp.int32).astype(F32)
    gain_in, offset_in = as_row(gains_in), as_row(offsets_in)
    acc1[...] = jnp.zeros_like(acc1)
    acc2[...] = jnp.zeros_like(acc2)
    for w in range(windows):

        def body(rows, w=w):
            first, second = acc1[rows, :], acc2[rows, :]
            for at in range(0, bins, TILE):
                x = xbuf[w, rows, at : at + TILE].astype(F32)
                kept = x * valid_rows[w : w + 1, at : at + TILE]
                first = first + lane_sum(kept)
                second = second + lane_sum(kept * x)
            acc1[rows, :] = first
            acc2[rows, :] = second

        by_rows(chans, body)
    plane = [PlaneSum(copies, place, msg.at[i], slots.at[i]) for i in range(3)]
    over_y = [copies.remote(ymsg.at[i], yin.at[i], partner) for i in range(3)]
    plane[0].start([to_row(acc1[...]), to_row(acc2[...]), count_row])

    put_rows(qext, LANES, lambda rows: xbuf[order[3], rows, :], bins)
    for tap in range(3):
        w_all[:, tap * chans : (tap + 1) * chans] = jnp.transpose(weight[tap])
    total = plane[0].finish()
    filled = total[2:3, :]
    ymsg[0] = jnp.concatenate([total[0:3, :], gain_in, offset_in, total[0:3, :]], axis=0)
    over_y[0].start()
    x1[2].start()
    x1[3].start()

    def norm_of(first, second, gain, offset):
        mean = first / filled
        scale = lax.rsqrt(second / filled - mean * mean + EPS)
        return mean, scale, scale * gain, offset - mean * scale * gain

    mean, scale, a_mine, b_mine = norm_of(total[0:1, :], total[1:2, :], gain_in, offset_in)
    column(A_MINE, a_mine)
    column(B_MINE, b_mine)
    rows_out[...] = jnp.zeros_like(rows_out)
    rows_out[0:1, :] = mean
    rows_out[1:2, :] = scale
    rows_out[2:3, :] = filled
    rows_out[6:7, :] = gain_in
    rows_out[7:8, :] = offset_in

    w_first.wait_recv()
    z_first = copies.take(4)
    w_z = []
    for step in range(1, 4):
        z = (group + step) % 4
        device = {"seq": z * 2 + core}
        out = copies.remote(
            w_other.at[mine_at], w_other.at[mine_at], device, z_first + step, z_first + group
        )
        from_at = share_rows(place.win, core, z)
        w_z.append(
            copies.remote(w_other.at[from_at], w_other.at[from_at], device, z_first + step, z_first + z)
        )
        out.start()

    pl.when(place.shard < 7)(to_left.wait_recv)
    pl.when(place.shard > 0)(to_right.wait_recv)
    put_rows(qext, 0, lambda rows: halo_l[order[3], rows, :], LANES)
    put_rows(qext, LANES + bins, lambda rows: halo_r[order[3], rows, :], LANES)
    ex_at, ec_at = copies.take(3), copies.take(3)
    ex_out = [
        copies.remote(
            qext.at[:, k * piece : (k + 1) * piece + 2 * LANES], ex,
            {"seq": jnp.minimum(place.shard + 2 * k, 7)}, ex_at + k - 1, ex_at,
        )
        for k in range(1, 4)
    ]
    ec_out = [
        copies.remote(
            qext.at[:, LANES + k * piece : LANES + (k + 1) * piece], ec,
            {"seq": jnp.minimum(place.shard + 2 * k, 7)}, ec_at + k - 1, ec_at,
        )
        for k in range(1, 4)
    ]

    @pl.when(group == 0)
    def _():
        for copy in ex_out:
            copy.start()
        put_rows(ex, 0, lambda rows: qext[rows, 0 : piece + 2 * LANES], piece + 2 * LANES)

    def activate(a, b, load, dst, at, size):
        mask = valid_ext[:, lanes_at(at, size)]

        def body(rows):
            pre = load(rows).astype(F32) * wide(a, rows, size) + wide(b, rows, size)
            dst[rows, lanes_at(at, size)] = (gelu(pre) * mask).astype(BF16)

        by_rows(chans, body)

    def mixed(right, left):
        return jnp.where(low, right.astype(F32), left.astype(F32)).astype(BF16)

    def first_halo(role):
        w = order[role]
        return lambda rows: mixed(halo_r[w, rows, :], halo_l[w, rows, :])

    def second_halo(role):
        w = order[2]

        def load(rows):
            near = xbuf[w, rows, half : half + LANES].astype(F32)
            far = xbuf[w, rows, half - LANES : half].astype(F32)
            right = jnp.where(role == 0, near, halo_r[w, rows, :].astype(F32))
            left = jnp.where(role == 0, halo_l[w, rows, :].astype(F32), far)
            return jnp.where(low, right, left).astype(BF16)

        return load

    def third_halo(role):
        return lambda rows: mixed(
            ex[rows, lanes_at(LANES + (role + 1) * eighth, LANES)], ex[rows, lanes_at(role * eighth, LANES)]
        )

    def run_segment(a, b, load, dst, at, size):
        def body(i):
            activate(a, b, lambda rows: load(rows, i * TILE), dst, at + i * TILE, TILE)

        times(size // TILE, body)

    put_rows(hb.at[0], 0, first_halo(side), LANES)
    put_rows(hb.at[1], 0, second_halo(side), LANES)
    activate(A_MINE, B_MINE, lambda rows: hb[0, rows, :], act_m, 0, LANES)
    activate(A_MINE, B_MINE, lambda rows: hb[0, rows, :], act_m, LANES + bins, LANES)
    run_segment(
        A_MINE, B_MINE, lambda rows, at: xbuf[order[side], rows, lanes_at(at, TILE)], act_m, LANES, bins
    )
    put_rows(p1b, 0, first_halo(other), LANES)
    put_rows(p1b, LANES, second_halo(other), LANES)
    put_rows(p1b, 2 * LANES, lambda rows: xbuf[order[2], rows, lanes_at(other * half, half)], half)
    cuts2 = (0, 2 * LANES + half // 2, 2 * LANES + half, 3 * LANES + half + eighth)
    x2 = [copies.remote(p1b.at[:, lo:hi], p2b.at[:, lo:hi], partner) for lo, hi in zip(cuts2, cuts2[1:])]
    x2[0].start()
    for copy in w_z:
        copy.wait_recv()
    block = share_rows(place.win, core, 0, 4)
    block_in = share_rows(1 - place.win, core, 0, 4)
    across = {"win": 1 - place.win}
    w_x_at = copies.take()
    w_x = copies.remote(w_other.at[block], w_other.at[block], across, w_x_at, w_x_at)
    w_x_in = copies.remote(w_other.at[block_in], w_other.at[block_in], across, w_x_at, w_x_at)
    w_x.start()
    activate(A_MINE, B_MINE, lambda rows: hb[1, rows, :], act_m, base2, LANES)
    activate(A_MINE, B_MINE, lambda rows: hb[1, rows, :], act_m, base2 + LANES + half, LANES)
    run_segment(
        A_MINE, B_MINE, lambda rows, at: xbuf[order[2], rows, lanes_at(side * half + at, TILE)],
        act_m, base2 + LANES, half,
    )
    pl.when(place.shard > 0)(to_left.wait_send)
    pl.when(place.shard < 7)(to_right.wait_send)
    cot_loads = [copies.local(cin.at[w], xbuf.at[w]) for w in range(windows)]
    for copy in cot_loads:
        copy.start()
    w_x_in.wait_recv()
    sibling = {"seq": group * 2 + 1 - core}
    w_c_at = [copies.take() for _ in range(2)]
    w_c, w_c_in = [], []
    for w in range(2):
        rows = share_rows(w, core, 0, 4)
        rows_in = share_rows(w, 1 - core, 0, 4)
        w_c.append(copies.remote(w_other.at[rows], w_other.at[rows], sibling, w_c_at[w], w_c_at[w]))
        w_c_in.append(
            copies.remote(w_other.at[rows_in], w_other.at[rows_in], sibling, w_c_at[w], w_c_at[w])
        )
        w_c[w].start()

    over_y[0].wait_recv()
    _, _, a_other, b_other = norm_of(*(yin[0, i : i + 1, :] for i in (0, 1, 3, 4)))
    column(A_OTHER, a_other)
    column(B_OTHER, b_other)
    for copy in w_c_in:
        copy.wait_recv()
    for tap in range(3):
        w_all[:, (3 + tap) * chans : (4 + tap) * chans] = jnp.transpose(
            w_other[tap * chans : (tap + 1) * chans, :]
        )
    for i in range(4):
        x1[i].wait_recv()
        run_segment(
            A_OTHER, B_OTHER, lambda rows, at, i=i: p2a[rows, lanes_at(i * chunk + at, TILE)],
            act_o, LANES + i * chunk, chunk,
        )
        if i == 2:
            for copy in x1:
                copy.wait_send()
            x2[1].start()
    pl.when(group > 0)(lambda: ex_out[0].wait_recv())
    put_rows(p1b, cuts2[2], third_halo(other), LANES)
    put_rows(
        p1b, cuts2[2] + LANES, lambda rows: ex[rows, lanes_at(LANES + other * eighth, eighth)], eighth
    )
    x2[2].start()
    put_rows(hb.at[2], 0, third_halo(side), LANES)
    activate(A_MINE, B_MINE, lambda rows: hb[2, rows, :], act_m, base3, LANES)
    activate(A_MINE, B_MINE, lambda rows: hb[2, rows, :], act_m, base3 + LANES + eighth, LANES)
    run_segment(
        A_MINE, B_MINE, lambda rows, at: ex[rows, lanes_at(LANES + side * eighth + at, TILE)],
        act_m, base3 + LANES, eighth,
    )
    for copy in cot_loads:
        copy.wait()
    put_rows(p2a, 0, lambda rows: xbuf[order[other], rows, :], bins)

    def fill_taps(start):
        for at_half, ref in enumerate((act_m, act_o)):
            cells = ref[:, lanes_at(start, TILE + 2 * LANES)]
            for tap in range(3):
                at = LANES + (tap - 1) * DILATION_BINS
                row = (at_half * 3 + tap) * chans
                cat[row : row + chans, :] = cells[:, at : at + TILE]

    def conv_tiles(start, own, count):
        def body(i):
            fill_taps(start + i * TILE)
            out = dot(w_all[...], cat[...])
            conv[:, lanes_at(own + i * TILE, TILE)] = out
            kept = out * valid_own[:, lanes_at(own + i * TILE, TILE)]
            acc1[...] += lane_sum(kept)
            acc2[...] += lane_sum(kept * out)

        times(count, body)

    acc1[...] = jnp.zeros_like(acc1)
    acc2[...] = jnp.zeros_like(acc2)
    x2[0].wait_recv()
    other_halo = lambda at: lambda rows: p2b[rows, at : at + LANES]
    activate(A_OTHER, B_OTHER, other_halo(0), act_o, 0, LANES)
    activate(A_OTHER, B_OTHER, other_halo(0), act_o, LANES + bins, LANES)
    activate(A_OTHER, B_OTHER, other_halo(LANES), act_o, base2, LANES)
    activate(A_OTHER, B_OTHER, other_halo(LANES), act_o, base2 + LANES + half, LANES)
    other_second = lambda rows, at: p2b[rows, lanes_at(2 * LANES + at, TILE)]
    run_segment(A_OTHER, B_OTHER, other_second, act_o, base2 + LANES, half // 2)
    conv_tiles(0, 0, bins // TILE)
    x2[1].wait_recv()
    c1 = [
        copies.remote(p2a.at[:, i * chunk : (i + 1) * chunk], p1a.at[:, i * chunk : (i + 1) * chunk], partner)
        for i in range(4)
    ]
    c1[0].start()
    c1[1].start()
    run_segment(
        A_OTHER, B_OTHER, lambda rows, at: other_second(rows, half // 2 + at),
        act_o, base2 + LANES + half // 2, half // 2,
    )
    conv_tiles(base2, own2, half // TILE)
    x2[2].wait_recv()
    activate(A_OTHER, B_OTHER, other_halo(cuts2[2]), act_o, base3, LANES)
    activate(A_OTHER, B_OTHER, other_halo(cuts2[2]), act_o, base3 + LANES + eighth, LANES)
    run_segment(
        A_OTHER, B_OTHER, lambda rows, at: p2b[rows, lanes_at(cuts2[2] + LANES + at, TILE)],
        act_o, base3 + LANES, eighth,
    )
    conv_tiles(base3, own3, eighth // TILE)
    plane[1].start([to_row(acc1[...]), to_row(acc2[...])])
    for copy in x2:
        copy.wait_send()
    c1[2].start()

    acc1[...] = jnp.zeros_like(acc1)
    for w in range(windows):

        def body(rows, w=w):
            acc1[rows, :] += lane_sum(xbuf[w, rows, :].astype(F32))

        by_rows(chans, body)
    bias_row = to_row(acc1[...])
    total = plane[1].finish()
    ymsg[1] = total
    over_y[1].start()
    c1[3].start()

    @pl.when(group == 0)
    def _():
        for copy in ex_out:
            copy.wait_send()

    put_rows(qext, LANES, lambda rows: xbuf[order[3], rows, :], bins)

    @pl.when(group == 0)
    def _():
        for copy in ec_out:
            copy.start()
        put_rows(ec, 0, lambda rows: qext[rows, LANES : LANES + piece], piece)
    put_rows(p2b, 0, lambda rows: xbuf[order[2], rows, lanes_at(other * half, half)], half)
    cuts = (0, half // 2, half, half + eighth)
    c2 = [copies.remote(p2b.at[:, lo:hi], p1b.at[:, lo:hi], partner) for lo, hi in zip(cuts, cuts[1:])]
    c1[2].wait_recv()
    c2[0].start()

    over_y[1].wait_recv()
    total = ymsg[1] + yin[1]
    gain_mid, offset_mid = as_row(gains_mid), as_row(offsets_mid)
    mean = total[0:1, :] / filled
    scale = lax.rsqrt(total[1:2, :] / filled - mean * mean + EPS)
    for at, row in ((MEAN, mean), (SCALE, scale), (GAIN, gain_mid), (OFFSET, offset_mid), (FACTOR, gain_mid * scale)):
        column(at, row)

    def act_tile(i):
        at = lanes_at(i * TILE, TILE)
        mask = valid_own[:, at]

        def body(rows):
            norm = (conv[rows, at] - wide(MEAN, rows, TILE)) * wide(SCALE, rows, TILE)
            pre = norm * wide(GAIN, rows, TILE) + wide(OFFSET, rows, TILE)
            actm[rows, at] = (gelu(pre) * mask).astype(BF16)

        by_rows(chans, body)

    times(conv.shape[1] // TILE, act_tile)
    back_to = {"seq": core}
    e_at = copies.take(8)
    e_parts = ((actm.at[:, own3:], side), (e_act, other))
    e_home = [
        copies.remote(
            src, acts.at[3, :, lanes_at(group * piece + role * eighth, eighth)], back_to,
            e_at + which, e_at + 2 * group + which,
        )
        for which, (src, role) in enumerate(e_parts)
    ]
    e_mine = [copies.local(src, acts.at[3, :, lanes_at(role * eighth, eighth)]) for src, role in e_parts]
    pl.when(group > 0)(e_home[0].start)
    pl.when(group == 0)(e_mine[0].start)
    keeps = [
        copies.local(actm.at[:, 0:bins], acts.at[side]),
        copies.local(actm.at[:, own2:own3], acts.at[2, :, lanes_at(side * half, half)]),
    ]
    for copy in keeps:
        copy.start()

    acc1[...] = jnp.zeros_like(acc1)
    acc2[...] = jnp.zeros_like(acc2)
    gp[...] = jnp.zeros_like(gp)

    def back_product(mine, theirs):
        cat[0:chans, :] = mine
        cat[chans : 2 * chans, :] = theirs
        tmp[...] = dot(point[...], cat[0:chans, :]) + dot(w_other[3 * chans :, :], cat[chans : 2 * chans, :])

    def grad_rows(rows, at, mask):
        norm = (conv[rows, at] - wide(MEAN, rows, TILE)) * wide(SCALE, rows, TILE)
        pre = norm * wide(GAIN, rows, TILE) + wide(OFFSET, rows, TILE)
        return norm, mask * gelu_slope(pre) * tmp[rows, :]

    def sum_tile(mine, theirs, own):
        back_product(mine, theirs)
        at = lanes_at(own, TILE)
        mask = valid_own[:, at]

        def body(rows):
            norm, part = grad_rows(rows, at, mask)
            acc1[rows, :] += lane_sum(part)
            acc2[rows, :] += lane_sum(part * norm)

        by_rows(chans, body)
        gp[...] += dot_t(actm[:, at], cat[0 : 2 * chans, :])

    def grad_tile(mine, theirs, own):
        back_product(mine, theirs)
        at = lanes_at(own, TILE)
        mask = valid_own[:, at]

        def body(rows):
            norm, part = grad_rows(rows, at, mask)
            kept = mask * (wide(BETA, rows, TILE) + norm * wide(GAMMA, rows, TILE))
            gco[rows, at] = (wide(FACTOR, rows, TILE) * (part - kept)).astype(BF16)

        by_rows(chans, body)

    def over_first(run, lo, hi):
        def body(i):
            at = lanes_at(lo + i * TILE, TILE)
            run(xbuf[order[side], :, at], p1a[:, at], lo + i * TILE)

        times((hi - lo) // TILE, body)

    def over_second(run, lo, hi):
        def body(i):
            at = lo + i * TILE
            run(
                xbuf[order[2], :, lanes_at(side * half + at, TILE)], p1b[:, lanes_at(at, TILE)], own2 + at
            )

        times((hi - lo) // TILE, body)

    def over_third(run):
        run(ec[:, lanes_at(side * eighth, TILE)], p1b[:, half : half + TILE], own3)

    t3_extra = copies.remote(actm.at[:, own3:], e_act, partner)
    t3 = [
        copies.remote(
            actm.at[:, own2 + i * TILE : own2 + (i + 1) * TILE],
            acts.at[2, :, lanes_at(side * half + i * TILE, TILE)],
            partner,
        )
        for i in range(half // TILE)
    ]
    for i in range(4):
        if i != 2:
            c1[i].wait_recv()
        if i == 3:
            c2[1].start()
        over_first(sum_tile, i * chunk, (i + 1) * chunk)
    pl.when(group > 0)(lambda: ec_out[0].wait_recv())
    put_rows(p2b, half, lambda rows: ec[rows, lanes_at(other * eighth, eighth)], eighth)
    c2[2].start()
    c2[0].wait_recv()
    over_second(sum_tile, 0, half // 2)
    c2[1].wait_recv()
    t3_extra.start()
    t3[0].start()
    over_second(sum_tile, half // 2, half)
    c2[2].wait_recv()
    over_third(sum_tile)
    plane[2].start([to_row(acc1[...]), to_row(acc2[...]), bias_row])
    total = plane[2].finish()
    ymsg[2] = total
    over_y[2].start()
    for copy in t3[1:]:
        copy.start()
    t3_extra.wait_recv()
    pl.when(group > 0)(e_home[1].start)
    pl.when(group == 0)(e_mine[1].start)
    over_y[2].wait_recv()
    beta = ymsg[2, 0:1, :] + yin[2, 0:1, :]
    gamma = ymsg[2, 1:2, :] + yin[2, 1:2, :]
    rows_out[3:4, :] = beta
    rows_out[4:5, :] = gamma
    rows_out[5:6, :] = ymsg[2, 2:3, :]
    column(BETA, beta / filled)
    column(GAMMA, gamma / filled)

    over_third(grad_tile)
    t4_extra = copies.remote(gco.at[:, own3:], g_extra, partner)
    t4_extra.start()
    over_second(grad_tile, 0, half // 2)
    t4 = copies.remote(gco.at[:, own2 : own2 + half // 2], g_two, partner)
    t4.start()
    over_second(grad_tile, half // 2, half)
    over_first(grad_tile, 0, bins)
    g_keep = copies.local(gco, g_own)
    g_keep.start()

    weight_sum = conv.at[:, 0 : 6 * chans]
    weight_sum[...] = jnp.zeros_like(weight_sum)

    def weight_tiles(start, own, count):
        def body(i):
            fill_taps(start + i * TILE)
            weight_sum[...] += dot_t(gco[:, lanes_at(own + i * TILE, TILE)], cat[...])

        times(count, body)

    weight_tiles(0, 0, bins // TILE)
    weight_tiles(base2, own2, half // TILE)
    weight_tiles(base3, own3, eighth // TILE)

    gw_keep = copies.local(weight_sum, gw)
    gw_keep.start()

    @pl.when(group > 0)
    def _():
        for copy in e_home:
            copy.wait_send()

    @pl.when(group == 0)
    def _():
        for copy in e_mine:
            copy.wait()
        for copy in ec_out:
            copy.wait_send()
        for z in range(1, 4):
            for which, role in enumerate((side, other)):
                at = acts.at[3, :, lanes_at(z * piece + role * eighth, eighth)]
                copies.remote(at, at, back_to, e_at, e_at + 2 * z + which).wait_recv()

    for copy in keeps + [g_keep, gw_keep]:
        copy.wait()
    for copy in plane:
        copy.drain()
    for copy in [w_first, w_x, *w_c, *w_z, *over_y, *c1, *c2, t3_extra, *t3, t4_extra, t4]:
        copy.wait_send()
    for copy in [*t3, t4_extra, t4]:
        copy.wait_recv()


def second_kernel(
    lengths, xin, acts_in, g_own, g_two, g_extra, gw, gp, weights, rows_in,
    acts, grads, rows_out, conv_grad, point_grad,
    gs, xbuf, halo_r, halo_l, cat, tmp, acc1, acc2, cols, msg, slots,
    parts, parts_core, parts_win, parts_z, parts_side, summed, weight, send, recv,
):
    del acts_in
    place = Place()
    side, group, core, partner = place.side, place.group, place.core, place.partner
    other = 1 - side
    copies = Copies(send, recv)
    windows, chans, bins = xbuf.shape
    half, piece, eighth, chunk = bins // 2, bins // 4, bins // 8, bins // 4
    own2, own3 = bins, bins + half

    own_loads = [
        copies.local(g_own.at[:, 0:bins], gs.at[side, :, LANES : LANES + bins]),
        copies.local(g_own.at[:, own2:own3], gs.at[2, :, lanes_at(LANES + side * half, half)]),
        copies.local(g_two, gs.at[2, :, lanes_at(LANES + other * half, half // 2)]),
    ]
    extra = ((g_own.at[:, own3:], side), (g_extra, other))
    extra_loads = [
        copies.local(src, gs.at[3, :, lanes_at(LANES + role * eighth, eighth)]) for src, role in extra
    ]
    loads = [copies.local(xin.at[w], xbuf.at[w]) for w in range(windows)]
    depth = conv_grad.shape[0] * chans
    part_loads = [copies.local(gw.at[:, i * depth : (i + 1) * depth], parts.at[i, :, :depth]) for i in (0, 1)]
    part_loads += [copies.local(gp.at[:, i * chans : (i + 1) * chans], parts.at[i, :, depth:]) for i in (0, 1)]
    for copy in own_loads + loads + part_loads:
        copy.start()

    @pl.when(group == 0)
    def _():
        for copy in extra_loads:
            copy.start()

    place.greet()
    t4 = copies.remote(
        g_own.at[:, own2 + half // 2 : own3],
        gs.at[2, :, lanes_at(LANES + side * half + half // 2, half // 2)],
        partner,
    )
    t4_first = [
        copies.remote(
            g_own.at[:, i * chunk : (i + 1) * chunk],
            gs.at[side, :, LANES + i * chunk : LANES + (i + 1) * chunk],
            partner,
        )
        for i in range(4)
    ]
    t3_first = []
    for i in range(4):
        at = acts.at[side, :, i * chunk : (i + 1) * chunk]
        t3_first.append(copies.remote(at, at, partner))
    t4.start()
    for copy in t4_first:
        copy.start()
    t3_first[0].start()

    tail = parts_side.shape[0]
    core_rows = lambda c: pl.ds(pl.multiple_of(8 * tail * c, tail), 8 * tail)
    win_rows = lambda w: pl.ds(pl.multiple_of(8 * tail * core + 4 * tail * w, tail), 4 * tail)
    z_rows = lambda z: pl.ds(
        pl.multiple_of(8 * tail * core + 4 * tail * place.win + tail * z, tail), tail
    )
    sibling, across = {"seq": group * 2 + 1 - core}, {"win": 1 - place.win}
    s_core = copies.remote(parts.at[:, core_rows(1 - core), :], parts_core, sibling)
    s_win = copies.remote(parts.at[:, win_rows(1 - place.win), :], parts_win, across)
    s_z_at = copies.take(4)
    s_z, s_z_in = [], []
    g_z_at = copies.take(4)
    g_z, g_z_in = [], []
    for step in range(1, 4):
        z = (group + step) % 4
        device = {"seq": z * 2 + core}
        s_z.append(
            copies.remote(parts.at[:, z_rows(z), :], parts_z.at[group], device, s_z_at + step, s_z_at + group)
        )
        s_z_in.append(
            copies.remote(parts.at[:, z_rows(z), :], parts_z.at[z], device, s_z_at + step, s_z_at + z)
        )
        g_z.append(
            copies.remote(
                summed.at[z_rows(group), :], summed.at[z_rows(group), :], device, g_z_at + step, g_z_at + group
            )
        )
        g_z_in.append(
            copies.remote(summed.at[z_rows(z), :], summed.at[z_rows(z), :], device, g_z_at + step, g_z_at + z)
        )
    s_side = copies.remote(parts.at[1, z_rows(group), :], parts_side, partner)
    g_win_at, g_core_at = copies.take(), copies.take()
    both = lambda at, rows, rows_in, device: tuple(
        copies.remote(summed.at[r, :], summed.at[r, :], device, at, at) for r in (rows, rows_in)
    )
    g_win, g_win_in = both(g_win_at, win_rows(place.win), win_rows(1 - place.win), across)
    g_core, g_core_in = both(g_core_at, core_rows(core), core_rows(1 - core), sibling)
    for copy in part_loads:
        copy.wait()
    s_core.start()

    class Halo:
        def __init__(self, slot, last):
            self.slot, self.last = slot, last
            self.left = copies.remote(
                gs.at[slot, :, LANES : 2 * LANES], halo_r.at[slot], {"seq": jnp.maximum(place.shard - 1, 0)}
            )
            self.right = copies.remote(
                gs.at[slot, :, bins : bins + LANES], halo_l.at[slot], {"seq": jnp.minimum(place.shard + 1, 7)}
            )

        def start(self):
            pl.when((place.shard > 0) & (place.shard <= self.last))(self.left.start)
            pl.when(place.shard < self.last)(self.right.start)

        def finish(self):
            @pl.when(place.shard < self.last)
            def _():
                self.left.wait_recv()
                gs[self.slot, :, LANES + bins :] = halo_r[self.slot]

            @pl.when(place.shard >= self.last)
            def _():
                gs[self.slot, :, LANES + bins :] = jnp.zeros((chans, LANES), BF16)

            @pl.when(place.shard > 0)
            def _():
                self.right.wait_recv()
                gs[self.slot, :, 0:LANES] = halo_l[self.slot]

            @pl.when(place.shard == 0)
            def _():
                gs[self.slot, :, 0:LANES] = jnp.zeros((chans, LANES), BF16)

            pl.when((place.shard > 0) & (place.shard <= self.last))(self.left.wait_send)
            pl.when(place.shard < self.last)(self.right.wait_send)

    halos = {name: Halo(slot, last) for name, slot, last in (("own", side, 7), ("third", 2, 7), ("other", other, 7), ("quarter", 3, 1))}
    own_loads[0].wait()
    halos["own"].start()
    e_at = copies.take(8)
    back_to = {"seq": core}
    e_home = [
        copies.remote(
            src, gs.at[3, :, lanes_at(LANES + group * piece + role * eighth, eighth)], back_to,
            e_at + which, e_at + 2 * group + which,
        )
        for which, (src, role) in enumerate(extra)
    ]

    @pl.when(group > 0)
    def _():
        for copy in e_home:
            copy.start()

    order = Order(lengths)
    for tap in range(weights.shape[0]):
        weight[:, tap * chans : (tap + 1) * chans] = weights[tap]
    names = {"mean": 0, "scale": 1, "gain": 2, "offset": 3}
    for at, row in enumerate((0, 1, 6, 7)):
        cols[at] = to_column(rows_in[row : row + 1, :])
    wide = lambda name, rows: spread_lanes(cols[names[name], rows, :], TILE)
    acc1[...] = jnp.zeros_like(acc1)
    acc2[...] = jnp.zeros_like(acc2)

    def through(slot):
        def tile(i):
            cells = gs[slot, :, lanes_at(i * TILE, TILE + 2 * LANES)]
            for tap in range(3):
                at = LANES - (tap - 1) * DILATION_BINS
                cat[tap * chans : (tap + 1) * chans, :] = cells[:, at : at + TILE]
            tmp[...] = dot(weight[...], cat[...])
            at = lanes_at(i * TILE, TILE)
            mask = valid_lanes(place.shard * bins + i * TILE, TILE, order.size(slot))
            window = order[slot]

            def body(rows):
                norm = (xbuf[window, rows, at].astype(F32) - wide("mean", rows)) * wide("scale", rows)
                part = mask * gelu_slope(norm * wide("gain", rows) + wide("offset", rows)) * tmp[rows, :]
                acc1[rows, :] += lane_sum(part)
                acc2[rows, :] += lane_sum(part * norm)
                gs[slot, rows, at] = part.astype(BF16)

            by_rows(chans, body)

        times(bins // TILE, tile)

    keeps = []

    def keep(slot):
        copy = copies.local(gs.at[slot, :, 0:bins], grads.at[slot])
        copy.start()
        keeps.append(copy)

    for copy in loads:
        copy.wait()
    halos["own"].finish()
    through(side)
    keep(side)
    s_core.wait_recv()
    parts[:, core_rows(core), :] += parts_core[...]
    s_win.start()
    own_loads[1].wait()
    own_loads[2].wait()
    t4.wait_recv()
    halos["third"].start()
    quarter_keep = copies.local(gs.at[3, :, 0:bins], grads.at[3])

    @pl.when(group == 0)
    def _():
        for copy in extra_loads:
            copy.wait()
        for z in range(1, 4):
            for which, role in enumerate((side, other)):
                at = gs.at[3, :, lanes_at(LANES + z * piece + role * eighth, eighth)]
                copies.remote(at, at, back_to, e_at, e_at + 2 * z + which).wait_recv()
        halos["quarter"].start()

    halos["third"].finish()
    through(2)
    keep(2)
    s_win.wait_recv()
    parts[:, win_rows(place.win), :] += parts_win[...]
    for copy in s_z:
        copy.start()

    @pl.when(group == 0)
    def _():
        halos["quarter"].finish()
        through(3)
        quarter_keep.start()

    for copy in s_z_in:
        copy.wait_recv()
    parts_z[group] = parts[:, z_rows(group), :]
    total = parts_z[0]
    for z in range(1, 4):
        total = total + parts_z[z]
    parts[:, z_rows(group), :] = total
    s_side.start()
    for copy in t3_first[1:]:
        copy.start()
    for copy in t4_first:
        copy.wait_recv()
    halos["other"].start()
    halos["other"].finish()
    s_side.wait_recv()
    summed[z_rows(group), :] = parts[0, z_rows(group), :] + parts_side[...]
    for copy in g_z:
        copy.start()
    through(other)
    keep(other)
    plane = PlaneSum(copies, place, msg, slots)
    plane.start([to_row(acc1[...]), to_row(acc2[...])])
    for copy in g_z_in:
        copy.wait_recv()
    g_win.start()
    rows_out[...] = plane.finish()
    g_win_in.wait_recv()
    g_core.start()
    plane.drain()
    g_core_in.wait_recv()
    for tap in range(conv_grad.shape[0]):
        conv_grad[tap] = jnp.transpose(summed[:, tap * chans : (tap + 1) * chans])
    point_grad[...] = summed[:, depth:]
    for copy in [s_core, s_win, s_side, *s_z, *g_z, g_win, g_core]:
        copy.wait_send()
    for copy in keeps:
        copy.wait()

    @pl.when(group == 0)
    def _():
        quarter_keep.wait()

    @pl.when(group > 0)
    def _():
        for copy in e_home:
            copy.wait_send()

    for copy in [t4, *t4_first, *t3_first]:
        copy.wait_send()
    for copy in t3_first:
        copy.wait_recv()


def last_kernel(
    lengths, x, c, act, grad, point, bias, rows_one, rows_two, conv_in, point_in,
    out, grad_out, gain_in, offset_in, gain_mid, offset_mid, grad_bias, conv_out, point_out,
    weight, cols, tmp,
):
    window, tile = pl.program_id(0), pl.program_id(1)
    side, shard = lax.axis_index("ch"), lax.axis_index("seq")
    conv_out[...] = conv_in[...]
    point_out[...] = point_in[...]

    @pl.when((window == 0) & (tile == 0))
    def _():
        weight[...] = jnp.transpose(point[...])
        mean, scale, filled, gain = (rows_one[i : i + 1, :] for i in (0, 1, 2, 6))
        beta, gamma = rows_two[0:1, :], rows_two[1:2, :]
        factor = gain * scale
        slope = factor * scale * gamma / filled
        for at, row in enumerate(
            (factor, slope, factor * beta / filled - mean * slope, bias[...].reshape(beta.shape))
        ):
            cols[at] = to_column(row)
        size = gain_in.shape[0]
        gain_in[...] = gamma.reshape(size)
        offset_in[...] = beta.reshape(size)
        grad_bias[...] = rows_one[5:6, :].reshape(size)
        part = size // 2
        for ref, row in ((gain_mid, rows_one[4:5, :]), (offset_mid, rows_one[3:4, :])):
            ref[...] = jnp.where(side == 0, row[:, :part], row[:, part:])

    size = x.shape[2]
    bins = pl.num_programs(1) * size
    mask = valid_lanes(shard * bins + tile * size, size, lengths[window]) > 0.0
    tmp[...] = dot(weight[...], act[0])
    def body(rows):
        factor, slope, shift, more = (spread_lanes(cols[i, rows, :], TILE) for i in range(4))
        for at in range(0, size, TILE):
            lanes = slice(at, at + TILE)
            kept = mask[:, lanes]
            xs = x[0, rows, lanes].astype(F32)
            out[0, rows, lanes] = (xs + jnp.where(kept, tmp[rows, lanes], 0.0) + more).astype(BF16)
            back = factor * grad[0, rows, lanes].astype(F32) - xs * slope - shift
            grad_out[0, rows, lanes] = (
                c[0, rows, lanes].astype(F32) + jnp.where(kept, back, 0.0)
            ).astype(BF16)

    by_rows(x.shape[1], body)


def local_pair(
    inputs,
    lengths,
    gain_in,
    offset_in,
    conv_weight,
    gain_mid,
    offset_mid,
    point_weight,
    point_bias,
    cotangent,
):
    windows, chans, bins = inputs.shape
    taps, _, bottle = conv_weight.shape
    piece, half, eighth = bins // 4, bins // 2, bins // 8
    widened, packed = bins + half + eighth + 6 * LANES, bins + half + eighth

    vmem = pl.BlockSpec(memory_space=pltpu.VMEM)
    hbm = pl.BlockSpec(memory_space=pltpu.HBM)
    smem = pl.BlockSpec(memory_space=pltpu.SMEM)
    shape = jax.ShapeDtypeStruct
    acts, g_own, g_two, g_extra, gw, gp, rows_one = pl.pallas_call(
        first_kernel,
        in_specs=[smem, hbm, hbm, hbm, hbm, vmem, vmem, vmem, vmem, vmem, vmem],
        out_specs=[hbm, hbm, hbm, hbm, hbm, vmem, vmem],
        out_shape=[
            shape((windows, bottle, bins), BF16),
            shape((bottle, packed), BF16),
            shape((bottle, half // 2), BF16),
            shape((bottle, eighth), BF16),
            shape((bottle, 2 * taps * chans), F32),
            shape((bottle, 2 * chans), F32),
            shape((8, chans), F32),
        ],
        scratch_shapes=[
            pltpu.VMEM((windows, chans, bins), BF16),
            pltpu.VMEM((chans, bins), BF16),
            pltpu.VMEM((chans, bins), BF16),
            pltpu.VMEM((chans, half + eighth + 3 * LANES), BF16),
            pltpu.VMEM((chans, half + eighth + 3 * LANES), BF16),
            pltpu.VMEM((chans, bins + 2 * LANES), BF16),
            pltpu.VMEM((chans, piece + 2 * LANES), BF16),
            pltpu.VMEM((chans, piece), BF16),
            pltpu.VMEM((windows, chans, LANES), BF16),
            pltpu.VMEM((windows, chans, LANES), BF16),
            pltpu.VMEM((3, chans, LANES), BF16),
            pltpu.VMEM((chans, widened), BF16),
            pltpu.VMEM((chans, widened), BF16),
            pltpu.VMEM((bottle, packed), F32),
            pltpu.VMEM((bottle, packed), BF16),
            pltpu.VMEM((bottle, packed), BF16),
            pltpu.VMEM((bottle, 2 * taps * chans), BF16),
            pltpu.VMEM(((taps + 1) * chans, bottle), BF16),
            pltpu.VMEM((bottle, eighth), BF16),
            pltpu.VMEM((2 * taps * chans, TILE), BF16),
            pltpu.VMEM((bottle, TILE), F32),
            pltpu.VMEM((chans, LANES), F32),
            pltpu.VMEM((chans, LANES), F32),
            pltpu.VMEM((11, chans, LANES), F32),
            pltpu.VMEM((3, 8, chans), F32),
            pltpu.VMEM((3, PLANE, 8, chans), F32),
            pltpu.VMEM((3, 8, chans), F32),
            pltpu.VMEM((3, 8, chans), F32),
            pltpu.VMEM((windows, bins), F32),
            pltpu.VMEM((1, widened), F32),
            pltpu.VMEM((1, packed), F32),
            pltpu.SemaphoreType.DMA((128,)),
            pltpu.SemaphoreType.DMA((128,)),
        ],
        compiler_params=pltpu.CompilerParams(
            collective_id=0, has_side_effects=True, vmem_limit_bytes=VMEM_BYTES
        ),
        cost_estimate=pl.CostEstimate(flops=60 * 10**9, bytes_accessed=10**8, transcendentals=0),
    )(
        lengths, inputs, cotangent, conv_weight, point_weight, conv_weight, point_weight,
        gain_in, offset_in, gain_mid, offset_mid,
    )

    share = bottle // PLANE
    acts, grads, rows_two, conv_grad, point_grad = pl.pallas_call(
        second_kernel,
        in_specs=[smem, hbm, hbm, hbm, hbm, hbm, hbm, hbm, vmem, vmem],
        out_specs=[hbm, hbm, vmem, vmem, vmem],
        out_shape=[
            shape((windows, bottle, bins), BF16),
            shape((windows, chans, bins), BF16),
            shape((8, chans), F32),
            shape((taps, chans, bottle), F32),
            shape((bottle, chans), F32),
        ],
        input_output_aliases={2: 0},
        scratch_shapes=[
            pltpu.VMEM((windows, bottle, bins + 2 * LANES), BF16),
            pltpu.VMEM((windows, chans, bins), BF16),
            pltpu.VMEM((windows, bottle, LANES), BF16),
            pltpu.VMEM((windows, bottle, LANES), BF16),
            pltpu.VMEM((taps * bottle, TILE), BF16),
            pltpu.VMEM((chans, TILE), F32),
            pltpu.VMEM((chans, LANES), F32),
            pltpu.VMEM((chans, LANES), F32),
            pltpu.VMEM((4, chans, LANES), F32),
            pltpu.VMEM((8, chans), F32),
            pltpu.VMEM((PLANE, 8, chans), F32),
            pltpu.VMEM((2, bottle, (taps + 1) * chans), F32),
            pltpu.VMEM((2, bottle // 2, (taps + 1) * chans), F32),
            pltpu.VMEM((2, bottle // 4, (taps + 1) * chans), F32),
            pltpu.VMEM((4, 2, share, (taps + 1) * chans), F32),
            pltpu.VMEM((share, (taps + 1) * chans), F32),
            pltpu.VMEM((bottle, (taps + 1) * chans), F32),
            pltpu.VMEM((chans, taps * bottle), BF16),
            pltpu.SemaphoreType.DMA((128,)),
            pltpu.SemaphoreType.DMA((128,)),
        ],
        compiler_params=pltpu.CompilerParams(
            collective_id=1, has_side_effects=True, vmem_limit_bytes=VMEM_BYTES
        ),
        cost_estimate=pl.CostEstimate(flops=60 * 10**9, bytes_accessed=10**8, transcendentals=0),
    )(lengths, inputs, acts, g_own, g_two, g_extra, gw, gp, conv_weight, rows_one)

    def slot_of(window, sizes):
        rank = jnp.int32(0)
        for other in range(windows):
            longer = sizes[other] > sizes[window]
            ahead = (sizes[other] == sizes[window]) & (other < window)
            rank = rank + jnp.where(longer | ahead, 1, 0)
        return rank

    tile = bins
    at = pl.BlockSpec((1, chans, tile), lambda w, i, p: (w, 0, i))
    at_slot = pl.BlockSpec((1, chans, tile), lambda w, i, p: (slot_of(w, p), 0, i))
    whole = lambda rows, size: pl.BlockSpec((rows, size), lambda w, i, p: (0, 0))
    steps = bins // tile
    part = chans // (windows * steps)
    conv_at = pl.BlockSpec((taps, part, bottle), lambda w, i, p: (0, w * steps + i, 0))
    point_at = pl.BlockSpec((part, chans), lambda w, i, p: (w * steps + i, 0))
    line = lambda size: pl.BlockSpec((size,), lambda w, i, p: (0,))
    outputs, grad_inputs, gamma_in, beta_in, gamma_mid, beta_mid, grad_bias, conv_grad, point_grad = pl.pallas_call(
        last_kernel,
        grid_spec=pltpu.PrefetchScalarGridSpec(
            num_scalar_prefetch=1,
            grid=(windows, bins // tile),
            in_specs=[
                at, at, at_slot, at_slot,
                whole(bottle, chans), line(chans), whole(8, chans), whole(8, chans), conv_at, point_at,
            ],
            out_specs=[
                at, at, line(chans), line(chans), whole(1, bottle // 2), whole(1, bottle // 2),
                line(chans), conv_at, point_at,
            ],
            scratch_shapes=[
                pltpu.VMEM((chans, bottle), BF16),
                pltpu.VMEM((4, chans, LANES), F32),
                pltpu.VMEM((chans, tile), F32),
            ],
        ),
        out_shape=[
            shape(inputs.shape, BF16),
            shape(inputs.shape, BF16),
            shape((chans,), F32),
            shape((chans,), F32),
            shape((1, bottle // 2), F32),
            shape((1, bottle // 2), F32),
            shape((chans,), F32),
            shape((taps, chans, bottle), F32),
            shape((bottle, chans), F32),
        ],
        compiler_params=pltpu.CompilerParams(vmem_limit_bytes=VMEM_BYTES),
        cost_estimate=pl.CostEstimate(flops=4 * 10**9, bytes_accessed=6 * 10**7, transcendentals=0),
    )(
        lengths, inputs, cotangent, acts, grads, point_weight, point_bias, rows_one, rows_two,
        conv_grad, point_grad,
    )
    return (
        outputs,
        grad_inputs,
        gamma_in,
        beta_in,
        conv_grad,
        gamma_mid[0],
        beta_mid[0],
        point_grad,
        grad_bias,
    )


def solution(mesh):
    paired = mesh.shape["ch"] == 2 and mesh.shape["seq"] == 8 and mesh.shape["win"] == 2

    def local(*args):
        windows, chans, bins = args[0].shape
        if paired and windows == 4 and chans == args[4].shape[2] and bins == 8 * TILE:
            return local_pair(*args)
        return local_any(*args)

    return jax.shard_map(
        local,
        mesh=mesh,
        in_specs=(
            P("win", "ch", "seq"),
            P("win"),
            P("ch"),
            P("ch"),
            P(None, "ch", None),
            P(),
            P(),
            P(None, "ch"),
            P("ch"),
            P("win", "ch", "seq"),
        ),
        out_specs=(
            P("win", "ch", "seq"),
            P("win", "ch", "seq"),
            P("ch"),
            P("ch"),
            P(None, "ch", None),
            P("ch"),
            P("ch"),
            P(None, "ch"),
            P("ch"),
        ),
        check_vma=False,
    )
```

```python
import jax
import jax.numpy as jnp
from jax import lax
from jax.experimental import pallas as pl
from jax.experimental.pallas import tpu as pltpu
from jax.sharding import PartitionSpec as P

DILATION_BINS = 57


EPS = 1e-05
LANES = 128
TILE = 384
VMEM_BYTES = 63 * 1000 * 1000


def with_halo(cells, sides, width):
    for axis, dim in sides:
        count = lax.axis_size(axis)
        ends = count - 1
        head = lax.slice_in_dim(cells, 0, width, axis=dim)
        tail = lax.slice_in_dim(cells, cells.shape[dim] - width, cells.shape[dim], axis=dim)
        cells = jnp.concatenate(
            [
                lax.ppermute(tail, axis, [(i, (i + 1) % count) for i in range(ends)]),
                cells,
                lax.ppermute(head, axis, [((i + 1) % count, i) for i in range(ends)]),
            ],
            axis=dim,
        )
    return cells


def norm_sums(first_term, second_term):
    return lax.psum((first_term, second_term), ("seq", "win"))


def column(vector):
    return vector[:, None]


def local_any(
    inputs,
    lengths,
    gain_in,
    offset_in,
    conv_weight,
    gain_mid,
    offset_mid,
    point_weight,
    point_bias,
    cotangent,
):
    win_count, chan_local, count_of_bins = inputs.shape
    count_of_taps = conv_weight.shape[0]
    bottle = conv_weight.shape[2]
    bottle_local = bottle // lax.axis_size("ch")
    offset_at = lax.axis_index("ch") * bottle_local
    places = lax.axis_index("seq") * count_of_bins + jnp.arange(count_of_bins, dtype=jnp.int32)
    valid_rows = (places[None, :] < lengths[:, None]).astype(jnp.float32)[:, None, :]
    x_wide = inputs.astype(jnp.float32)
    sum_first = jnp.sum(valid_rows * x_wide, axis=(0, 2))
    sum_second = jnp.sum(valid_rows * x_wide * x_wide, axis=(0, 2))
    sum_first, sum_second, filled = lax.psum(
        (sum_first, sum_second, jnp.sum(valid_rows)), ("seq", "win")
    )
    mean_in = sum_first / filled
    scale_in = lax.rsqrt(sum_second / filled - mean_in * mean_in + EPS)
    norm_in = (x_wide - column(mean_in)) * column(scale_in)
    pre_in = norm_in * column(gain_in) + column(offset_in)
    input_activation, gelu_in_back = jax.vjp(jax.nn.gelu, pre_in)
    lowered_activation = (input_activation * valid_rows).astype(jnp.bfloat16)
    padded_input = with_halo(lowered_activation, (("seq", 2),), DILATION_BINS)
    stacked_taps = jnp.concatenate(
        [
            padded_input[
                :,
                :,
                kernel_tap_index * DILATION_BINS : kernel_tap_index * DILATION_BINS + count_of_bins,
            ]
            for kernel_tap_index in range(count_of_taps)
        ],
        axis=1,
    )
    flat_weight = conv_weight.reshape(count_of_taps * chan_local, bottle)
    partial_value = jnp.einsum(
        "wkt,kf->wft", stacked_taps, flat_weight, preferred_element_type=jnp.float32
    )
    conv_out = lax.psum_scatter(partial_value, "ch", scatter_dimension=1, tiled=True)
    gain_part = lax.dynamic_slice_in_dim(gain_mid, offset_at, bottle_local)
    offset_part = lax.dynamic_slice_in_dim(offset_mid, offset_at, bottle_local)
    mid_first, mid_second = norm_sums(
        jnp.sum(valid_rows * conv_out, axis=(0, 2)),
        jnp.sum(valid_rows * conv_out * conv_out, axis=(0, 2)),
    )
    mean_mid = mid_first / filled
    scale_mid = lax.rsqrt(mid_second / filled - mean_mid * mean_mid + EPS)
    norm_mid = (conv_out - column(mean_mid)) * column(scale_mid)
    pre_mid = norm_mid * column(gain_part) + column(offset_part)
    act_mid, gelu_mid_back = jax.vjp(jax.nn.gelu, pre_mid)
    act_mid_low = (act_mid * valid_rows).astype(jnp.bfloat16)
    mixed_in = lax.all_gather(act_mid_low, "ch", axis=1, tiled=True)
    branch = jnp.einsum("wft,fc->wct", mixed_in, point_weight, preferred_element_type=jnp.float32)
    outputs = (x_wide + branch + column(point_bias)).astype(jnp.bfloat16)
    grad_point = jnp.einsum("wft,wct->fc", mixed_in, cotangent, preferred_element_type=jnp.float32)
    grad_bias = jnp.sum(cotangent.astype(jnp.float32), axis=(0, 2))
    partial_back = jnp.einsum(
        "wct,fc->wft", cotangent, point_weight, preferred_element_type=jnp.float32
    )
    grad_act_mid = lax.psum_scatter(partial_back, "ch", scatter_dimension=1, tiled=True)
    grad_pre_mid = gelu_mid_back(grad_act_mid * valid_rows)[0]
    local_beta = jnp.sum(grad_pre_mid, axis=(0, 2))
    local_gamma = jnp.sum(grad_pre_mid * norm_mid, axis=(0, 2))
    grad_point, grad_bias, beta_mid, gamma_mid = lax.psum(
        (grad_point, grad_bias, local_beta, local_gamma), ("seq", "win")
    )
    grad_conv_out = column(gain_part * scale_mid) * (
        grad_pre_mid - valid_rows * (column(beta_mid) + norm_mid * column(gamma_mid)) / filled
    )
    grad_low = grad_conv_out.astype(jnp.bfloat16)
    complete_gradient = lax.all_gather(grad_low, "ch", axis=1, tiled=True)
    grad_conv = jnp.einsum(
        "wkt,wft->kf", stacked_taps, complete_gradient, preferred_element_type=jnp.float32
    )
    grad_conv = grad_conv.reshape(count_of_taps, chan_local, bottle)
    padded_gradient = with_halo(complete_gradient, (("seq", 2),), DILATION_BINS)
    back_taps = jnp.concatenate(
        [
            padded_gradient[
                :,
                :,
                (count_of_taps - 1 - kernel_tap_index)
                * DILATION_BINS : (count_of_taps - 1 - kernel_tap_index)
                * DILATION_BINS
                + count_of_bins,
            ]
            for kernel_tap_index in range(count_of_taps)
        ],
        axis=1,
    )
    back_weight = jnp.transpose(conv_weight, (0, 2, 1)).reshape(count_of_taps * bottle, chan_local)
    grad_act_in = jnp.einsum(
        "wkt,kc->wct", back_taps, back_weight, preferred_element_type=jnp.float32
    )
    grad_pre_in = gelu_in_back(grad_act_in * valid_rows)[0]
    local_beta_in = jnp.sum(grad_pre_in, axis=(0, 2))
    local_gamma_in = jnp.sum(grad_pre_in * norm_in, axis=(0, 2))
    grad_conv, beta_in, gamma_in = lax.psum(
        (grad_conv, local_beta_in, local_gamma_in), ("seq", "win")
    )
    grad_inputs = (
        cotangent.astype(jnp.float32)
        + column(gain_in * scale_in)
        * (grad_pre_in - valid_rows * (column(beta_in) + norm_in * column(gamma_in)) / filled)
    ).astype(jnp.bfloat16)
    return (
        outputs,
        grad_inputs,
        gamma_in,
        beta_in,
        grad_conv,
        gamma_mid,
        beta_mid,
        grad_point,
        grad_bias,
    )


MESH = pl.DeviceIdType.MESH
ROWS = 32
PLANE = 16
F32 = jnp.float32
BF16 = jnp.bfloat16
GELU_A = 0.7978845608028654
GELU_B = 0.044715


def dot(a, b):
    return jnp.dot(a, b, preferred_element_type=F32)


def dot_t(a, b):
    return lax.dot_general(a, b, (((1,), (1,)), ((), ())), preferred_element_type=F32)


def lane_sum(cells):
    total = cells[:, :LANES]
    for at in range(LANES, cells.shape[1], LANES):
        total = total + cells[:, at : at + LANES]
    return total


def gelu(v):
    return 0.5 * v * (1.0 + jnp.tanh(GELU_A * (v + GELU_B * (v * v * v))))


def gelu_slope(v):
    square = v * v
    th = jnp.tanh(GELU_A * (v + GELU_B * (v * square)))
    return 0.5 * (1.0 + th) + 0.5 * v * (1.0 - th * th) * (GELU_A * (1.0 + 3.0 * GELU_B * square))


def lanes_at(at, size):
    return pl.ds(pl.multiple_of(at, LANES), size)


def by_rows(count, body):
    def step(i, carry):
        body(pl.ds(pl.multiple_of(i * ROWS, ROWS), ROWS))
        return carry

    lax.fori_loop(0, count // ROWS, step, 0, unroll=3)


def times(count, body):
    def step(i, carry):
        body(i)
        return carry

    lax.fori_loop(0, count, step, 0)


def spread_lanes(cells, size):
    return jnp.concatenate([cells] * (size // LANES), axis=1)


def to_column(row):
    return jnp.transpose(jnp.broadcast_to(row, (LANES, row.shape[1])))


def to_row(cells):
    return jnp.sum(jnp.transpose(cells), axis=0, keepdims=True)


class Copies:
    def __init__(self, send, recv):
        self.send, self.recv, self.used = send, recv, 0

    def take(self, count=1):
        self.used += count
        return self.used - count

    def remote(self, src, dst, device, send_at=None, recv_at=None):
        if send_at is None:
            send_at = self.take()
        if recv_at is None:
            recv_at = send_at
        return pltpu.make_async_remote_copy(
            src_ref=src,
            dst_ref=dst,
            send_sem=self.send.at[send_at],
            recv_sem=self.recv.at[recv_at],
            device_id=device,
            device_id_type=MESH,
        )

    def local(self, src, dst):
        return pltpu.make_async_copy(src, dst, self.send.at[self.take()])


class Place:
    def __init__(self):
        self.side, self.shard, self.win = (lax.axis_index(n) for n in ("ch", "seq", "win"))
        self.group, self.core = self.shard // 2, self.shard % 2
        self.me = self.win * 8 + self.shard
        self.partner = {"ch": 1 - self.side}

    def peer(self, step):
        at = (self.me + step) % PLANE
        return at, {"seq": at % 8, "win": at // 8}

    def greet(self):
        barrier = pltpu.get_barrier_semaphore()
        pl.semaphore_signal(barrier, 1, device_id=self.partner, device_id_type=MESH)
        for step in range(1, PLANE):
            pl.semaphore_signal(barrier, 1, device_id=self.peer(step)[1], device_id_type=MESH)
        pl.semaphore_wait(barrier, PLANE)


class PlaneSum:
    def __init__(self, copies, place, mine, slots):
        self.place, self.mine, self.slots = place, mine, slots
        first = copies.take(PLANE)
        self.out, self.into = [], []
        for step in range(1, PLANE):
            at, device = place.peer(step)
            self.out.append(
                copies.remote(mine, slots.at[place.me], device, first + step, first + place.me)
            )
            self.into.append(copies.remote(mine, slots.at[at], device, first + step, first + at))

    def start(self, rows):
        for at, row in enumerate(rows):
            self.mine[at : at + 1, :] = row
        for copy in self.out:
            copy.start()
        self.slots[self.place.me] = self.mine[...]

    def finish(self):
        for copy in self.into:
            copy.wait_recv()
        total = self.slots[0]
        for at in range(1, PLANE):
            total = total + self.slots[at]
        return total

    def drain(self):
        for copy in self.out:
            copy.wait_send()


A_MINE, B_MINE, A_OTHER, B_OTHER, MEAN, SCALE, GAIN, OFFSET, FACTOR, BETA, GAMMA = range(11)


class Order:
    def __init__(self, lengths):
        self.lengths = [lengths[i] for i in range(4)]
        ranks = []
        for i, mine in enumerate(self.lengths):
            rank = jnp.int32(0)
            for j, their in enumerate(self.lengths):
                if j < i:
                    rank = rank + jnp.where(their >= mine, 1, 0)
                elif j > i:
                    rank = rank + jnp.where(their > mine, 1, 0)
            ranks.append(rank)

        def at_slot(slot, values):
            found = jnp.int32(0)
            for rank, value in zip(ranks, values, strict=True):
                found = found + jnp.where(rank == slot, value, 0)
            return found

        self.windows = [at_slot(slot, range(4)) for slot in range(4)]
        self.sizes = [at_slot(slot, self.lengths) for slot in range(4)]

    def of(self, values, slot):
        if isinstance(slot, int):
            return values[slot]
        found = values[0]
        for at in range(1, 4):
            found = jnp.where(slot == at, values[at], found)
        return found

    def __getitem__(self, slot):
        return self.of(self.windows, slot)

    def size(self, slot):
        return self.of(self.sizes, slot)


def valid_lanes(start, size, limit):
    spots = start + lax.broadcasted_iota(jnp.int32, (1, size), 1)
    return ((spots >= 0) & (spots < limit)).astype(F32)


def as_row(ref):
    return ref[...].reshape(1, ref.shape[0])


def first_kernel(
    lengths, xin, cin, weight_hbm, point_hbm, weight, point, gains_in, offsets_in, gains_mid, offsets_mid,
    acts, g_own, g_two, g_extra, gw, gp, rows_out,
    xbuf, p1a, p2a, p1b, p2b, qext, ex, ec, halo_r, halo_l, hb,
    act_m, act_o, conv, actm, gco, w_all, w_other, e_act, cat, tmp, acc1, acc2, cols,
    msg, slots, ymsg, yin, valid_rows, valid_ext, valid_own, send, recv,
):
    place = Place()
    side, group, core, partner = place.side, place.group, place.core, place.partner
    other = 1 - side
    copies = Copies(send, recv)
    windows, chans, bins = xbuf.shape
    half, piece, eighth, chunk = bins // 2, bins // 4, bins // 8, bins // 4
    base2, base3 = bins + 2 * LANES, bins + half + 4 * LANES
    own2, own3 = bins, bins + half
    low = lax.broadcasted_iota(jnp.int32, (ROWS, LANES), 1) < LANES // 2
    order = Order(lengths)

    def put_rows(dst, at, load, size):
        def body(rows):
            dst[rows, lanes_at(at, size)] = load(rows)

        by_rows(chans, body)

    def column(at, row):
        cols[at] = to_column(row)

    def wide(at, rows, size):
        return spread_lanes(cols[at, rows, :], size)

    loads = [copies.local(xin.at[w], xbuf.at[w]) for w in range(windows)]
    for copy in loads:
        copy.start()
    place.greet()
    share = w_other.shape[0] // PLANE
    share_rows = lambda w, c, z, size=1: pl.ds(
        pl.multiple_of((w * 8 + c * 4 + z) * share, share), size * share
    )
    mine_at = share_rows(place.win, core, group)
    share_at = place.win * 8 + core * 4 + group
    taps, conv_shares = weight.shape[0], weight.shape[0] * chans // share
    per_tap = chans // share
    w_at = copies.take()
    w_tap = copies.remote(
        weight_hbm.at[jnp.minimum(share_at // per_tap, taps - 1), pl.ds(pl.multiple_of(share_at % per_tap * share, share), share)],
        w_other.at[mine_at], partner, w_at, w_at,
    )
    w_point = copies.remote(
        point_hbm.at[pl.ds(pl.multiple_of(share_at % per_tap * share, share), share)],
        w_other.at[mine_at], partner, w_at, w_at,
    )
    w_first = w_point
    pl.when(share_at < conv_shares)(w_tap.start)
    pl.when(share_at >= conv_shares)(w_point.start)
    for copy in loads:
        copy.wait()
    x1 = [
        copies.remote(p1a.at[:, i * chunk : (i + 1) * chunk], p2a.at[:, i * chunk : (i + 1) * chunk], partner)
        for i in range(4)
    ]
    for i in range(4):
        put_rows(p1a, i * chunk, lambda rows, i=i: xbuf[order[other], rows, i * chunk : (i + 1) * chunk], chunk)
        if i < 2:
            x1[i].start()
    to_left = copies.remote(xbuf.at[:, :, 0:LANES], halo_r, {"seq": jnp.maximum(place.shard - 1, 0)})
    to_right = copies.remote(xbuf.at[:, :, bins - LANES : bins], halo_l, {"seq": jnp.minimum(place.shard + 1, 7)})
    pl.when(place.shard > 0)(to_left.start)
    pl.when(place.shard < 7)(to_right.start)

    @pl.when(place.shard == 0)
    def _():
        halo_l[...] = jnp.zeros_like(halo_l)

    @pl.when(place.shard == 7)
    def _():
        halo_r[...] = jnp.zeros_like(halo_r)

    for w in range(windows):
        valid_rows[w : w + 1, :] = valid_lanes(place.shard * bins, bins, order.lengths[w])
    at = 0
    for start, size, limit in (
        (place.shard * bins, bins, order.size(side)),
        (place.shard * bins + side * half, half, order.size(2)),
        (core * bins + group * piece + side * eighth, eighth, order.size(3)),
    ):
        valid_ext[:, at : at + size + 2 * LANES] = valid_lanes(start - LANES, size + 2 * LANES, limit)
        at += size + 2 * LANES
    for to, at, size in ((0, LANES, bins), (own2, base2 + LANES, half), (own3, base3 + LANES, eighth)):
        valid_own[:, to : to + size] = valid_ext[:, at : at + size]
    count = jnp.int32(0)
    for length in order.lengths:
        count = count + jnp.clip(length - place.shard * bins, 0, bins)
    count_row = jnp.full((1, chans), count, jnp.int32).astype(F32)
    gain_in, offset_in = as_row(gains_in), as_row(offsets_in)
    acc1[...] = jnp.zeros_like(acc1)
    acc2[...] = jnp.zeros_like(acc2)
    for w in range(windows):

        def body(rows, w=w):
            first, second = acc1[rows, :], acc2[rows, :]
            for at in range(0, bins, TILE):
                x = xbuf[w, rows, at : at + TILE].astype(F32)
                kept = x * valid_rows[w : w + 1, at : at + TILE]
                first = first + lane_sum(kept)
                second = second + lane_sum(kept * x)
            acc1[rows, :] = first
            acc2[rows, :] = second

        by_rows(chans, body)
    plane = [PlaneSum(copies, place, msg.at[i], slots.at[i]) for i in range(3)]
    over_y = [copies.remote(ymsg.at[i], yin.at[i], partner) for i in range(3)]
    plane[0].start([to_row(acc1[...]), to_row(acc2[...]), count_row])

    put_rows(qext, LANES, lambda rows: xbuf[order[3], rows, :], bins)
    for tap in range(3):
        w_all[:, tap * chans : (tap + 1) * chans] = jnp.transpose(weight[tap])
    total = plane[0].finish()
    filled = total[2:3, :]
    ymsg[0] = jnp.concatenate([total[0:3, :], gain_in, offset_in, total[0:3, :]], axis=0)
    over_y[0].start()
    x1[2].start()
    x1[3].start()

    def norm_of(first, second, gain, offset):
        mean = first / filled
        scale = lax.rsqrt(second / filled - mean * mean + EPS)
        return mean, scale, scale * gain, offset - mean * scale * gain

    mean, scale, a_mine, b_mine = norm_of(total[0:1, :], total[1:2, :], gain_in, offset_in)
    column(A_MINE, a_mine)
    column(B_MINE, b_mine)
    rows_out[...] = jnp.zeros_like(rows_out)
    rows_out[0:1, :] = mean
    rows_out[1:2, :] = scale
    rows_out[2:3, :] = filled
    rows_out[6:7, :] = gain_in
    rows_out[7:8, :] = offset_in

    w_first.wait_recv()
    z_first = copies.take(4)
    w_z = []
    for step in range(1, 4):
        z = (group + step) % 4
        device = {"seq": z * 2 + core}
        out = copies.remote(
            w_other.at[mine_at], w_other.at[mine_at], device, z_first + step, z_first + group
        )
        from_at = share_rows(place.win, core, z)
        w_z.append(
            copies.remote(w_other.at[from_at], w_other.at[from_at], device, z_first + step, z_first + z)
        )
        out.start()

    pl.when(place.shard < 7)(to_left.wait_recv)
    pl.when(place.shard > 0)(to_right.wait_recv)
    put_rows(qext, 0, lambda rows: halo_l[order[3], rows, :], LANES)
    put_rows(qext, LANES + bins, lambda rows: halo_r[order[3], rows, :], LANES)
    ex_at, ec_at = copies.take(3), copies.take(3)
    ex_out = [
        copies.remote(
            qext.at[:, k * piece : (k + 1) * piece + 2 * LANES], ex,
            {"seq": jnp.minimum(place.shard + 2 * k, 7)}, ex_at + k - 1, ex_at,
        )
        for k in range(1, 4)
    ]
    ec_out = [
        copies.remote(
            qext.at[:, LANES + k * piece : LANES + (k + 1) * piece], ec,
            {"seq": jnp.minimum(place.shard + 2 * k, 7)}, ec_at + k - 1, ec_at,
        )
        for k in range(1, 4)
    ]

    @pl.when(group == 0)
    def _():
        for copy in ex_out:
            copy.start()
        put_rows(ex, 0, lambda rows: qext[rows, 0 : piece + 2 * LANES], piece + 2 * LANES)

    def activate(a, b, load, dst, at, size):
        mask = valid_ext[:, lanes_at(at, size)]

        def body(rows):
            pre = load(rows).astype(F32) * wide(a, rows, size) + wide(b, rows, size)
            dst[rows, lanes_at(at, size)] = (gelu(pre) * mask).astype(BF16)

        by_rows(chans, body)

    def mixed(right, left):
        return jnp.where(low, right.astype(F32), left.astype(F32)).astype(BF16)

    def first_halo(role):
        w = order[role]
        return lambda rows: mixed(halo_r[w, rows, :], halo_l[w, rows, :])

    def second_halo(role):
        w = order[2]

        def load(rows):
            near = xbuf[w, rows, half : half + LANES].astype(F32)
            far = xbuf[w, rows, half - LANES : half].astype(F32)
            right = jnp.where(role == 0, near, halo_r[w, rows, :].astype(F32))
            left = jnp.where(role == 0, halo_l[w, rows, :].astype(F32), far)
            return jnp.where(low, right, left).astype(BF16)

        return load

    def third_halo(role):
        return lambda rows: mixed(
            ex[rows, lanes_at(LANES + (role + 1) * eighth, LANES)], ex[rows, lanes_at(role * eighth, LANES)]
        )

    def run_segment(a, b, load, dst, at, size):
        def body(i):
            activate(a, b, lambda rows: load(rows, i * TILE), dst, at + i * TILE, TILE)

        times(size // TILE, body)

    put_rows(hb.at[0], 0, first_halo(side), LANES)
    put_rows(hb.at[1], 0, second_halo(side), LANES)
    activate(A_MINE, B_MINE, lambda rows: hb[0, rows, :], act_m, 0, LANES)
    activate(A_MINE, B_MINE, lambda rows: hb[0, rows, :], act_m, LANES + bins, LANES)
    run_segment(
        A_MINE, B_MINE, lambda rows, at: xbuf[order[side], rows, lanes_at(at, TILE)], act_m, LANES, bins
    )
    put_rows(p1b, 0, first_halo(other), LANES)
    put_rows(p1b, LANES, second_halo(other), LANES)
    put_rows(p1b, 2 * LANES, lambda rows: xbuf[order[2], rows, lanes_at(other * half, half)], half)
    cuts2 = (0, 2 * LANES + half // 2, 2 * LANES + half, 3 * LANES + half + eighth)
    x2 = [copies.remote(p1b.at[:, lo:hi], p2b.at[:, lo:hi], partner) for lo, hi in zip(cuts2, cuts2[1:])]
    x2[0].start()
    for copy in w_z:
        copy.wait_recv()
    block = share_rows(place.win, core, 0, 4)
    block_in = share_rows(1 - place.win, core, 0, 4)
    across = {"win": 1 - place.win}
    w_x_at = copies.take()
    w_x = copies.remote(w_other.at[block], w_other.at[block], across, w_x_at, w_x_at)
    w_x_in = copies.remote(w_other.at[block_in], w_other.at[block_in], across, w_x_at, w_x_at)
    w_x.start()
    activate(A_MINE, B_MINE, lambda rows: hb[1, rows, :], act_m, base2, LANES)
    activate(A_MINE, B_MINE, lambda rows: hb[1, rows, :], act_m, base2 + LANES + half, LANES)
    run_segment(
        A_MINE, B_MINE, lambda rows, at: xbuf[order[2], rows, lanes_at(side * half + at, TILE)],
        act_m, base2 + LANES, half,
    )
    pl.when(place.shard > 0)(to_left.wait_send)
    pl.when(place.shard < 7)(to_right.wait_send)
    cot_loads = [copies.local(cin.at[w], xbuf.at[w]) for w in range(windows)]
    for copy in cot_loads:
        copy.start()
    w_x_in.wait_recv()
    sibling = {"seq": group * 2 + 1 - core}
    w_c_at = [copies.take() for _ in range(2)]
    w_c, w_c_in = [], []
    for w in range(2):
        rows = share_rows(w, core, 0, 4)
        rows_in = share_rows(w, 1 - core, 0, 4)
        w_c.append(copies.remote(w_other.at[rows], w_other.at[rows], sibling, w_c_at[w], w_c_at[w]))
        w_c_in.append(
            copies.remote(w_other.at[rows_in], w_other.at[rows_in], sibling, w_c_at[w], w_c_at[w])
        )
        w_c[w].start()

    over_y[0].wait_recv()
    _, _, a_other, b_other = norm_of(*(yin[0, i : i + 1, :] for i in (0, 1, 3, 4)))
    column(A_OTHER, a_other)
    column(B_OTHER, b_other)
    for copy in w_c_in:
        copy.wait_recv()
    for tap in range(3):
        w_all[:, (3 + tap) * chans : (4 + tap) * chans] = jnp.transpose(
            w_other[tap * chans : (tap + 1) * chans, :]
        )
    for i in range(4):
        x1[i].wait_recv()
        run_segment(
            A_OTHER, B_OTHER, lambda rows, at, i=i: p2a[rows, lanes_at(i * chunk + at, TILE)],
            act_o, LANES + i * chunk, chunk,
        )
        if i == 2:
            for copy in x1:
                copy.wait_send()
            x2[1].start()
    pl.when(group > 0)(lambda: ex_out[0].wait_recv())
    put_rows(p1b, cuts2[2], third_halo(other), LANES)
    put_rows(
        p1b, cuts2[2] + LANES, lambda rows: ex[rows, lanes_at(LANES + other * eighth, eighth)], eighth
    )
    x2[2].start()
    put_rows(hb.at[2], 0, third_halo(side), LANES)
    activate(A_MINE, B_MINE, lambda rows: hb[2, rows, :], act_m, base3, LANES)
    activate(A_MINE, B_MINE, lambda rows: hb[2, rows, :], act_m, base3 + LANES + eighth, LANES)
    run_segment(
        A_MINE, B_MINE, lambda rows, at: ex[rows, lanes_at(LANES + side * eighth + at, TILE)],
        act_m, base3 + LANES, eighth,
    )
    for copy in cot_loads:
        copy.wait()
    put_rows(p2a, 0, lambda rows: xbuf[order[other], rows, :], bins)

    def fill_taps(start):
        for at_half, ref in enumerate((act_m, act_o)):
            cells = ref[:, lanes_at(start, TILE + 2 * LANES)]
            for tap in range(3):
                at = LANES + (tap - 1) * DILATION_BINS
                row = (at_half * 3 + tap) * chans
                cat[row : row + chans, :] = cells[:, at : at + TILE]

    def conv_tiles(start, own, count):
        def body(i):
            fill_taps(start + i * TILE)
            out = dot(w_all[...], cat[...])
            conv[:, lanes_at(own + i * TILE, TILE)] = out
            kept = out * valid_own[:, lanes_at(own + i * TILE, TILE)]
            acc1[...] += lane_sum(kept)
            acc2[...] += lane_sum(kept * out)

        times(count, body)

    acc1[...] = jnp.zeros_like(acc1)
    acc2[...] = jnp.zeros_like(acc2)
    x2[0].wait_recv()
    other_halo = lambda at: lambda rows: p2b[rows, at : at + LANES]
    activate(A_OTHER, B_OTHER, other_halo(0), act_o, 0, LANES)
    activate(A_OTHER, B_OTHER, other_halo(0), act_o, LANES + bins, LANES)
    activate(A_OTHER, B_OTHER, other_halo(LANES), act_o, base2, LANES)
    activate(A_OTHER, B_OTHER, other_halo(LANES), act_o, base2 + LANES + half, LANES)
    other_second = lambda rows, at: p2b[rows, lanes_at(2 * LANES + at, TILE)]
    run_segment(A_OTHER, B_OTHER, other_second, act_o, base2 + LANES, half // 2)
    conv_tiles(0, 0, bins // TILE)
    x2[1].wait_recv()
    c1 = [
        copies.remote(p2a.at[:, i * chunk : (i + 1) * chunk], p1a.at[:, i * chunk : (i + 1) * chunk], partner)
        for i in range(4)
    ]
    c1[0].start()
    c1[1].start()
    run_segment(
        A_OTHER, B_OTHER, lambda rows, at: other_second(rows, half // 2 + at),
        act_o, base2 + LANES + half // 2, half // 2,
    )
    conv_tiles(base2, own2, half // TILE)
    x2[2].wait_recv()
    activate(A_OTHER, B_OTHER, other_halo(cuts2[2]), act_o, base3, LANES)
    activate(A_OTHER, B_OTHER, other_halo(cuts2[2]), act_o, base3 + LANES + eighth, LANES)
    run_segment(
        A_OTHER, B_OTHER, lambda rows, at: p2b[rows, lanes_at(cuts2[2] + LANES + at, TILE)],
        act_o, base3 + LANES, eighth,
    )
    conv_tiles(base3, own3, eighth // TILE)
    plane[1].start([to_row(acc1[...]), to_row(acc2[...])])
    for copy in x2:
        copy.wait_send()
    c1[2].start()

    acc1[...] = jnp.zeros_like(acc1)
    for w in range(windows):

        def body(rows, w=w):
            acc1[rows, :] += lane_sum(xbuf[w, rows, :].astype(F32))

        by_rows(chans, body)
    bias_row = to_row(acc1[...])
    total = plane[1].finish()
    ymsg[1] = total
    over_y[1].start()
    c1[3].start()

    @pl.when(group == 0)
    def _():
        for copy in ex_out:
            copy.wait_send()

    put_rows(qext, LANES, lambda rows: xbuf[order[3], rows, :], bins)

    @pl.when(group == 0)
    def _():
        for copy in ec_out:
            copy.start()
        put_rows(ec, 0, lambda rows: qext[rows, LANES : LANES + piece], piece)
    put_rows(p2b, 0, lambda rows: xbuf[order[2], rows, lanes_at(other * half, half)], half)
    cuts = (0, half // 2, half, half + eighth)
    c2 = [copies.remote(p2b.at[:, lo:hi], p1b.at[:, lo:hi], partner) for lo, hi in zip(cuts, cuts[1:])]
    c1[2].wait_recv()
    c2[0].start()

    over_y[1].wait_recv()
    total = ymsg[1] + yin[1]
    gain_mid, offset_mid = as_row(gains_mid), as_row(offsets_mid)
    mean = total[0:1, :] / filled
    scale = lax.rsqrt(total[1:2, :] / filled - mean * mean + EPS)
    for at, row in ((MEAN, mean), (SCALE, scale), (GAIN, gain_mid), (OFFSET, offset_mid), (FACTOR, gain_mid * scale)):
        column(at, row)

    def act_tile(i):
        at = lanes_at(i * TILE, TILE)
        mask = valid_own[:, at]

        def body(rows):
            norm = (conv[rows, at] - wide(MEAN, rows, TILE)) * wide(SCALE, rows, TILE)
            pre = norm * wide(GAIN, rows, TILE) + wide(OFFSET, rows, TILE)
            actm[rows, at] = (gelu(pre) * mask).astype(BF16)

        by_rows(chans, body)

    times(conv.shape[1] // TILE, act_tile)
    back_to = {"seq": core}
    e_at = copies.take(8)
    e_parts = ((actm.at[:, own3:], side), (e_act, other))
    e_home = [
        copies.remote(
            src, acts.at[3, :, lanes_at(group * piece + role * eighth, eighth)], back_to,
            e_at + which, e_at + 2 * group + which,
        )
        for which, (src, role) in enumerate(e_parts)
    ]
    e_mine = [copies.local(src, acts.at[3, :, lanes_at(role * eighth, eighth)]) for src, role in e_parts]
    pl.when(group > 0)(e_home[0].start)
    pl.when(group == 0)(e_mine[0].start)
    keeps = [
        copies.local(actm.at[:, 0:bins], acts.at[side]),
        copies.local(actm.at[:, own2:own3], acts.at[2, :, lanes_at(side * half, half)]),
    ]
    for copy in keeps:
        copy.start()

    acc1[...] = jnp.zeros_like(acc1)
    acc2[...] = jnp.zeros_like(acc2)
    gp[...] = jnp.zeros_like(gp)

    def back_product(mine, theirs):
        cat[0:chans, :] = mine
        cat[chans : 2 * chans, :] = theirs
        tmp[...] = dot(point[...], cat[0:chans, :]) + dot(w_other[3 * chans :, :], cat[chans : 2 * chans, :])

    def grad_rows(rows, at, mask):
        norm = (conv[rows, at] - wide(MEAN, rows, TILE)) * wide(SCALE, rows, TILE)
        pre = norm * wide(GAIN, rows, TILE) + wide(OFFSET, rows, TILE)
        return norm, mask * gelu_slope(pre) * tmp[rows, :]

    def sum_tile(mine, theirs, own):
        back_product(mine, theirs)
        at = lanes_at(own, TILE)
        mask = valid_own[:, at]

        def body(rows):
            norm, part = grad_rows(rows, at, mask)
            acc1[rows, :] += lane_sum(part)
            acc2[rows, :] += lane_sum(part * norm)

        by_rows(chans, body)
        gp[...] += dot_t(actm[:, at], cat[0 : 2 * chans, :])

    def grad_tile(mine, theirs, own):
        back_product(mine, theirs)
        at = lanes_at(own, TILE)
        mask = valid_own[:, at]

        def body(rows):
            norm, part = grad_rows(rows, at, mask)
            kept = mask * (wide(BETA, rows, TILE) + norm * wide(GAMMA, rows, TILE))
            gco[rows, at] = (wide(FACTOR, rows, TILE) * (part - kept)).astype(BF16)

        by_rows(chans, body)

    def over_first(run, lo, hi):
        def body(i):
            at = lanes_at(lo + i * TILE, TILE)
            run(xbuf[order[side], :, at], p1a[:, at], lo + i * TILE)

        times((hi - lo) // TILE, body)

    def over_second(run, lo, hi):
        def body(i):
            at = lo + i * TILE
            run(
                xbuf[order[2], :, lanes_at(side * half + at, TILE)], p1b[:, lanes_at(at, TILE)], own2 + at
            )

        times((hi - lo) // TILE, body)

    def over_third(run):
        run(ec[:, lanes_at(side * eighth, TILE)], p1b[:, half : half + TILE], own3)

    t3_extra = copies.remote(actm.at[:, own3:], e_act, partner)
    t3 = [
        copies.remote(
            actm.at[:, own2 + i * TILE : own2 + (i + 1) * TILE],
            acts.at[2, :, lanes_at(side * half + i * TILE, TILE)],
            partner,
        )
        for i in range(half // TILE)
    ]
    for i in range(4):
        if i != 2:
            c1[i].wait_recv()
        if i == 3:
            c2[1].start()
        over_first(sum_tile, i * chunk, (i + 1) * chunk)
    pl.when(group > 0)(lambda: ec_out[0].wait_recv())
    put_rows(p2b, half, lambda rows: ec[rows, lanes_at(other * eighth, eighth)], eighth)
    c2[2].start()
    c2[0].wait_recv()
    over_second(sum_tile, 0, half // 2)
    c2[1].wait_recv()
    t3_extra.start()
    t3[0].start()
    over_second(sum_tile, half // 2, half)
    c2[2].wait_recv()
    over_third(sum_tile)
    plane[2].start([to_row(acc1[...]), to_row(acc2[...]), bias_row])
    total = plane[2].finish()
    ymsg[2] = total
    over_y[2].start()
    for copy in t3[1:]:
        copy.start()
    t3_extra.wait_recv()
    pl.when(group > 0)(e_home[1].start)
    pl.when(group == 0)(e_mine[1].start)
    over_y[2].wait_recv()
    beta = ymsg[2, 0:1, :] + yin[2, 0:1, :]
    gamma = ymsg[2, 1:2, :] + yin[2, 1:2, :]
    rows_out[3:4, :] = beta
    rows_out[4:5, :] = gamma
    rows_out[5:6, :] = ymsg[2, 2:3, :]
    column(BETA, beta / filled)
    column(GAMMA, gamma / filled)

    over_third(grad_tile)
    t4_extra = copies.remote(gco.at[:, own3:], g_extra, partner)
    t4_extra.start()
    over_second(grad_tile, 0, half // 2)
    t4 = copies.remote(gco.at[:, own2 : own2 + half // 2], g_two, partner)
    t4.start()
    over_second(grad_tile, half // 2, half)
    over_first(grad_tile, 0, bins)
    g_keep = copies.local(gco, g_own)
    g_keep.start()

    weight_sum = conv.at[:, 0 : 6 * chans]
    weight_sum[...] = jnp.zeros_like(weight_sum)

    def weight_tiles(start, own, count):
        def body(i):
            fill_taps(start + i * TILE)
            weight_sum[...] += dot_t(gco[:, lanes_at(own + i * TILE, TILE)], cat[...])

        times(count, body)

    weight_tiles(0, 0, bins // TILE)
    weight_tiles(base2, own2, half // TILE)
    weight_tiles(base3, own3, eighth // TILE)

    gw_keep = copies.local(weight_sum, gw)
    gw_keep.start()

    @pl.when(group > 0)
    def _():
        for copy in e_home:
            copy.wait_send()

    @pl.when(group == 0)
    def _():
        for copy in e_mine:
            copy.wait()
        for copy in ec_out:
            copy.wait_send()
        for z in range(1, 4):
            for which, role in enumerate((side, other)):
                at = acts.at[3, :, lanes_at(z * piece + role * eighth, eighth)]
                copies.remote(at, at, back_to, e_at, e_at + 2 * z + which).wait_recv()

    for copy in keeps + [g_keep, gw_keep]:
        copy.wait()
    for copy in plane:
        copy.drain()
    for copy in [w_first, w_x, *w_c, *w_z, *over_y, *c1, *c2, t3_extra, *t3, t4_extra, t4]:
        copy.wait_send()
    for copy in [*t3, t4_extra, t4]:
        copy.wait_recv()


def second_kernel(
    lengths, xin, acts_in, g_own, g_two, g_extra, gw, gp, weights, rows_in,
    acts, grads, rows_out, conv_grad, point_grad,
    gs, xbuf, halo_r, halo_l, cat, tmp, acc1, acc2, cols, msg, slots,
    parts, parts_core, parts_win, parts_z, parts_side, summed, weight, send, recv,
):
    del acts_in
    place = Place()
    side, group, core, partner = place.side, place.group, place.core, place.partner
    other = 1 - side
    copies = Copies(send, recv)
    windows, chans, bins = xbuf.shape
    half, piece, eighth, chunk = bins // 2, bins // 4, bins // 8, bins // 4
    own2, own3 = bins, bins + half

    own_loads = [
        copies.local(g_own.at[:, 0:bins], gs.at[side, :, LANES : LANES + bins]),
        copies.local(g_own.at[:, own2:own3], gs.at[2, :, lanes_at(LANES + side * half, half)]),
        copies.local(g_two, gs.at[2, :, lanes_at(LANES + other * half, half // 2)]),
    ]
    extra = ((g_own.at[:, own3:], side), (g_extra, other))
    extra_loads = [
        copies.local(src, gs.at[3, :, lanes_at(LANES + role * eighth, eighth)]) for src, role in extra
    ]
    loads = [copies.local(xin.at[w], xbuf.at[w]) for w in range(windows)]
    depth = conv_grad.shape[0] * chans
    part_loads = [copies.local(gw.at[:, i * depth : (i + 1) * depth], parts.at[i, :, :depth]) for i in (0, 1)]
    part_loads += [copies.local(gp.at[:, i * chans : (i + 1) * chans], parts.at[i, :, depth:]) for i in (0, 1)]
    for copy in own_loads + loads + part_loads:
        copy.start()

    @pl.when(group == 0)
    def _():
        for copy in extra_loads:
            copy.start()

    place.greet()
    t4 = copies.remote(
        g_own.at[:, own2 + half // 2 : own3],
        gs.at[2, :, lanes_at(LANES + side * half + half // 2, half // 2)],
        partner,
    )
    t4_first = [
        copies.remote(
            g_own.at[:, i * chunk : (i + 1) * chunk],
            gs.at[side, :, LANES + i * chunk : LANES + (i + 1) * chunk],
            partner,
        )
        for i in range(4)
    ]
    t3_first = []
    for i in range(4):
        at = acts.at[side, :, i * chunk : (i + 1) * chunk]
        t3_first.append(copies.remote(at, at, partner))
    t4.start()
    for copy in t4_first:
        copy.start()
    t3_first[0].start()

    tail = parts_side.shape[0]
    core_rows = lambda c: pl.ds(pl.multiple_of(8 * tail * c, tail), 8 * tail)
    win_rows = lambda w: pl.ds(pl.multiple_of(8 * tail * core + 4 * tail * w, tail), 4 * tail)
    z_rows = lambda z: pl.ds(
        pl.multiple_of(8 * tail * core + 4 * tail * place.win + tail * z, tail), tail
    )
    sibling, across = {"seq": group * 2 + 1 - core}, {"win": 1 - place.win}
    s_core = copies.remote(parts.at[:, core_rows(1 - core), :], parts_core, sibling)
    s_win = copies.remote(parts.at[:, win_rows(1 - place.win), :], parts_win, across)
    s_z_at = copies.take(4)
    s_z, s_z_in = [], []
    g_z_at = copies.take(4)
    g_z, g_z_in = [], []
    for step in range(1, 4):
        z = (group + step) % 4
        device = {"seq": z * 2 + core}
        s_z.append(
            copies.remote(parts.at[:, z_rows(z), :], parts_z.at[group], device, s_z_at + step, s_z_at + group)
        )
        s_z_in.append(
            copies.remote(parts.at[:, z_rows(z), :], parts_z.at[z], device, s_z_at + step, s_z_at + z)
        )
        g_z.append(
            copies.remote(
                summed.at[z_rows(group), :], summed.at[z_rows(group), :], device, g_z_at + step, g_z_at + group
            )
        )
        g_z_in.append(
            copies.remote(summed.at[z_rows(z), :], summed.at[z_rows(z), :], device, g_z_at + step, g_z_at + z)
        )
    s_side = copies.remote(parts.at[1, z_rows(group), :], parts_side, partner)
    g_win_at, g_core_at = copies.take(), copies.take()
    both = lambda at, rows, rows_in, device: tuple(
        copies.remote(summed.at[r, :], summed.at[r, :], device, at, at) for r in (rows, rows_in)
    )
    g_win, g_win_in = both(g_win_at, win_rows(place.win), win_rows(1 - place.win), across)
    g_core, g_core_in = both(g_core_at, core_rows(core), core_rows(1 - core), sibling)
    for copy in part_loads:
        copy.wait()
    s_core.start()

    class Halo:
        def __init__(self, slot, last):
            self.slot, self.last = slot, last
            self.left = copies.remote(
                gs.at[slot, :, LANES : 2 * LANES], halo_r.at[slot], {"seq": jnp.maximum(place.shard - 1, 0)}
            )
            self.right = copies.remote(
                gs.at[slot, :, bins : bins + LANES], halo_l.at[slot], {"seq": jnp.minimum(place.shard + 1, 7)}
            )

        def start(self):
            pl.when((place.shard > 0) & (place.shard <= self.last))(self.left.start)
            pl.when(place.shard < self.last)(self.right.start)

        def finish(self):
            @pl.when(place.shard < self.last)
            def _():
                self.left.wait_recv()
                gs[self.slot, :, LANES + bins :] = halo_r[self.slot]

            @pl.when(place.shard >= self.last)
            def _():
                gs[self.slot, :, LANES + bins :] = jnp.zeros((chans, LANES), BF16)

            @pl.when(place.shard > 0)
            def _():
                self.right.wait_recv()
                gs[self.slot, :, 0:LANES] = halo_l[self.slot]

            @pl.when(place.shard == 0)
            def _():
                gs[self.slot, :, 0:LANES] = jnp.zeros((chans, LANES), BF16)

            pl.when((place.shard > 0) & (place.shard <= self.last))(self.left.wait_send)
            pl.when(place.shard < self.last)(self.right.wait_send)

    halos = {name: Halo(slot, last) for name, slot, last in (("own", side, 7), ("third", 2, 7), ("other", other, 7), ("quarter", 3, 1))}
    own_loads[0].wait()
    halos["own"].start()
    e_at = copies.take(8)
    back_to = {"seq": core}
    e_home = [
        copies.remote(
            src, gs.at[3, :, lanes_at(LANES + group * piece + role * eighth, eighth)], back_to,
            e_at + which, e_at + 2 * group + which,
        )
        for which, (src, role) in enumerate(extra)
    ]

    @pl.when(group > 0)
    def _():
        for copy in e_home:
            copy.start()

    order = Order(lengths)
    for tap in range(weights.shape[0]):
        weight[:, tap * chans : (tap + 1) * chans] = weights[tap]
    names = {"mean": 0, "scale": 1, "gain": 2, "offset": 3}
    for at, row in enumerate((0, 1, 6, 7)):
        cols[at] = to_column(rows_in[row : row + 1, :])
    wide = lambda name, rows: spread_lanes(cols[names[name], rows, :], TILE)
    acc1[...] = jnp.zeros_like(acc1)
    acc2[...] = jnp.zeros_like(acc2)

    def through(slot):
        def tile(i):
            cells = gs[slot, :, lanes_at(i * TILE, TILE + 2 * LANES)]
            for tap in range(3):
                at = LANES - (tap - 1) * DILATION_BINS
                cat[tap * chans : (tap + 1) * chans, :] = cells[:, at : at + TILE]
            tmp[...] = dot(weight[...], cat[...])
            at = lanes_at(i * TILE, TILE)
            mask = valid_lanes(place.shard * bins + i * TILE, TILE, order.size(slot))
            window = order[slot]

            def body(rows):
                norm = (xbuf[window, rows, at].astype(F32) - wide("mean", rows)) * wide("scale", rows)
                part = mask * gelu_slope(norm * wide("gain", rows) + wide("offset", rows)) * tmp[rows, :]
                acc1[rows, :] += lane_sum(part)
                acc2[rows, :] += lane_sum(part * norm)
                gs[slot, rows, at] = part.astype(BF16)

            by_rows(chans, body)

        times(bins // TILE, tile)

    keeps = []

    def keep(slot):
        copy = copies.local(gs.at[slot, :, 0:bins], grads.at[slot])
        copy.start()
        keeps.append(copy)

    for copy in loads:
        copy.wait()
    halos["own"].finish()
    through(side)
    keep(side)
    s_core.wait_recv()
    parts[:, core_rows(core), :] += parts_core[...]
    s_win.start()
    own_loads[1].wait()
    own_loads[2].wait()
    t4.wait_recv()
    halos["third"].start()
    quarter_keep = copies.local(gs.at[3, :, 0:bins], grads.at[3])

    @pl.when(group == 0)
    def _():
        for copy in extra_loads:
            copy.wait()
        for z in range(1, 4):
            for which, role in enumerate((side, other)):
                at = gs.at[3, :, lanes_at(LANES + z * piece + role * eighth, eighth)]
                copies.remote(at, at, back_to, e_at, e_at + 2 * z + which).wait_recv()
        halos["quarter"].start()

    halos["third"].finish()
    through(2)
    keep(2)
    s_win.wait_recv()
    parts[:, win_rows(place.win), :] += parts_win[...]
    for copy in s_z:
        copy.start()

    @pl.when(group == 0)
    def _():
        halos["quarter"].finish()
        through(3)
        quarter_keep.start()

    for copy in s_z_in:
        copy.wait_recv()
    parts_z[group] = parts[:, z_rows(group), :]
    total = parts_z[0]
    for z in range(1, 4):
        total = total + parts_z[z]
    parts[:, z_rows(group), :] = total
    s_side.start()
    for copy in t3_first[1:]:
        copy.start()
    for copy in t4_first:
        copy.wait_recv()
    halos["other"].start()
    halos["other"].finish()
    s_side.wait_recv()
    summed[z_rows(group), :] = parts[0, z_rows(group), :] + parts_side[...]
    for copy in g_z:
        copy.start()
    through(other)
    keep(other)
    plane = PlaneSum(copies, place, msg, slots)
    plane.start([to_row(acc1[...]), to_row(acc2[...])])
    for copy in g_z_in:
        copy.wait_recv()
    g_win.start()
    rows_out[...] = plane.finish()
    g_win_in.wait_recv()
    g_core.start()
    plane.drain()
    g_core_in.wait_recv()
    for tap in range(conv_grad.shape[0]):
        conv_grad[tap] = jnp.transpose(summed[:, tap * chans : (tap + 1) * chans])
    point_grad[...] = summed[:, depth:]
    for copy in [s_core, s_win, s_side, *s_z, *g_z, g_win, g_core]:
        copy.wait_send()
    for copy in keeps:
        copy.wait()

    @pl.when(group == 0)
    def _():
        quarter_keep.wait()

    @pl.when(group > 0)
    def _():
        for copy in e_home:
            copy.wait_send()

    for copy in [t4, *t4_first, *t3_first]:
        copy.wait_send()
    for copy in t3_first:
        copy.wait_recv()


def last_kernel(
    lengths, x, c, act, grad, point, bias, rows_one, rows_two, conv_in, point_in,
    out, grad_out, gain_in, offset_in, gain_mid, offset_mid, grad_bias, conv_out, point_out,
    weight, cols, tmp,
):
    window, tile = pl.program_id(0), pl.program_id(1)
    side, shard = lax.axis_index("ch"), lax.axis_index("seq")
    conv_out[...] = conv_in[...]
    point_out[...] = point_in[...]

    @pl.when((window == 0) & (tile == 0))
    def _():
        weight[...] = jnp.transpose(point[...])
        mean, scale, filled, gain = (rows_one[i : i + 1, :] for i in (0, 1, 2, 6))
        beta, gamma = rows_two[0:1, :], rows_two[1:2, :]
        factor = gain * scale
        slope = factor * scale * gamma / filled
        for at, row in enumerate(
            (factor, slope, factor * beta / filled - mean * slope, bias[...].reshape(beta.shape))
        ):
            cols[at] = to_column(row)
        size = gain_in.shape[0]
        gain_in[...] = gamma.reshape(size)
        offset_in[...] = beta.reshape(size)
        grad_bias[...] = rows_one[5:6, :].reshape(size)
        part = size // 2
        for ref, row in ((gain_mid, rows_one[4:5, :]), (offset_mid, rows_one[3:4, :])):
            ref[...] = jnp.where(side == 0, row[:, :part], row[:, part:])

    size = x.shape[2]
    bins = pl.num_programs(1) * size
    mask = valid_lanes(shard * bins + tile * size, size, lengths[window]) > 0.0
    tmp[...] = dot(weight[...], act[0])
    def body(rows):
        factor, slope, shift, more = (spread_lanes(cols[i, rows, :], TILE) for i in range(4))
        for at in range(0, size, TILE):
            lanes = slice(at, at + TILE)
            kept = mask[:, lanes]
            xs = x[0, rows, lanes].astype(F32)
            out[0, rows, lanes] = (xs + jnp.where(kept, tmp[rows, lanes], 0.0) + more).astype(BF16)
            back = factor * grad[0, rows, lanes].astype(F32) - xs * slope - shift
            grad_out[0, rows, lanes] = (
                c[0, rows, lanes].astype(F32) + jnp.where(kept, back, 0.0)
            ).astype(BF16)

    by_rows(x.shape[1], body)


def local_pair(
    inputs,
    lengths,
    gain_in,
    offset_in,
    conv_weight,
    gain_mid,
    offset_mid,
    point_weight,
    point_bias,
    cotangent,
):
    windows, chans, bins = inputs.shape
    taps, _, bottle = conv_weight.shape
    piece, half, eighth = bins // 4, bins // 2, bins // 8
    widened, packed = bins + half + eighth + 6 * LANES, bins + half + eighth

    vmem = pl.BlockSpec(memory_space=pltpu.VMEM)
    hbm = pl.BlockSpec(memory_space=pltpu.HBM)
    smem = pl.BlockSpec(memory_space=pltpu.SMEM)
    shape = jax.ShapeDtypeStruct
    acts, g_own, g_two, g_extra, gw, gp, rows_one = pl.pallas_call(
        first_kernel,
        in_specs=[smem, hbm, hbm, hbm, hbm, vmem, vmem, vmem, vmem, vmem, vmem],
        out_specs=[hbm, hbm, hbm, hbm, hbm, vmem, vmem],
        out_shape=[
            shape((windows, bottle, bins), BF16),
            shape((bottle, packed), BF16),
            shape((bottle, half // 2), BF16),
            shape((bottle, eighth), BF16),
            shape((bottle, 2 * taps * chans), F32),
            shape((bottle, 2 * chans), F32),
            shape((8, chans), F32),
        ],
        scratch_shapes=[
            pltpu.VMEM((windows, chans, bins), BF16),
            pltpu.VMEM((chans, bins), BF16),
            pltpu.VMEM((chans, bins), BF16),
            pltpu.VMEM((chans, half + eighth + 3 * LANES), BF16),
            pltpu.VMEM((chans, half + eighth + 3 * LANES), BF16),
            pltpu.VMEM((chans, bins + 2 * LANES), BF16),
            pltpu.VMEM((chans, piece + 2 * LANES), BF16),
            pltpu.VMEM((chans, piece), BF16),
            pltpu.VMEM((windows, chans, LANES), BF16),
            pltpu.VMEM((windows, chans, LANES), BF16),
            pltpu.VMEM((3, chans, LANES), BF16),
            pltpu.VMEM((chans, widened), BF16),
            pltpu.VMEM((chans, widened), BF16),
            pltpu.VMEM((bottle, packed), F32),
            pltpu.VMEM((bottle, packed), BF16),
            pltpu.VMEM((bottle, packed), BF16),
            pltpu.VMEM((bottle, 2 * taps * chans), BF16),
            pltpu.VMEM(((taps + 1) * chans, bottle), BF16),
            pltpu.VMEM((bottle, eighth), BF16),
            pltpu.VMEM((2 * taps * chans, TILE), BF16),
            pltpu.VMEM((bottle, TILE), F32),
            pltpu.VMEM((chans, LANES), F32),
            pltpu.VMEM((chans, LANES), F32),
            pltpu.VMEM((11, chans, LANES), F32),
            pltpu.VMEM((3, 8, chans), F32),
            pltpu.VMEM((3, PLANE, 8, chans), F32),
            pltpu.VMEM((3, 8, chans), F32),
            pltpu.VMEM((3, 8, chans), F32),
            pltpu.VMEM((windows, bins), F32),
            pltpu.VMEM((1, widened), F32),
            pltpu.VMEM((1, packed), F32),
            pltpu.SemaphoreType.DMA((128,)),
            pltpu.SemaphoreType.DMA((128,)),
        ],
        compiler_params=pltpu.CompilerParams(
            collective_id=0, has_side_effects=True, vmem_limit_bytes=VMEM_BYTES
        ),
        cost_estimate=pl.CostEstimate(flops=60 * 10**9, bytes_accessed=10**8, transcendentals=0),
    )(
        lengths, inputs, cotangent, conv_weight, point_weight, conv_weight, point_weight,
        gain_in, offset_in, gain_mid, offset_mid,
    )

    share = bottle // PLANE
    acts, grads, rows_two, conv_grad, point_grad = pl.pallas_call(
        second_kernel,
        in_specs=[smem, hbm, hbm, hbm, hbm, hbm, hbm, hbm, vmem, vmem],
        out_specs=[hbm, hbm, vmem, vmem, vmem],
        out_shape=[
            shape((windows, bottle, bins), BF16),
            shape((windows, chans, bins), BF16),
            shape((8, chans), F32),
            shape((taps, chans, bottle), F32),
            shape((bottle, chans), F32),
        ],
        input_output_aliases={2: 0},
        scratch_shapes=[
            pltpu.VMEM((windows, bottle, bins + 2 * LANES), BF16),
            pltpu.VMEM((windows, chans, bins), BF16),
            pltpu.VMEM((windows, bottle, LANES), BF16),
            pltpu.VMEM((windows, bottle, LANES), BF16),
            pltpu.VMEM((taps * bottle, TILE), BF16),
            pltpu.VMEM((chans, TILE), F32),
            pltpu.VMEM((chans, LANES), F32),
            pltpu.VMEM((chans, LANES), F32),
            pltpu.VMEM((4, chans, LANES), F32),
            pltpu.VMEM((8, chans), F32),
            pltpu.VMEM((PLANE, 8, chans), F32),
            pltpu.VMEM((2, bottle, (taps + 1) * chans), F32),
            pltpu.VMEM((2, bottle // 2, (taps + 1) * chans), F32),
            pltpu.VMEM((2, bottle // 4, (taps + 1) * chans), F32),
            pltpu.VMEM((4, 2, share, (taps + 1) * chans), F32),
            pltpu.VMEM((share, (taps + 1) * chans), F32),
            pltpu.VMEM((bottle, (taps + 1) * chans), F32),
            pltpu.VMEM((chans, taps * bottle), BF16),
            pltpu.SemaphoreType.DMA((128,)),
            pltpu.SemaphoreType.DMA((128,)),
        ],
        compiler_params=pltpu.CompilerParams(
            collective_id=1, has_side_effects=True, vmem_limit_bytes=VMEM_BYTES
        ),
        cost_estimate=pl.CostEstimate(flops=60 * 10**9, bytes_accessed=10**8, transcendentals=0),
    )(lengths, inputs, acts, g_own, g_two, g_extra, gw, gp, conv_weight, rows_one)

    def slot_of(window, sizes):
        rank = jnp.int32(0)
        for other in range(windows):
            longer = sizes[other] > sizes[window]
            ahead = (sizes[other] == sizes[window]) & (other < window)
            rank = rank + jnp.where(longer | ahead, 1, 0)
        return rank

    tile = bins
    at = pl.BlockSpec((1, chans, tile), lambda w, i, p: (w, 0, i))
    at_slot = pl.BlockSpec((1, chans, tile), lambda w, i, p: (slot_of(w, p), 0, i))
    whole = lambda rows, size: pl.BlockSpec((rows, size), lambda w, i, p: (0, 0))
    steps = bins // tile
    part = chans // (windows * steps)
    conv_at = pl.BlockSpec((taps, part, bottle), lambda w, i, p: (0, w * steps + i, 0))
    point_at = pl.BlockSpec((part, chans), lambda w, i, p: (w * steps + i, 0))
    line = lambda size: pl.BlockSpec((size,), lambda w, i, p: (0,))
    outputs, grad_inputs, gamma_in, beta_in, gamma_mid, beta_mid, grad_bias, conv_grad, point_grad = pl.pallas_call(
        last_kernel,
        grid_spec=pltpu.PrefetchScalarGridSpec(
            num_scalar_prefetch=1,
            grid=(windows, bins // tile),
            in_specs=[
                at, at, at_slot, at_slot,
                whole(bottle, chans), line(chans), whole(8, chans), whole(8, chans), conv_at, point_at,
            ],
            out_specs=[
                at, at, line(chans), line(chans), whole(1, bottle // 2), whole(1, bottle // 2),
                line(chans), conv_at, point_at,
            ],
            scratch_shapes=[
                pltpu.VMEM((chans, bottle), BF16),
                pltpu.VMEM((4, chans, LANES), F32),
                pltpu.VMEM((chans, tile), F32),
            ],
        ),
        out_shape=[
            shape(inputs.shape, BF16),
            shape(inputs.shape, BF16),
            shape((chans,), F32),
            shape((chans,), F32),
            shape((1, bottle // 2), F32),
            shape((1, bottle // 2), F32),
            shape((chans,), F32),
            shape((taps, chans, bottle), F32),
            shape((bottle, chans), F32),
        ],
        compiler_params=pltpu.CompilerParams(vmem_limit_bytes=VMEM_BYTES),
        cost_estimate=pl.CostEstimate(flops=4 * 10**9, bytes_accessed=6 * 10**7, transcendentals=0),
    )(
        lengths, inputs, cotangent, acts, grads, point_weight, point_bias, rows_one, rows_two,
        conv_grad, point_grad,
    )
    return (
        outputs,
        grad_inputs,
        gamma_in,
        beta_in,
        conv_grad,
        gamma_mid[0],
        beta_mid[0],
        point_grad,
        grad_bias,
    )


def solution(mesh):
    paired = mesh.shape["ch"] == 2 and mesh.shape["seq"] == 8 and mesh.shape["win"] == 2

    def local(*args):
        windows, chans, bins = args[0].shape
        if paired and windows == 4 and chans == args[4].shape[2] and bins == 8 * TILE:
            return local_pair(*args)
        return local_any(*args)

    return jax.shard_map(
        local,
        mesh=mesh,
        in_specs=(
            P("win", "ch", "seq"),
            P("win"),
            P("ch"),
            P("ch"),
            P(None, "ch", None),
            P(),
            P(),
            P(None, "ch"),
            P("ch"),
            P("win", "ch", "seq"),
        ),
        out_specs=(
            P("win", "ch", "seq"),
            P("win", "ch", "seq"),
            P("ch"),
            P("ch"),
            P(None, "ch", None),
            P("ch"),
            P("ch"),
            P(None, "ch"),
            P("ch"),
        ),
        check_vma=False,
    )
```

```python
import functools

import jax
import jax.numpy as jnp
from jax import lax
from jax.experimental import pallas as pl
from jax.experimental.pallas import tpu as pltpu
from jax.sharding import PartitionSpec as P

DILATION_BINS = 57


EPS = 1e-05
LANES = 128
TILE = 384
VMEM_BYTES = 63 * 1000 * 1000


def with_halo(cells, sides, width):
    for axis, dim in sides:
        count = lax.axis_size(axis)
        ends = count - 1
        head = lax.slice_in_dim(cells, 0, width, axis=dim)
        tail = lax.slice_in_dim(cells, cells.shape[dim] - width, cells.shape[dim], axis=dim)
        cells = jnp.concatenate(
            [
                lax.ppermute(tail, axis, [(i, (i + 1) % count) for i in range(ends)]),
                cells,
                lax.ppermute(head, axis, [((i + 1) % count, i) for i in range(ends)]),
            ],
            axis=dim,
        )
    return cells


def norm_sums(first_term, second_term):
    return lax.psum((first_term, second_term), ("seq", "win"))


def column(vector):
    return vector[:, None]


def local_any(
    inputs,
    lengths,
    gain_in,
    offset_in,
    conv_weight,
    gain_mid,
    offset_mid,
    point_weight,
    point_bias,
    cotangent,
):
    win_count, chan_local, count_of_bins = inputs.shape
    count_of_taps = conv_weight.shape[0]
    bottle = conv_weight.shape[2]
    bottle_local = bottle // lax.axis_size("ch")
    offset_at = lax.axis_index("ch") * bottle_local
    places = lax.axis_index("seq") * count_of_bins + jnp.arange(count_of_bins, dtype=jnp.int32)
    valid_rows = (places[None, :] < lengths[:, None]).astype(jnp.float32)[:, None, :]
    x_wide = inputs.astype(jnp.float32)
    sum_first = jnp.sum(valid_rows * x_wide, axis=(0, 2))
    sum_second = jnp.sum(valid_rows * x_wide * x_wide, axis=(0, 2))
    sum_first, sum_second, filled = lax.psum(
        (sum_first, sum_second, jnp.sum(valid_rows)), ("seq", "win")
    )
    mean_in = sum_first / filled
    scale_in = lax.rsqrt(sum_second / filled - mean_in * mean_in + EPS)
    norm_in = (x_wide - column(mean_in)) * column(scale_in)
    pre_in = norm_in * column(gain_in) + column(offset_in)
    input_activation, gelu_in_back = jax.vjp(jax.nn.gelu, pre_in)
    lowered_activation = (input_activation * valid_rows).astype(jnp.bfloat16)
    padded_input = with_halo(lowered_activation, (("seq", 2),), DILATION_BINS)
    stacked_taps = jnp.concatenate(
        [
            padded_input[
                :,
                :,
                kernel_tap_index * DILATION_BINS : kernel_tap_index * DILATION_BINS + count_of_bins,
            ]
            for kernel_tap_index in range(count_of_taps)
        ],
        axis=1,
    )
    flat_weight = conv_weight.reshape(count_of_taps * chan_local, bottle)
    partial_value = jnp.einsum(
        "wkt,kf->wft", stacked_taps, flat_weight, preferred_element_type=jnp.float32
    )
    conv_out = lax.psum_scatter(partial_value, "ch", scatter_dimension=1, tiled=True)
    gain_part = lax.dynamic_slice_in_dim(gain_mid, offset_at, bottle_local)
    offset_part = lax.dynamic_slice_in_dim(offset_mid, offset_at, bottle_local)
    mid_first, mid_second = norm_sums(
        jnp.sum(valid_rows * conv_out, axis=(0, 2)),
        jnp.sum(valid_rows * conv_out * conv_out, axis=(0, 2)),
    )
    mean_mid = mid_first / filled
    scale_mid = lax.rsqrt(mid_second / filled - mean_mid * mean_mid + EPS)
    norm_mid = (conv_out - column(mean_mid)) * column(scale_mid)
    pre_mid = norm_mid * column(gain_part) + column(offset_part)
    act_mid, gelu_mid_back = jax.vjp(jax.nn.gelu, pre_mid)
    act_mid_low = (act_mid * valid_rows).astype(jnp.bfloat16)
    mixed_in = lax.all_gather(act_mid_low, "ch", axis=1, tiled=True)
    branch = jnp.einsum("wft,fc->wct", mixed_in, point_weight, preferred_element_type=jnp.float32)
    outputs = (x_wide + branch + column(point_bias)).astype(jnp.bfloat16)
    grad_point = jnp.einsum("wft,wct->fc", mixed_in, cotangent, preferred_element_type=jnp.float32)
    grad_bias = jnp.sum(cotangent.astype(jnp.float32), axis=(0, 2))
    partial_back = jnp.einsum(
        "wct,fc->wft", cotangent, point_weight, preferred_element_type=jnp.float32
    )
    grad_act_mid = lax.psum_scatter(partial_back, "ch", scatter_dimension=1, tiled=True)
    grad_pre_mid = gelu_mid_back(grad_act_mid * valid_rows)[0]
    local_beta = jnp.sum(grad_pre_mid, axis=(0, 2))
    local_gamma = jnp.sum(grad_pre_mid * norm_mid, axis=(0, 2))
    grad_point, grad_bias, beta_mid, gamma_mid = lax.psum(
        (grad_point, grad_bias, local_beta, local_gamma), ("seq", "win")
    )
    grad_conv_out = column(gain_part * scale_mid) * (
        grad_pre_mid - valid_rows * (column(beta_mid) + norm_mid * column(gamma_mid)) / filled
    )
    grad_low = grad_conv_out.astype(jnp.bfloat16)
    complete_gradient = lax.all_gather(grad_low, "ch", axis=1, tiled=True)
    grad_conv = jnp.einsum(
        "wkt,wft->kf", stacked_taps, complete_gradient, preferred_element_type=jnp.float32
    )
    grad_conv = grad_conv.reshape(count_of_taps, chan_local, bottle)
    padded_gradient = with_halo(complete_gradient, (("seq", 2),), DILATION_BINS)
    back_taps = jnp.concatenate(
        [
            padded_gradient[
                :,
                :,
                (count_of_taps - 1 - kernel_tap_index)
                * DILATION_BINS : (count_of_taps - 1 - kernel_tap_index)
                * DILATION_BINS
                + count_of_bins,
            ]
            for kernel_tap_index in range(count_of_taps)
        ],
        axis=1,
    )
    back_weight = jnp.transpose(conv_weight, (0, 2, 1)).reshape(count_of_taps * bottle, chan_local)
    grad_act_in = jnp.einsum(
        "wkt,kc->wct", back_taps, back_weight, preferred_element_type=jnp.float32
    )
    grad_pre_in = gelu_in_back(grad_act_in * valid_rows)[0]
    local_beta_in = jnp.sum(grad_pre_in, axis=(0, 2))
    local_gamma_in = jnp.sum(grad_pre_in * norm_in, axis=(0, 2))
    grad_conv, beta_in, gamma_in = lax.psum(
        (grad_conv, local_beta_in, local_gamma_in), ("seq", "win")
    )
    grad_inputs = (
        cotangent.astype(jnp.float32)
        + column(gain_in * scale_in)
        * (grad_pre_in - valid_rows * (column(beta_in) + norm_in * column(gamma_in)) / filled)
    ).astype(jnp.bfloat16)
    return (
        outputs,
        grad_inputs,
        gamma_in,
        beta_in,
        grad_conv,
        gamma_mid,
        beta_mid,
        grad_point,
        grad_bias,
    )


MESH = pl.DeviceIdType.MESH
ROWS = 32
PLANE = 16
F32 = jnp.float32
BF16 = jnp.bfloat16
GELU_A = 0.7978845608028654
GELU_B = 0.044715


def dot(a, b):
    return jnp.dot(a, b, preferred_element_type=F32)


def dot_t(a, b):
    return lax.dot_general(a, b, (((1,), (1,)), ((), ())), preferred_element_type=F32)


def lane_sum(cells):
    total = cells[:, :LANES]
    for at in range(LANES, cells.shape[1], LANES):
        total = total + cells[:, at : at + LANES]
    return total


def gelu(v):
    return 0.5 * v * (1.0 + jnp.tanh(GELU_A * (v + GELU_B * (v * v * v))))


def gelu_slope(v):
    square = v * v
    th = jnp.tanh(GELU_A * (v + GELU_B * (v * square)))
    return 0.5 * (1.0 + th) + 0.5 * v * (1.0 - th * th) * (GELU_A * (1.0 + 3.0 * GELU_B * square))


def lanes_at(at, size):
    return pl.ds(pl.multiple_of(at, LANES), size)


def by_rows(count, body):
    def step(i, carry):
        body(pl.ds(pl.multiple_of(i * ROWS, ROWS), ROWS))
        return carry

    lax.fori_loop(0, count // ROWS, step, 0, unroll=6)


def times(count, body):
    def step(i, carry):
        body(i)
        return carry

    lax.fori_loop(0, count, step, 0)


def spread_lanes(cells, size):
    return jnp.concatenate([cells] * (size // LANES), axis=1)


def to_column(row):
    return jnp.transpose(jnp.broadcast_to(row, (LANES, row.shape[1])))


def to_row(cells):
    return jnp.sum(jnp.transpose(cells), axis=0, keepdims=True)


class Copies:
    def __init__(self, send, recv):
        self.send, self.recv, self.used = send, recv, 0

    def take(self, count=1):
        self.used += count
        return self.used - count

    def remote(self, src, dst, device, send_at=None, recv_at=None):
        if send_at is None:
            send_at = self.take()
        if recv_at is None:
            recv_at = send_at
        return pltpu.make_async_remote_copy(
            src_ref=src,
            dst_ref=dst,
            send_sem=self.send.at[send_at],
            recv_sem=self.recv.at[recv_at],
            device_id=device,
            device_id_type=MESH,
        )

    def local(self, src, dst):
        return pltpu.make_async_copy(src, dst, self.send.at[self.take()])


class Place:
    def __init__(self):
        self.side, self.shard, self.win = (lax.axis_index(n) for n in ("ch", "seq", "win"))
        self.group, self.core = self.shard // 2, self.shard % 2
        self.me = self.win * 8 + self.shard
        self.partner = {"ch": 1 - self.side}

    def peer(self, step):
        at = (self.me + step) % PLANE
        return at, {"seq": at % 8, "win": at // 8}

    def greet(self):
        barrier = pltpu.get_barrier_semaphore()
        pl.semaphore_signal(barrier, 1, device_id=self.partner, device_id_type=MESH)
        for step in range(1, PLANE):
            pl.semaphore_signal(barrier, 1, device_id=self.peer(step)[1], device_id_type=MESH)
        pl.semaphore_wait(barrier, PLANE)


class PlaneSum:
    def __init__(self, copies, place, mine, slots):
        self.place, self.mine, self.slots = place, mine, slots
        first = copies.take(PLANE)
        self.out, self.into = [], []
        for step in range(1, PLANE):
            at, device = place.peer(step)
            self.out.append(
                copies.remote(mine, slots.at[place.me], device, first + step, first + place.me)
            )
            self.into.append(copies.remote(mine, slots.at[at], device, first + step, first + at))

    def start(self, rows):
        for at, row in enumerate(rows):
            self.mine[at : at + 1, :] = row
        for copy in self.out:
            copy.start()
        self.slots[self.place.me] = self.mine[...]

    def finish(self):
        for copy in self.into:
            copy.wait_recv()
        total = self.slots[0]
        for at in range(1, PLANE):
            total = total + self.slots[at]
        return total

    def drain(self):
        for copy in self.out:
            copy.wait_send()


A_MINE, B_MINE, A_OTHER, B_OTHER, MEAN, SCALE, GAIN, OFFSET, FACTOR, BETA, GAMMA = range(11)


class Order:
    def __init__(self, lengths):
        self.lengths = [lengths[i] for i in range(4)]
        ranks = []
        for i, mine in enumerate(self.lengths):
            rank = jnp.int32(0)
            for j, their in enumerate(self.lengths):
                if j < i:
                    rank = rank + jnp.where(their >= mine, 1, 0)
                elif j > i:
                    rank = rank + jnp.where(their > mine, 1, 0)
            ranks.append(rank)

        def at_slot(slot, values):
            found = jnp.int32(0)
            for rank, value in zip(ranks, values, strict=True):
                found = found + jnp.where(rank == slot, value, 0)
            return found

        self.windows = [at_slot(slot, range(4)) for slot in range(4)]
        self.sizes = [at_slot(slot, self.lengths) for slot in range(4)]

    def of(self, values, slot):
        if isinstance(slot, int):
            return values[slot]
        found = values[0]
        for at in range(1, 4):
            found = jnp.where(slot == at, values[at], found)
        return found

    def __getitem__(self, slot):
        return self.of(self.windows, slot)

    def size(self, slot):
        return self.of(self.sizes, slot)


def valid_lanes(start, size, limit):
    spots = start + lax.broadcasted_iota(jnp.int32, (1, size), 1)
    return ((spots >= 0) & (spots < limit)).astype(F32)


def as_row(ref):
    return ref[...].reshape(1, ref.shape[0])


def first_kernel(
    lengths, xin, cin, weight_hbm, point_hbm, weight, point, gains_in, offsets_in, gains_mid, offsets_mid,
    acts, g_own, g_two, g_extra, gw, gp, rows_out,
    xbuf, p1a, p2a, p1b, p2b, qext, ex, ec, halo_r, halo_l, hb,
    act_m, act_o, conv, actm, gco, w_all, w_other, e_act, cat, tmp, acc1, acc2, cols,
    msg, slots, ymsg, yin, valid_rows, valid_ext, valid_own, send, recv,
):
    place = Place()
    side, group, core, partner = place.side, place.group, place.core, place.partner
    other = 1 - side
    copies = Copies(send, recv)
    windows, chans, bins = xbuf.shape
    half, piece, eighth, chunk = bins // 2, bins // 4, bins // 8, bins // 4
    base2, base3 = bins + 2 * LANES, bins + half + 4 * LANES
    own2, own3 = bins, bins + half
    low = lax.broadcasted_iota(jnp.int32, (ROWS, LANES), 1) < LANES // 2
    order = Order(lengths)

    def put_rows(dst, at, load, size):
        def body(rows):
            dst[rows, lanes_at(at, size)] = load(rows)

        by_rows(chans, body)

    def column(at, row):
        cols[at] = to_column(row)

    def wide(at, rows, size):
        return spread_lanes(cols[at, rows, :], size)

    loads = [copies.local(xin.at[w], xbuf.at[w]) for w in range(windows)]
    for copy in loads:
        copy.start()
    place.greet()
    share = w_other.shape[0] // PLANE
    share_rows = lambda w, c, z, size=1: pl.ds(
        pl.multiple_of((w * 8 + c * 4 + z) * share, share), size * share
    )
    mine_at = share_rows(place.win, core, group)
    share_at = place.win * 8 + core * 4 + group
    taps, conv_shares = weight.shape[0], weight.shape[0] * chans // share
    per_tap = chans // share
    w_at = copies.take()
    w_tap = copies.remote(
        weight_hbm.at[jnp.minimum(share_at // per_tap, taps - 1), pl.ds(pl.multiple_of(share_at % per_tap * share, share), share)],
        w_other.at[mine_at], partner, w_at, w_at,
    )
    w_point = copies.remote(
        point_hbm.at[pl.ds(pl.multiple_of(share_at % per_tap * share, share), share)],
        w_other.at[mine_at], partner, w_at, w_at,
    )
    w_first = w_point
    pl.when(share_at < conv_shares)(w_tap.start)
    pl.when(share_at >= conv_shares)(w_point.start)
    for copy in loads:
        copy.wait()
    x1 = [
        copies.remote(p1a.at[:, i * chunk : (i + 1) * chunk], p2a.at[:, i * chunk : (i + 1) * chunk], partner)
        for i in range(4)
    ]
    for i in range(4):
        put_rows(p1a, i * chunk, lambda rows, i=i: xbuf[order[other], rows, i * chunk : (i + 1) * chunk], chunk)
        if i < 2:
            x1[i].start()
    to_left = copies.remote(xbuf.at[:, :, 0:LANES], halo_r, {"seq": jnp.maximum(place.shard - 1, 0)})
    to_right = copies.remote(xbuf.at[:, :, bins - LANES : bins], halo_l, {"seq": jnp.minimum(place.shard + 1, 7)})
    pl.when(place.shard > 0)(to_left.start)
    pl.when(place.shard < 7)(to_right.start)

    @pl.when(place.shard == 0)
    def _():
        halo_l[...] = jnp.zeros_like(halo_l)

    @pl.when(place.shard == 7)
    def _():
        halo_r[...] = jnp.zeros_like(halo_r)

    for w in range(windows):
        valid_rows[w : w + 1, :] = valid_lanes(place.shard * bins, bins, order.lengths[w])
    at = 0
    for start, size, limit in (
        (place.shard * bins, bins, order.size(side)),
        (place.shard * bins + side * half, half, order.size(2)),
        (core * bins + group * piece + side * eighth, eighth, order.size(3)),
    ):
        valid_ext[:, at : at + size + 2 * LANES] = valid_lanes(start - LANES, size + 2 * LANES, limit)
        at += size + 2 * LANES
    for to, at, size in ((0, LANES, bins), (own2, base2 + LANES, half), (own3, base3 + LANES, eighth)):
        valid_own[:, to : to + size] = valid_ext[:, at : at + size]
    count = jnp.int32(0)
    for length in order.lengths:
        count = count + jnp.clip(length - place.shard * bins, 0, bins)
    count_row = jnp.full((1, chans), count, jnp.int32).astype(F32)
    gain_in, offset_in = as_row(gains_in), as_row(offsets_in)
    acc1[...] = jnp.zeros_like(acc1)
    acc2[...] = jnp.zeros_like(acc2)
    for w in range(windows):

        def body(rows, w=w):
            first, second = acc1[rows, :], acc2[rows, :]
            for at in range(0, bins, TILE):
                x = xbuf[w, rows, at : at + TILE].astype(F32)
                kept = x * valid_rows[w : w + 1, at : at + TILE]
                first = first + lane_sum(kept)
                second = second + lane_sum(kept * x)
            acc1[rows, :] = first
            acc2[rows, :] = second

        by_rows(chans, body)
    plane = [PlaneSum(copies, place, msg.at[i], slots.at[i]) for i in range(3)]
    over_y = [copies.remote(ymsg.at[i], yin.at[i], partner) for i in range(3)]
    plane[0].start([to_row(acc1[...]), to_row(acc2[...]), count_row])

    put_rows(qext, LANES, lambda rows: xbuf[order[3], rows, :], bins)
    for tap in range(3):
        w_all[:, tap * chans : (tap + 1) * chans] = jnp.transpose(weight[tap])
    total = plane[0].finish()
    filled = total[2:3, :]
    ymsg[0] = jnp.concatenate([total[0:3, :], gain_in, offset_in, total[0:3, :]], axis=0)
    over_y[0].start()
    x1[2].start()
    x1[3].start()

    def norm_of(first, second, gain, offset):
        mean = first / filled
        scale = lax.rsqrt(second / filled - mean * mean + EPS)
        return mean, scale, scale * gain, offset - mean * scale * gain

    mean, scale, a_mine, b_mine = norm_of(total[0:1, :], total[1:2, :], gain_in, offset_in)
    column(A_MINE, a_mine)
    column(B_MINE, b_mine)
    rows_out[...] = jnp.zeros_like(rows_out)
    rows_out[0:1, :] = mean
    rows_out[1:2, :] = scale
    rows_out[2:3, :] = filled
    rows_out[6:7, :] = gain_in
    rows_out[7:8, :] = offset_in

    w_first.wait_recv()
    z_first = copies.take(4)
    w_z = []
    for step in range(1, 4):
        z = (group + step) % 4
        device = {"seq": z * 2 + core}
        out = copies.remote(
            w_other.at[mine_at], w_other.at[mine_at], device, z_first + step, z_first + group
        )
        from_at = share_rows(place.win, core, z)
        w_z.append(
            copies.remote(w_other.at[from_at], w_other.at[from_at], device, z_first + step, z_first + z)
        )
        out.start()

    pl.when(place.shard < 7)(to_left.wait_recv)
    pl.when(place.shard > 0)(to_right.wait_recv)
    put_rows(qext, 0, lambda rows: halo_l[order[3], rows, :], LANES)
    put_rows(qext, LANES + bins, lambda rows: halo_r[order[3], rows, :], LANES)
    ex_at, ec_at = copies.take(3), copies.take(3)
    ex_out = [
        copies.remote(
            qext.at[:, k * piece : (k + 1) * piece + 2 * LANES], ex,
            {"seq": jnp.minimum(place.shard + 2 * k, 7)}, ex_at + k - 1, ex_at,
        )
        for k in range(1, 4)
    ]
    ec_out = [
        copies.remote(
            qext.at[:, LANES + k * piece : LANES + (k + 1) * piece], ec,
            {"seq": jnp.minimum(place.shard + 2 * k, 7)}, ec_at + k - 1, ec_at,
        )
        for k in range(1, 4)
    ]

    @pl.when(group == 0)
    def _():
        for copy in ex_out:
            copy.start()
        put_rows(ex, 0, lambda rows: qext[rows, 0 : piece + 2 * LANES], piece + 2 * LANES)

    def activate(a, b, load, dst, at, size):
        mask = valid_ext[:, lanes_at(at, size)]

        def body(rows):
            pre = load(rows).astype(F32) * wide(a, rows, size) + wide(b, rows, size)
            dst[rows, lanes_at(at, size)] = (gelu(pre) * mask).astype(BF16)

        by_rows(chans, body)

    def mixed(right, left):
        return jnp.where(low, right.astype(F32), left.astype(F32)).astype(BF16)

    def first_halo(role):
        w = order[role]
        return lambda rows: mixed(halo_r[w, rows, :], halo_l[w, rows, :])

    def second_halo(role):
        w = order[2]

        def load(rows):
            near = xbuf[w, rows, half : half + LANES].astype(F32)
            far = xbuf[w, rows, half - LANES : half].astype(F32)
            right = jnp.where(role == 0, near, halo_r[w, rows, :].astype(F32))
            left = jnp.where(role == 0, halo_l[w, rows, :].astype(F32), far)
            return jnp.where(low, right, left).astype(BF16)

        return load

    def third_halo(role):
        return lambda rows: mixed(
            ex[rows, lanes_at(LANES + (role + 1) * eighth, LANES)], ex[rows, lanes_at(role * eighth, LANES)]
        )

    def run_segment(a, b, load, dst, at, size):
        def body(i):
            activate(a, b, lambda rows: load(rows, i * TILE), dst, at + i * TILE, TILE)

        times(size // TILE, body)

    put_rows(hb.at[0], 0, first_halo(side), LANES)
    put_rows(hb.at[1], 0, second_halo(side), LANES)
    activate(A_MINE, B_MINE, lambda rows: hb[0, rows, :], act_m, 0, LANES)
    activate(A_MINE, B_MINE, lambda rows: hb[0, rows, :], act_m, LANES + bins, LANES)
    run_segment(
        A_MINE, B_MINE, lambda rows, at: xbuf[order[side], rows, lanes_at(at, TILE)], act_m, LANES, bins
    )
    put_rows(p1b, 0, first_halo(other), LANES)
    put_rows(p1b, LANES, second_halo(other), LANES)
    put_rows(p1b, 2 * LANES, lambda rows: xbuf[order[2], rows, lanes_at(other * half, half)], half)
    cuts2 = (0, 2 * LANES + half // 2, 2 * LANES + half, 3 * LANES + half + eighth)
    x2 = [copies.remote(p1b.at[:, lo:hi], p2b.at[:, lo:hi], partner) for lo, hi in zip(cuts2, cuts2[1:])]
    x2[0].start()
    for copy in w_z:
        copy.wait_recv()
    block = share_rows(place.win, core, 0, 4)
    block_in = share_rows(1 - place.win, core, 0, 4)
    across = {"win": 1 - place.win}
    w_x_at = copies.take()
    w_x = copies.remote(w_other.at[block], w_other.at[block], across, w_x_at, w_x_at)
    w_x_in = copies.remote(w_other.at[block_in], w_other.at[block_in], across, w_x_at, w_x_at)
    w_x.start()
    activate(A_MINE, B_MINE, lambda rows: hb[1, rows, :], act_m, base2, LANES)
    activate(A_MINE, B_MINE, lambda rows: hb[1, rows, :], act_m, base2 + LANES + half, LANES)
    run_segment(
        A_MINE, B_MINE, lambda rows, at: xbuf[order[2], rows, lanes_at(side * half + at, TILE)],
        act_m, base2 + LANES, half,
    )
    pl.when(place.shard > 0)(to_left.wait_send)
    pl.when(place.shard < 7)(to_right.wait_send)
    cot_loads = [copies.local(cin.at[w], xbuf.at[w]) for w in range(windows)]
    for copy in cot_loads:
        copy.start()
    w_x_in.wait_recv()
    sibling = {"seq": group * 2 + 1 - core}
    w_c_at = [copies.take() for _ in range(2)]
    w_c, w_c_in = [], []
    for w in range(2):
        rows = share_rows(w, core, 0, 4)
        rows_in = share_rows(w, 1 - core, 0, 4)
        w_c.append(copies.remote(w_other.at[rows], w_other.at[rows], sibling, w_c_at[w], w_c_at[w]))
        w_c_in.append(
            copies.remote(w_other.at[rows_in], w_other.at[rows_in], sibling, w_c_at[w], w_c_at[w])
        )
        w_c[w].start()

    over_y[0].wait_recv()
    _, _, a_other, b_other = norm_of(*(yin[0, i : i + 1, :] for i in (0, 1, 3, 4)))
    column(A_OTHER, a_other)
    column(B_OTHER, b_other)
    for copy in w_c_in:
        copy.wait_recv()
    for tap in range(3):
        w_all[:, (3 + tap) * chans : (4 + tap) * chans] = jnp.transpose(
            w_other[tap * chans : (tap + 1) * chans, :]
        )
    for i in range(4):
        x1[i].wait_recv()
        run_segment(
            A_OTHER, B_OTHER, lambda rows, at, i=i: p2a[rows, lanes_at(i * chunk + at, TILE)],
            act_o, LANES + i * chunk, chunk,
        )
        if i == 2:
            for copy in x1:
                copy.wait_send()
            x2[1].start()
    pl.when(group > 0)(lambda: ex_out[0].wait_recv())
    put_rows(p1b, cuts2[2], third_halo(other), LANES)
    put_rows(
        p1b, cuts2[2] + LANES, lambda rows: ex[rows, lanes_at(LANES + other * eighth, eighth)], eighth
    )
    x2[2].start()
    put_rows(hb.at[2], 0, third_halo(side), LANES)
    activate(A_MINE, B_MINE, lambda rows: hb[2, rows, :], act_m, base3, LANES)
    activate(A_MINE, B_MINE, lambda rows: hb[2, rows, :], act_m, base3 + LANES + eighth, LANES)
    run_segment(
        A_MINE, B_MINE, lambda rows, at: ex[rows, lanes_at(LANES + side * eighth + at, TILE)],
        act_m, base3 + LANES, eighth,
    )
    for copy in cot_loads:
        copy.wait()
    put_rows(p2a, 0, lambda rows: xbuf[order[other], rows, :], bins)

    def fill_taps(start):
        for at_half, ref in enumerate((act_m, act_o)):
            cells = ref[:, lanes_at(start, TILE + 2 * LANES)]
            for tap in range(3):
                at = LANES + (tap - 1) * DILATION_BINS
                row = (at_half * 3 + tap) * chans
                cat[row : row + chans, :] = cells[:, at : at + TILE]

    def conv_tiles(start, own, count):
        def body(i):
            fill_taps(start + i * TILE)
            out = dot(w_all[...], cat[...])
            conv[:, lanes_at(own + i * TILE, TILE)] = out
            kept = out * valid_own[:, lanes_at(own + i * TILE, TILE)]
            acc1[...] += lane_sum(kept)
            acc2[...] += lane_sum(kept * out)

        times(count, body)

    acc1[...] = jnp.zeros_like(acc1)
    acc2[...] = jnp.zeros_like(acc2)
    x2[0].wait_recv()
    other_halo = lambda at: lambda rows: p2b[rows, at : at + LANES]
    activate(A_OTHER, B_OTHER, other_halo(0), act_o, 0, LANES)
    activate(A_OTHER, B_OTHER, other_halo(0), act_o, LANES + bins, LANES)
    activate(A_OTHER, B_OTHER, other_halo(LANES), act_o, base2, LANES)
    activate(A_OTHER, B_OTHER, other_halo(LANES), act_o, base2 + LANES + half, LANES)
    other_second = lambda rows, at: p2b[rows, lanes_at(2 * LANES + at, TILE)]
    run_segment(A_OTHER, B_OTHER, other_second, act_o, base2 + LANES, half // 2)
    conv_tiles(0, 0, bins // TILE)
    x2[1].wait_recv()
    c1 = [
        copies.remote(p2a.at[:, i * chunk : (i + 1) * chunk], p1a.at[:, i * chunk : (i + 1) * chunk], partner)
        for i in range(4)
    ]
    c1[0].start()
    c1[1].start()
    run_segment(
        A_OTHER, B_OTHER, lambda rows, at: other_second(rows, half // 2 + at),
        act_o, base2 + LANES + half // 2, half // 2,
    )
    conv_tiles(base2, own2, half // TILE)
    x2[2].wait_recv()
    activate(A_OTHER, B_OTHER, other_halo(cuts2[2]), act_o, base3, LANES)
    activate(A_OTHER, B_OTHER, other_halo(cuts2[2]), act_o, base3 + LANES + eighth, LANES)
    run_segment(
        A_OTHER, B_OTHER, lambda rows, at: p2b[rows, lanes_at(cuts2[2] + LANES + at, TILE)],
        act_o, base3 + LANES, eighth,
    )
    conv_tiles(base3, own3, eighth // TILE)
    plane[1].start([to_row(acc1[...]), to_row(acc2[...])])
    for copy in x2:
        copy.wait_send()
    c1[2].start()

    acc1[...] = jnp.zeros_like(acc1)
    for w in range(windows):

        def body(rows, w=w):
            acc1[rows, :] += lane_sum(xbuf[w, rows, :].astype(F32))

        by_rows(chans, body)
    bias_row = to_row(acc1[...])
    total = plane[1].finish()
    ymsg[1] = total
    over_y[1].start()
    c1[3].start()

    @pl.when(group == 0)
    def _():
        for copy in ex_out:
            copy.wait_send()

    put_rows(qext, LANES, lambda rows: xbuf[order[3], rows, :], bins)

    @pl.when(group == 0)
    def _():
        for copy in ec_out:
            copy.start()
        put_rows(ec, 0, lambda rows: qext[rows, LANES : LANES + piece], piece)
    put_rows(p2b, 0, lambda rows: xbuf[order[2], rows, lanes_at(other * half, half)], half)
    cuts = (0, half // 2, half, half + eighth)
    c2 = [copies.remote(p2b.at[:, lo:hi], p1b.at[:, lo:hi], partner) for lo, hi in zip(cuts, cuts[1:])]
    c1[2].wait_recv()
    c2[0].start()

    over_y[1].wait_recv()
    total = ymsg[1] + yin[1]
    gain_mid, offset_mid = as_row(gains_mid), as_row(offsets_mid)
    mean = total[0:1, :] / filled
    scale = lax.rsqrt(total[1:2, :] / filled - mean * mean + EPS)
    for at, row in ((MEAN, mean), (SCALE, scale), (GAIN, gain_mid), (OFFSET, offset_mid), (FACTOR, gain_mid * scale)):
        column(at, row)

    def act_tile(i):
        at = lanes_at(i * TILE, TILE)
        mask = valid_own[:, at]

        def body(rows):
            norm = (conv[rows, at] - wide(MEAN, rows, TILE)) * wide(SCALE, rows, TILE)
            pre = norm * wide(GAIN, rows, TILE) + wide(OFFSET, rows, TILE)
            actm[rows, at] = (gelu(pre) * mask).astype(BF16)

        by_rows(chans, body)

    times(conv.shape[1] // TILE, act_tile)
    back_to = {"seq": core}
    e_at = copies.take(8)
    e_parts = ((actm.at[:, own3:], side), (e_act, other))
    e_home = [
        copies.remote(
            src, acts.at[3, :, lanes_at(group * piece + role * eighth, eighth)], back_to,
            e_at + which, e_at + 2 * group + which,
        )
        for which, (src, role) in enumerate(e_parts)
    ]
    e_mine = [copies.local(src, acts.at[3, :, lanes_at(role * eighth, eighth)]) for src, role in e_parts]
    pl.when(group > 0)(e_home[0].start)
    pl.when(group == 0)(e_mine[0].start)
    keeps = [
        copies.local(actm.at[:, 0:bins], acts.at[side]),
        copies.local(actm.at[:, own2:own3], acts.at[2, :, lanes_at(side * half, half)]),
    ]
    for copy in keeps:
        copy.start()

    acc1[...] = jnp.zeros_like(acc1)
    acc2[...] = jnp.zeros_like(acc2)
    gp[...] = jnp.zeros_like(gp)

    def back_product(mine, theirs):
        cat[0:chans, :] = mine
        cat[chans : 2 * chans, :] = theirs
        tmp[...] = dot(point[...], cat[0:chans, :]) + dot(w_other[3 * chans :, :], cat[chans : 2 * chans, :])

    def grad_rows(rows, at, mask):
        norm = (conv[rows, at] - wide(MEAN, rows, TILE)) * wide(SCALE, rows, TILE)
        pre = norm * wide(GAIN, rows, TILE) + wide(OFFSET, rows, TILE)
        return norm, mask * gelu_slope(pre) * tmp[rows, :]

    def sum_tile(mine, theirs, own):
        back_product(mine, theirs)
        at = lanes_at(own, TILE)
        mask = valid_own[:, at]

        def body(rows):
            norm, part = grad_rows(rows, at, mask)
            acc1[rows, :] += lane_sum(part)
            acc2[rows, :] += lane_sum(part * norm)

        by_rows(chans, body)
        gp[...] += dot_t(actm[:, at], cat[0 : 2 * chans, :])

    def grad_tile(mine, theirs, own):
        back_product(mine, theirs)
        at = lanes_at(own, TILE)
        mask = valid_own[:, at]

        def body(rows):
            norm, part = grad_rows(rows, at, mask)
            kept = mask * (wide(BETA, rows, TILE) + norm * wide(GAMMA, rows, TILE))
            gco[rows, at] = (wide(FACTOR, rows, TILE) * (part - kept)).astype(BF16)

        by_rows(chans, body)

    def over_first(run, lo, hi):
        def body(i):
            at = lanes_at(lo + i * TILE, TILE)
            run(xbuf[order[side], :, at], p1a[:, at], lo + i * TILE)

        times((hi - lo) // TILE, body)

    def over_second(run, lo, hi):
        def body(i):
            at = lo + i * TILE
            run(
                xbuf[order[2], :, lanes_at(side * half + at, TILE)], p1b[:, lanes_at(at, TILE)], own2 + at
            )

        times((hi - lo) // TILE, body)

    def over_third(run):
        run(ec[:, lanes_at(side * eighth, TILE)], p1b[:, half : half + TILE], own3)

    t3_extra = copies.remote(actm.at[:, own3:], e_act, partner)
    t3 = [
        copies.remote(
            actm.at[:, own2 + i * TILE : own2 + (i + 1) * TILE],
            acts.at[2, :, lanes_at(side * half + i * TILE, TILE)],
            partner,
        )
        for i in range(half // TILE)
    ]
    for i in range(4):
        if i != 2:
            c1[i].wait_recv()
        if i == 3:
            c2[1].start()
        over_first(sum_tile, i * chunk, (i + 1) * chunk)
    pl.when(group > 0)(lambda: ec_out[0].wait_recv())
    put_rows(p2b, half, lambda rows: ec[rows, lanes_at(other * eighth, eighth)], eighth)
    c2[2].start()
    c2[0].wait_recv()
    over_second(sum_tile, 0, half // 2)
    c2[1].wait_recv()
    t3_extra.start()
    t3[0].start()
    over_second(sum_tile, half // 2, half)
    c2[2].wait_recv()
    over_third(sum_tile)
    plane[2].start([to_row(acc1[...]), to_row(acc2[...]), bias_row])
    total = plane[2].finish()
    ymsg[2] = total
    over_y[2].start()
    for copy in t3[1:]:
        copy.start()
    t3_extra.wait_recv()
    pl.when(group > 0)(e_home[1].start)
    pl.when(group == 0)(e_mine[1].start)
    over_y[2].wait_recv()
    beta = ymsg[2, 0:1, :] + yin[2, 0:1, :]
    gamma = ymsg[2, 1:2, :] + yin[2, 1:2, :]
    rows_out[3:4, :] = beta
    rows_out[4:5, :] = gamma
    rows_out[5:6, :] = ymsg[2, 2:3, :]
    column(BETA, beta / filled)
    column(GAMMA, gamma / filled)

    over_third(grad_tile)
    t4_extra = copies.remote(gco.at[:, own3:], g_extra, partner)
    t4_extra.start()
    over_second(grad_tile, 0, half // 4)
    t4 = copies.remote(gco.at[:, own2 : own2 + half // 4], g_two, partner)
    t4.start()
    over_second(grad_tile, half // 4, half)
    over_first(grad_tile, 0, bins)
    g_keep = copies.local(gco, g_own)
    g_keep.start()

    weight_sum = conv.at[:, 0 : 6 * chans]
    weight_sum[...] = jnp.zeros_like(weight_sum)

    def weight_tiles(start, own, count):
        def body(i):
            fill_taps(start + i * TILE)
            weight_sum[...] += dot_t(gco[:, lanes_at(own + i * TILE, TILE)], cat[...])

        times(count, body)

    weight_tiles(0, 0, bins // TILE)
    weight_tiles(base2, own2, half // TILE)
    weight_tiles(base3, own3, eighth // TILE)

    gw_keep = copies.local(weight_sum, gw)
    gw_keep.start()

    @pl.when(group > 0)
    def _():
        for copy in e_home:
            copy.wait_send()

    @pl.when(group == 0)
    def _():
        for copy in e_mine:
            copy.wait()
        for copy in ec_out:
            copy.wait_send()
        for z in range(1, 4):
            for which, role in enumerate((side, other)):
                at = acts.at[3, :, lanes_at(z * piece + role * eighth, eighth)]
                copies.remote(at, at, back_to, e_at, e_at + 2 * z + which).wait_recv()

    for copy in keeps + [g_keep, gw_keep]:
        copy.wait()
    for copy in plane:
        copy.drain()
    for copy in [w_first, w_x, *w_c, *w_z, *over_y, *c1, *c2, t3_extra, *t3, t4_extra, t4]:
        copy.wait_send()
    for copy in [*t3, t4_extra, t4]:
        copy.wait_recv()


def second_kernel(
    lengths, xin, cin, acts_in, g_own, g_two, g_extra, gw, gp, weights, rows_in,
    acts, grads, rows_out, conv_grad, point_grad,
    gs, xbuf, cbuf, halo_r, halo_l, cat, tmp, acc1, acc2, cols, msg, slots,
    parts, parts_core, parts_win, parts_z, parts_side, summed, weight, send, recv,
):
    del acts_in
    place = Place()
    side, group, core, partner = place.side, place.group, place.core, place.partner
    other = 1 - side
    copies = Copies(send, recv)
    windows, chans, bins = xbuf.shape
    half, piece, eighth, chunk = bins // 2, bins // 4, bins // 8, bins // 4
    own2, own3 = bins, bins + half

    own_loads = [
        copies.local(g_own.at[:, 0:bins], gs.at[side, :, LANES : LANES + bins]),
        copies.local(g_own.at[:, own2:own3], gs.at[2, :, lanes_at(LANES + side * half, half)]),
        copies.local(g_two, gs.at[2, :, lanes_at(LANES + other * half, half // 4)]),
    ]
    extra = ((g_own.at[:, own3:], side), (g_extra, other))
    extra_loads = [
        copies.local(src, gs.at[3, :, lanes_at(LANES + role * eighth, eighth)]) for src, role in extra
    ]
    loads = [copies.local(xin.at[w], xbuf.at[w]) for w in range(windows)]
    depth = conv_grad.shape[0] * chans
    part_loads = [copies.local(gw.at[:, i * depth : (i + 1) * depth], parts.at[i, :, :depth]) for i in (0, 1)]
    part_loads += [copies.local(gp.at[:, i * chans : (i + 1) * chans], parts.at[i, :, depth:]) for i in (0, 1)]
    cot_loads = [copies.local(cin.at[w], cbuf.at[w]) for w in range(windows)]
    for copy in own_loads + loads + part_loads + cot_loads:
        copy.start()

    @pl.when(group == 0)
    def _():
        for copy in extra_loads:
            copy.start()

    place.greet()
    t4 = copies.remote(
        g_own.at[:, own2 + half // 4 : own3],
        gs.at[2, :, lanes_at(LANES + side * half + half // 4, half - half // 4)],
        partner,
    )
    t4_first = [
        copies.remote(
            g_own.at[:, i * chunk : (i + 1) * chunk],
            gs.at[side, :, LANES + i * chunk : LANES + (i + 1) * chunk],
            partner,
        )
        for i in range(4)
    ]
    t3_first = []
    for i in range(4):
        at = acts.at[side, :, i * chunk : (i + 1) * chunk]
        t3_first.append(copies.remote(at, at, partner))
    t4.start()
    for copy in t4_first:
        copy.start()
    t3_first[0].start()

    tail = parts_side.shape[0]
    core_rows = lambda c: pl.ds(pl.multiple_of(8 * tail * c, tail), 8 * tail)
    win_rows = lambda w: pl.ds(pl.multiple_of(8 * tail * core + 4 * tail * w, tail), 4 * tail)
    z_rows = lambda z: pl.ds(
        pl.multiple_of(8 * tail * core + 4 * tail * place.win + tail * z, tail), tail
    )
    sibling, across = {"seq": group * 2 + 1 - core}, {"win": 1 - place.win}
    s_core = copies.remote(parts.at[:, core_rows(1 - core), :], parts_core, sibling)
    s_win = copies.remote(parts.at[:, win_rows(1 - place.win), :], parts_win, across)
    s_z_at = copies.take(4)
    s_z, s_z_in = [], []
    g_z_at = copies.take(4)
    g_z, g_z_in = [], []
    for step in range(1, 4):
        z = (group + step) % 4
        device = {"seq": z * 2 + core}
        s_z.append(
            copies.remote(parts.at[:, z_rows(z), :], parts_z.at[group], device, s_z_at + step, s_z_at + group)
        )
        s_z_in.append(
            copies.remote(parts.at[:, z_rows(z), :], parts_z.at[z], device, s_z_at + step, s_z_at + z)
        )
        g_z.append(
            copies.remote(
                summed.at[z_rows(group), :], summed.at[z_rows(group), :], device, g_z_at + step, g_z_at + group
            )
        )
        g_z_in.append(
            copies.remote(summed.at[z_rows(z), :], summed.at[z_rows(z), :], device, g_z_at + step, g_z_at + z)
        )
    s_side = copies.remote(parts.at[1, z_rows(group), :], parts_side, partner)
    g_win_at, g_core_at = copies.take(), copies.take()
    both = lambda at, rows, rows_in, device: tuple(
        copies.remote(summed.at[r, :], summed.at[r, :], device, at, at) for r in (rows, rows_in)
    )
    g_win, g_win_in = both(g_win_at, win_rows(place.win), win_rows(1 - place.win), across)
    g_core, g_core_in = both(g_core_at, core_rows(core), core_rows(1 - core), sibling)
    for copy in part_loads:
        copy.wait()
    s_core.start()

    class Halo:
        def __init__(self, slot, last):
            self.slot, self.last = slot, last
            self.left = copies.remote(
                gs.at[slot, :, LANES : 2 * LANES], halo_r.at[slot], {"seq": jnp.maximum(place.shard - 1, 0)}
            )
            self.right = copies.remote(
                gs.at[slot, :, bins : bins + LANES], halo_l.at[slot], {"seq": jnp.minimum(place.shard + 1, 7)}
            )

        def start(self):
            pl.when((place.shard > 0) & (place.shard <= self.last))(self.left.start)
            pl.when(place.shard < self.last)(self.right.start)

        def finish(self):
            @pl.when(place.shard < self.last)
            def _():
                self.left.wait_recv()
                gs[self.slot, :, LANES + bins :] = halo_r[self.slot]

            @pl.when(place.shard >= self.last)
            def _():
                gs[self.slot, :, LANES + bins :] = jnp.zeros((chans, LANES), BF16)

            @pl.when(place.shard > 0)
            def _():
                self.right.wait_recv()
                gs[self.slot, :, 0:LANES] = halo_l[self.slot]

            @pl.when(place.shard == 0)
            def _():
                gs[self.slot, :, 0:LANES] = jnp.zeros((chans, LANES), BF16)

            pl.when((place.shard > 0) & (place.shard <= self.last))(self.left.wait_send)
            pl.when(place.shard < self.last)(self.right.wait_send)

    halos = {name: Halo(slot, last) for name, slot, last in (("own", side, 7), ("third", 2, 7), ("other", other, 7), ("quarter", 3, 1))}
    own_loads[0].wait()
    halos["own"].start()
    e_at = copies.take(8)
    back_to = {"seq": core}
    e_home = [
        copies.remote(
            src, gs.at[3, :, lanes_at(LANES + group * piece + role * eighth, eighth)], back_to,
            e_at + which, e_at + 2 * group + which,
        )
        for which, (src, role) in enumerate(extra)
    ]

    @pl.when(group > 0)
    def _():
        for copy in e_home:
            copy.start()

    order = Order(lengths)
    for tap in range(weights.shape[0]):
        weight[:, tap * chans : (tap + 1) * chans] = weights[tap]
    names = {"mean": 0, "scale": 1, "gain": 2, "offset": 3}
    for at, row in enumerate((0, 1, 6, 7)):
        cols[at] = to_column(rows_in[row : row + 1, :])
    wide = lambda name, rows: spread_lanes(cols[names[name], rows, :], TILE)
    acc1[...] = jnp.zeros_like(acc1)
    acc2[...] = jnp.zeros_like(acc2)

    def through(slot):
        def tile(i):
            cells = gs[slot, :, lanes_at(i * TILE, TILE + 2 * LANES)]
            for tap in range(3):
                at = LANES - (tap - 1) * DILATION_BINS
                cat[tap * chans : (tap + 1) * chans, :] = cells[:, at : at + TILE]
            tmp[...] = dot(weight[...], cat[...])
            at = lanes_at(i * TILE, TILE)
            mask = valid_lanes(place.shard * bins + i * TILE, TILE, order.size(slot))
            window = order[slot]

            def body(rows):
                norm = (xbuf[window, rows, at].astype(F32) - wide("mean", rows)) * wide("scale", rows)
                part = mask * gelu_slope(norm * wide("gain", rows) + wide("offset", rows)) * tmp[rows, :]
                acc1[rows, :] += lane_sum(part)
                acc2[rows, :] += lane_sum(part * norm)
                gs[slot, rows, at] = part.astype(BF16)

            by_rows(chans, body)

        times(bins // TILE, tile)

    keeps = []

    def keep(slot):
        copy = copies.local(gs.at[slot, :, 0:bins], grads.at[slot])
        copy.start()
        keeps.append(copy)

    for copy in loads:
        copy.wait()
    halos["own"].finish()
    through(side)
    s_core.wait_recv()
    parts[:, core_rows(core), :] += parts_core[...]
    s_win.start()
    own_loads[1].wait()
    own_loads[2].wait()
    t4.wait_recv()
    halos["third"].start()

    @pl.when(group == 0)
    def _():
        for copy in extra_loads:
            copy.wait()
        for z in range(1, 4):
            for which, role in enumerate((side, other)):
                at = gs.at[3, :, lanes_at(LANES + z * piece + role * eighth, eighth)]
                copies.remote(at, at, back_to, e_at, e_at + 2 * z + which).wait_recv()
        halos["quarter"].start()

    halos["third"].finish()
    through(2)
    s_win.wait_recv()
    parts[:, win_rows(place.win), :] += parts_win[...]
    for copy in s_z:
        copy.start()

    @pl.when(group == 0)
    def _():
        halos["quarter"].finish()
        through(3)

    for copy in s_z_in:
        copy.wait_recv()
    parts_z[group] = parts[:, z_rows(group), :]
    total = parts_z[0]
    for z in range(1, 4):
        total = total + parts_z[z]
    parts[:, z_rows(group), :] = total
    s_side.start()
    for copy in t3_first[1:]:
        copy.start()
    for copy in t4_first:
        copy.wait_recv()
    halos["other"].start()
    halos["other"].finish()
    s_side.wait_recv()
    summed[z_rows(group), :] = parts[0, z_rows(group), :] + parts_side[...]
    for copy in g_z:
        copy.start()
    through(other)
    plane = PlaneSum(copies, place, msg, slots)
    plane.start([to_row(acc1[...]), to_row(acc2[...])])
    for copy in g_z_in:
        copy.wait_recv()
    g_win.start()
    total = plane.finish()
    rows_out[...] = total
    mean, scale, filled, gain = (rows_in[i : i + 1, :] for i in (0, 1, 2, 6))
    factor = gain * scale
    slope = factor * scale * total[1:2, :] / filled
    for at, row in enumerate((factor, slope, factor * total[0:1, :] / filled - mean * slope)):
        cols[at] = to_column(row)
    for copy in cot_loads:
        copy.wait()

    def last(slot):
        window = order[slot]

        def tile(i):
            at = lanes_at(i * TILE, TILE)
            mask = valid_lanes(place.shard * bins + i * TILE, TILE, order.size(slot)) > 0.0

            def body(rows):
                factor, slope, shift = (spread_lanes(cols[i, rows, :], TILE) for i in range(3))
                back = factor * gs[slot, rows, at].astype(F32)
                back = back - xbuf[window, rows, at].astype(F32) * slope - shift
                sent = cbuf[window, rows, at].astype(F32)
                gs[slot, rows, at] = (sent + jnp.where(mask, back, 0.0)).astype(BF16)

            by_rows(chans, body)

        times(bins // TILE, tile)

    last(side)
    keep(side)
    g_win_in.wait_recv()
    g_core.start()
    last(2)
    keep(2)
    g_core_in.wait_recv()
    for tap in range(conv_grad.shape[0]):
        conv_grad[tap] = jnp.transpose(summed[:, tap * chans : (tap + 1) * chans])
    point_grad[...] = summed[:, depth:]
    last(3)
    keep(3)
    last(other)
    keep(other)
    plane.drain()
    for copy in [s_core, s_win, s_side, *s_z, *g_z, g_win, g_core]:
        copy.wait_send()
    for copy in keeps:
        copy.wait()

    @pl.when(group > 0)
    def _():
        for copy in e_home:
            copy.wait_send()

    for copy in [t4, *t4_first, *t3_first]:
        copy.wait_send()
    for copy in t3_first:
        copy.wait_recv()


def last_kernel(
    lengths, x, act, grad, point, bias, rows_one, rows_two, conv_in, point_in,
    out, grad_out, gain_in, offset_in, gain_mid, offset_mid, grad_bias, conv_out, point_out,
    weight, more, tmp,
):
    window, tile = pl.program_id(0), pl.program_id(1)
    side, shard = lax.axis_index("ch"), lax.axis_index("seq")
    conv_out[...] = conv_in[...]
    point_out[...] = point_in[...]

    @pl.when((window == 0) & (tile == 0))
    def _():
        weight[...] = jnp.transpose(point[...])
        beta, gamma = rows_two[0:1, :], rows_two[1:2, :]
        more[...] = to_column(bias[...].reshape(beta.shape))
        size = gain_in.shape[0]
        gain_in[...] = gamma.reshape(size)
        offset_in[...] = beta.reshape(size)
        grad_bias[...] = rows_one[5:6, :].reshape(size)
        part = size // 2
        for ref, row in ((gain_mid, rows_one[4:5, :]), (offset_mid, rows_one[3:4, :])):
            ref[...] = jnp.where(side == 0, row[:, :part], row[:, part:])

    size = x.shape[2]
    bins = pl.num_programs(1) * size
    mask = valid_lanes(shard * bins + tile * size, size, lengths[window]) > 0.0
    tmp[...] = dot(weight[...], act[0])
    grad_out[...] = grad[...]

    def body(rows):
        added = spread_lanes(more[rows, :], TILE)
        for at in range(0, size, TILE):
            lanes = slice(at, at + TILE)
            kept = jnp.where(mask[:, lanes], tmp[rows, lanes], 0.0)
            out[0, rows, lanes] = (x[0, rows, lanes].astype(F32) + kept + added).astype(BF16)

    by_rows(x.shape[1], body)


def local_pair(
    inputs,
    lengths,
    gain_in,
    offset_in,
    conv_weight,
    gain_mid,
    offset_mid,
    point_weight,
    point_bias,
    cotangent,
):
    windows, chans, bins = inputs.shape
    taps, _, bottle = conv_weight.shape
    piece, half, eighth = bins // 4, bins // 2, bins // 8
    widened, packed = bins + half + eighth + 6 * LANES, bins + half + eighth

    vmem = pl.BlockSpec(memory_space=pltpu.VMEM)
    hbm = pl.BlockSpec(memory_space=pltpu.HBM)
    smem = pl.BlockSpec(memory_space=pltpu.SMEM)
    shape = jax.ShapeDtypeStruct
    acts, g_own, g_two, g_extra, gw, gp, rows_one = pl.pallas_call(
        first_kernel,
        in_specs=[smem, hbm, hbm, hbm, hbm, vmem, vmem, vmem, vmem, vmem, vmem],
        out_specs=[hbm, hbm, hbm, hbm, hbm, vmem, vmem],
        out_shape=[
            shape((windows, bottle, bins), BF16),
            shape((bottle, packed), BF16),
            shape((bottle, half // 4), BF16),
            shape((bottle, eighth), BF16),
            shape((bottle, 2 * taps * chans), F32),
            shape((bottle, 2 * chans), F32),
            shape((8, chans), F32),
        ],
        scratch_shapes=[
            pltpu.VMEM((windows, chans, bins), BF16),
            pltpu.VMEM((chans, bins), BF16),
            pltpu.VMEM((chans, bins), BF16),
            pltpu.VMEM((chans, half + eighth + 3 * LANES), BF16),
            pltpu.VMEM((chans, half + eighth + 3 * LANES), BF16),
            pltpu.VMEM((chans, bins + 2 * LANES), BF16),
            pltpu.VMEM((chans, piece + 2 * LANES), BF16),
            pltpu.VMEM((chans, piece), BF16),
            pltpu.VMEM((windows, chans, LANES), BF16),
            pltpu.VMEM((windows, chans, LANES), BF16),
            pltpu.VMEM((3, chans, LANES), BF16),
            pltpu.VMEM((chans, widened), BF16),
            pltpu.VMEM((chans, widened), BF16),
            pltpu.VMEM((bottle, packed), F32),
            pltpu.VMEM((bottle, packed), BF16),
            pltpu.VMEM((bottle, packed), BF16),
            pltpu.VMEM((bottle, 2 * taps * chans), BF16),
            pltpu.VMEM(((taps + 1) * chans, bottle), BF16),
            pltpu.VMEM((bottle, eighth), BF16),
            pltpu.VMEM((2 * taps * chans, TILE), BF16),
            pltpu.VMEM((bottle, TILE), F32),
            pltpu.VMEM((chans, LANES), F32),
            pltpu.VMEM((chans, LANES), F32),
            pltpu.VMEM((11, chans, LANES), F32),
            pltpu.VMEM((3, 8, chans), F32),
            pltpu.VMEM((3, PLANE, 8, chans), F32),
            pltpu.VMEM((3, 8, chans), F32),
            pltpu.VMEM((3, 8, chans), F32),
            pltpu.VMEM((windows, bins), F32),
            pltpu.VMEM((1, widened), F32),
            pltpu.VMEM((1, packed), F32),
            pltpu.SemaphoreType.DMA((128,)),
            pltpu.SemaphoreType.DMA((128,)),
        ],
        compiler_params=pltpu.CompilerParams(
            collective_id=0, has_side_effects=True, vmem_limit_bytes=VMEM_BYTES
        ),
        cost_estimate=pl.CostEstimate(flops=60 * 10**9, bytes_accessed=10**8, transcendentals=0),
    )(
        lengths, inputs, cotangent, conv_weight, point_weight, conv_weight, point_weight,
        gain_in, offset_in, gain_mid, offset_mid,
    )

    share = bottle // PLANE
    acts, grads, rows_two, conv_grad, point_grad = pl.pallas_call(
        second_kernel,
        in_specs=[smem, hbm, hbm, hbm, hbm, hbm, hbm, hbm, hbm, vmem, vmem],
        out_specs=[hbm, hbm, vmem, vmem, vmem],
        out_shape=[
            shape((windows, bottle, bins), BF16),
            shape((windows, chans, bins), BF16),
            shape((8, chans), F32),
            shape((taps, chans, bottle), F32),
            shape((bottle, chans), F32),
        ],
        input_output_aliases={3: 0},
        scratch_shapes=[
            pltpu.VMEM((windows, bottle, bins + 2 * LANES), BF16),
            pltpu.VMEM((windows, chans, bins), BF16),
            pltpu.VMEM((windows, chans, bins), BF16),
            pltpu.VMEM((windows, bottle, LANES), BF16),
            pltpu.VMEM((windows, bottle, LANES), BF16),
            pltpu.VMEM((taps * bottle, TILE), BF16),
            pltpu.VMEM((chans, TILE), F32),
            pltpu.VMEM((chans, LANES), F32),
            pltpu.VMEM((chans, LANES), F32),
            pltpu.VMEM((4, chans, LANES), F32),
            pltpu.VMEM((8, chans), F32),
            pltpu.VMEM((PLANE, 8, chans), F32),
            pltpu.VMEM((2, bottle, (taps + 1) * chans), F32),
            pltpu.VMEM((2, bottle // 2, (taps + 1) * chans), F32),
            pltpu.VMEM((2, bottle // 4, (taps + 1) * chans), F32),
            pltpu.VMEM((4, 2, share, (taps + 1) * chans), F32),
            pltpu.VMEM((share, (taps + 1) * chans), F32),
            pltpu.VMEM((bottle, (taps + 1) * chans), F32),
            pltpu.VMEM((chans, taps * bottle), BF16),
            pltpu.SemaphoreType.DMA((128,)),
            pltpu.SemaphoreType.DMA((128,)),
        ],
        compiler_params=pltpu.CompilerParams(
            collective_id=1, has_side_effects=True, vmem_limit_bytes=VMEM_BYTES
        ),
        cost_estimate=pl.CostEstimate(flops=60 * 10**9, bytes_accessed=10**8, transcendentals=0),
    )(lengths, inputs, cotangent, acts, g_own, g_two, g_extra, gw, gp, conv_weight, rows_one)

    def slot_of(window, sizes):
        rank = jnp.int32(0)
        for other in range(windows):
            longer = sizes[other] > sizes[window]
            ahead = (sizes[other] == sizes[window]) & (other < window)
            rank = rank + jnp.where(longer | ahead, 1, 0)
        return rank

    tile = bins
    at = pl.BlockSpec((1, chans, tile), lambda w, i, p: (w, 0, i))
    at_slot = pl.BlockSpec((1, chans, tile), lambda w, i, p: (slot_of(w, p), 0, i))
    whole = lambda rows, size: pl.BlockSpec((rows, size), lambda w, i, p: (0, 0))
    steps = bins // tile
    part = chans // (windows * steps)
    conv_at = pl.BlockSpec((taps, part, bottle), lambda w, i, p: (0, w * steps + i, 0))
    point_at = pl.BlockSpec((part, chans), lambda w, i, p: (w * steps + i, 0))
    line = lambda size: pl.BlockSpec((size,), lambda w, i, p: (0,))
    outputs, grad_inputs, gamma_in, beta_in, gamma_mid, beta_mid, grad_bias, conv_grad, point_grad = pl.pallas_call(
        last_kernel,
        grid_spec=pltpu.PrefetchScalarGridSpec(
            num_scalar_prefetch=1,
            grid=(windows, bins // tile),
            in_specs=[
                at, at_slot, at_slot,
                whole(bottle, chans), line(chans), whole(8, chans), whole(8, chans), conv_at, point_at,
            ],
            out_specs=[
                at, at, line(chans), line(chans), whole(1, bottle // 2), whole(1, bottle // 2),
                line(chans), conv_at, point_at,
            ],
            scratch_shapes=[
                pltpu.VMEM((chans, bottle), BF16),
                pltpu.VMEM((chans, LANES), F32),
                pltpu.VMEM((chans, tile), F32),
            ],
        ),
        out_shape=[
            shape(inputs.shape, BF16),
            shape(inputs.shape, BF16),
            shape((chans,), F32),
            shape((chans,), F32),
            shape((1, bottle // 2), F32),
            shape((1, bottle // 2), F32),
            shape((chans,), F32),
            shape((taps, chans, bottle), F32),
            shape((bottle, chans), F32),
        ],
        compiler_params=pltpu.CompilerParams(vmem_limit_bytes=VMEM_BYTES),
        cost_estimate=pl.CostEstimate(flops=4 * 10**9, bytes_accessed=6 * 10**7, transcendentals=0),
    )(
        lengths, inputs, acts, grads, point_weight, point_bias, rows_one, rows_two,
        conv_grad, point_grad,
    )
    return (
        outputs,
        grad_inputs,
        gamma_in,
        beta_in,
        conv_grad,
        gamma_mid[0],
        beta_mid[0],
        point_grad,
        grad_bias,
    )


def solution(mesh):
    paired = mesh.shape["ch"] == 2 and mesh.shape["seq"] == 8 and mesh.shape["win"] == 2

    def local(*args):
        windows, chans, bins = args[0].shape
        if paired and windows == 4 and chans == args[4].shape[2] and bins == 8 * TILE:
            return local_pair(*args)
        return local_any(*args)

    return jax.shard_map(
        local,
        mesh=mesh,
        in_specs=(
            P("win", "ch", "seq"),
            P("win"),
            P("ch"),
            P("ch"),
            P(None, "ch", None),
            P(),
            P(),
            P(None, "ch"),
            P("ch"),
            P("win", "ch", "seq"),
        ),
        out_specs=(
            P("win", "ch", "seq"),
            P("win", "ch", "seq"),
            P("ch"),
            P("ch"),
            P(None, "ch", None),
            P("ch"),
            P("ch"),
            P(None, "ch"),
            P("ch"),
        ),
        check_vma=False,
    )
```
